32 devices in a mesh: parts: 2 (over x), dp: 16 (over z, y, core).
Axes of the slice: x: 2, y: 2, z: 4, core: 2. Of those that a mesh axis runs over, the one named last changes fastest.
Arguments:
- layer_input: bfloat16 [32768, 4096], P(('parts', 'dp')), parts along dimension 0, may hold values from -60 to 60
- out_grads: bfloat16 [32768, 2, 1024], P(('parts', 'dp')), parts along dimension 0, may hold values from -60 to 60, as said below
- in_proj: bfloat16 [2, 64, 4096], replicated, may hold values from -0.09375 to 0.09375
- out_proj: bfloat16 [2, 64, 1024], replicated, may hold values from -0.1875 to 0.1875
- queries: bfloat16 [256, 8192], P(('parts', 'dp')), parts along dimension 0, may hold values from -6 to 6
Outputs:
- scores: float32 [256, 128], P(('parts', 'dp')), parts along dimension 0
The draws below stay inside these ranges and needn't reach their ends.
There are 2 independent parts, one for each index of `parts`. The reference program is written for one: setup_inputs(seed, part) draws one part's arguments, and reference() takes and returns one part's arrays. A program takes and returns all parts, laid end to end along the dimension named above; an argument that names none is the same for every part. Nothing has to cross between parts.
Inputs may be any that keep to these rules, and one draw needn't show every extreme that they name: `out_grads`: output gradients at each token.
All inputs are finite; a program needn't handle non-finite values.
Results may differ from the reference program's by a relative error of at most 0.0054.
Values may be sent and summed in bfloat16 or wider, within the bound.
No kernel may reach another device: no remote copies, remote signals or barrier semaphores. Data moves between devices by JAX's collectives and lax.ppermute only.
A program may use at most 64 MiB of HBM per device.

```python
import jax
import jax.numpy as jnp
from jax import lax

D = 4096
KV = 1024
R = 64
LEN = 128
SEQS = 128
QUERIES = 128
TOKENS = 16384


def rising_scale(shape):
    position = jnp.arange(TOKENS, dtype=jnp.float32) / (TOKENS - 1)
    rising = jnp.exp(jnp.log(3.0) * position)
    return rising.reshape((TOKENS,) + (1,) * (len(shape) - 1))


def draw_layer_input(key, part):
    key = jax.random.fold_in(key, 11)
    base_key = jax.random.fold_in(key, 0)
    shape = (TOKENS, D)
    rising = rising_scale(shape)
    values = jnp.clip(jax.random.normal(base_key, shape, jnp.float32), -4.0, 4.0) * rising
    return values.astype(jnp.bfloat16)


def draw_out_grads(key, part):
    key = jax.random.fold_in(key, 12)
    base_key = jax.random.fold_in(key, 0)
    shape = (TOKENS, 2, KV)
    rising = rising_scale(shape)
    values = jnp.clip(jax.random.normal(base_key, shape, jnp.float32), -4.0, 4.0) * rising
    return values.astype(jnp.bfloat16)


def levels(key, dims, shards, smallest, top_value):
    factor_of, own = 1.0, jax.random.fold_in(key, 6)
    for dim, shards_of in shards:
        steps = jnp.exp(jax.random.uniform(jax.random.fold_in(own, dim), (shards_of,), jnp.float32, smallest / len(shards), top_value / len(shards)))
        factor_of = factor_of * jnp.repeat(steps, dims[dim] // shards_of).reshape([-1 if axis == dim else 1 for axis in range(len(dims))])
    return factor_of


def gaussian(rng, dims, deviation, limit, pieces=(), held_as=jnp.bfloat16):
    factor_of = levels(rng, dims, pieces, -0.22, 0.18) if pieces else 1.0
    entries = jax.random.normal(rng, dims, jnp.float32) * deviation * factor_of
    return jnp.minimum(jnp.maximum(entries, -limit), limit).astype(held_as)


def setup_inputs(seed: int = 0, part: int = 0) -> dict:
    streams_of = jax.random.split(jax.random.key(seed), 6)
    part_keys = jax.random.split(jax.random.fold_in(streams_of[5], part), 6)
    layer_input = draw_layer_input(jax.random.fold_in(jax.random.fold_in(streams_of[5], part), 71), part)
    out_grads = draw_out_grads(jax.random.fold_in(jax.random.fold_in(streams_of[5], part), 71), part)
    in_proj = gaussian(streams_of[2], (2, R, D), D ** -0.5, 0.09375)
    out_proj = gaussian(streams_of[3], (2, R, KV), KV ** -0.5, 0.1875)
    queries = gaussian(part_keys[4], (QUERIES, 2 * R * R), 1.0, 6.0, ((0, 16),))
    return {"layer_input": layer_input, "out_grads": out_grads, "in_proj": in_proj, "out_proj": out_proj, "queries": queries}


damping_ratio = 0.1

def damped_inverse(covariance):
    order_dim = covariance.shape[-1]
    identity = jnp.eye(order_dim, dtype=covariance.dtype)
    trace_sum = jnp.trace(covariance, axis1=1, axis2=2)
    damped = covariance + (damping_ratio * trace_sum / order_dim)[:, None, None] * identity
    factor = jnp.linalg.cholesky(damped)
    return jax.vmap(lambda lower: jax.scipy.linalg.cho_solve((lower, True), identity))(factor)

def reference(layer_input, out_grads, in_proj, out_proj, queries):
    total_tokens = layer_input.shape[0]
    in_flat = in_proj.reshape(2 * R, D)
    projected_in = jnp.dot(layer_input.astype(jnp.float32), in_flat.T.astype(jnp.float32), preferred_element_type=jnp.float32).astype(jnp.bfloat16)
    projected_in = projected_in.reshape(total_tokens, 2, R).astype(jnp.float32)
    projected_out = jnp.einsum('tmk,mrk->tmr', out_grads.astype(jnp.float32), out_proj.astype(jnp.float32), precision=lax.Precision.HIGHEST)
    projected_out = projected_out.astype(jnp.bfloat16).astype(jnp.float32)
    cov_in = jnp.einsum('tmr,tms->mrs', projected_in, projected_in, precision=lax.Precision.HIGHEST) / TOKENS
    cov_out = jnp.einsum('tmr,tms->mrs', projected_out, projected_out, precision=lax.Precision.HIGHEST) / TOKENS
    inv_in = damped_inverse(cov_in)
    inv_out = damped_inverse(cov_out)
    moments = jnp.einsum('slmo,slmc->smoc', projected_out.reshape(SEQS, LEN, 2, R), projected_in.reshape(SEQS, LEN, 2, R), precision=lax.Precision.HIGHEST) / LEN
    left_side = jnp.einsum('moa,smac->smoc', inv_out, moments, precision=lax.Precision.HIGHEST)
    precond = jnp.einsum('smoa,mac->smoc', left_side, inv_in, precision=lax.Precision.HIGHEST)
    precond = precond.astype(jnp.bfloat16).reshape(SEQS, 2 * R * R)
    return jnp.dot(precond.astype(jnp.float32), queries.T.astype(jnp.float32), preferred_element_type=jnp.float32)
```

```python
import functools

import jax
import jax.numpy as jnp
from jax import lax
from jax.experimental import pallas as pl
from jax.experimental.pallas import tpu as pltpu
from jax.sharding import Mesh, PartitionSpec as P

R = 64
LEN = 128
PAIR = 2 * R
DAMPING = 0.1
STEP = 512

F32 = jnp.float32
BF16 = jnp.bfloat16
MIB = 1024 * 1024


def dot(a, b, dims, precision=None):
    return lax.dot_general(a, b, (dims, ((), ())), precision=precision, preferred_element_type=F32)


NN = ((1,), (0,))
NT = ((1,), (1,))
TN = ((0,), (0,))


def statistics_kernel(core_ref, x_ref, w_ref, outs_ref, keep_cov, send_cov, keep_mom, send_mom, total):
    step = pl.program_id(0)
    term = dot(x_ref[...], w_ref[...], NT)

    @pl.when(step == 0)
    def _():
        total[...] = term

    @pl.when(step > 0)
    def _():
        total[...] += term

    @pl.when(step == pl.num_programs(0) - 1)
    def _():
        first = core_ref[0] == 0
        acts = total[...].astype(BF16)
        outs = outs_ref[...]
        low = lax.broadcasted_iota(jnp.int32, (R, PAIR), 1) < R
        cov_in = dot(acts, acts, TN)
        cov_out = dot(outs, outs, NT)
        cov0 = jnp.where(low, cov_in[:R], pltpu.roll(cov_out[:R], R, 1))
        cov1 = jnp.where(low, pltpu.roll(cov_in[R:], R, 1), cov_out[R:])
        keep_cov[...] = jnp.where(first, cov0, cov1)
        send_cov[...] = jnp.where(first, cov1, cov0)
        for pair in range(acts.shape[0] // LEN // 2):
            blocks = []
            for seq in (2 * pair, 2 * pair + 1):
                rows = slice(seq * LEN, (seq + 1) * LEN)
                blocks.append(dot(outs[:, rows], acts[rows], NN) * (1.0 / LEN))
            mom0 = jnp.where(low, blocks[0][:R], pltpu.roll(blocks[1][:R], R, 1))
            mom1 = jnp.where(low, pltpu.roll(blocks[0][R:], R, 1), blocks[1][R:])
            lanes = slice(pair * PAIR, (pair + 1) * PAIR)
            keep_mom[:, lanes] = jnp.where(first, mom0, mom1)
            send_mom[:, lanes] = jnp.where(first, mom1, mom0)


def statistics(core, layer_input, in_flat, outs):
    tokens, width = layer_input.shape
    seqs = tokens // LEN
    cov = jax.ShapeDtypeStruct((R, PAIR), F32)
    mom = jax.ShapeDtypeStruct((R, seqs * R), F32)
    whole = lambda shape: pl.BlockSpec(shape, lambda k: (0, 0))
    return pl.pallas_call(
        statistics_kernel,
        grid=(width // STEP,),
        in_specs=[
            pl.BlockSpec(memory_space=pltpu.SMEM),
            pl.BlockSpec((tokens, STEP), lambda k: (0, k)),
            pl.BlockSpec((PAIR, STEP), lambda k: (0, k)),
            whole(outs.shape),
        ],
        out_specs=[whole(cov.shape), whole(cov.shape), whole(mom.shape), whole(mom.shape)],
        out_shape=[cov, cov, mom, mom],
        scratch_shapes=[pltpu.VMEM((tokens, PAIR), F32)],
        compiler_params=pltpu.CompilerParams(vmem_limit_bytes=16 * MIB),
        cost_estimate=pl.CostEstimate(
            flops=2 * tokens * width * PAIR, bytes_accessed=2 * tokens * width, transcendentals=0
        ),
        name="statistics",
    )(core, layer_input, in_flat, outs)


def invert_pair(work):
    row = lax.broadcasted_iota(jnp.int32, (R, PAIR), 0)
    lane = lax.broadcasted_iota(jnp.int32, (R, PAIR), 1)
    low = lane < R
    column = jnp.where(low, lane, lane - R)
    for k in range(R):
        col = jnp.where(low, work[:, k : k + 1], work[:, R + k : R + k + 1])
        here = column[:1] == k
        pivot = jnp.where(here, 1.0, work[k : k + 1]) / col[k : k + 1]
        col = jnp.where(row == k, -1.0, col)
        work = jnp.where((row == k) | (column == k), 0.0, work) - col * pivot
    return work


def precondition_kernel(total_tokens, cov_ref, keep_ref, recv_ref, out_ref, inv_ref, flat_ref):
    row = lax.broadcasted_iota(jnp.int32, (R, PAIR), 0)
    lane = lax.broadcasted_iota(jnp.int32, (R, PAIR), 1)
    low = lane < R
    column = jnp.where(low, lane, lane - R)
    cov = cov_ref[...] / total_tokens
    diagonal = jnp.where(row == column, cov, 0.0)
    trace_in = jnp.sum(jnp.where(low, diagonal, 0.0), keepdims=True)
    trace_out = jnp.sum(jnp.where(low, 0.0, diagonal), keepdims=True)
    shift = jnp.where(low, trace_in, trace_out) * (DAMPING / R)
    inv = invert_pair(cov + jnp.where(row == column, shift, 0.0))
    inv_ref[...] = inv
    half = R // 2
    left = jnp.concatenate(
        [inv_ref[pl.ds(0, half, stride=2), :], inv_ref[pl.ds(1, half, stride=2), :]], axis=0
    )
    left = pltpu.roll(left, R, 1)[:, :R]
    moments = jnp.concatenate([keep_ref[...], recv_ref[...]], axis=1)
    mixed = dot(left, moments, NN, lax.Precision.HIGHEST)
    pairs = moments.shape[1] // PAIR
    stack = jnp.concatenate(
        [
            jnp.concatenate(
                [mixed[:half, j * PAIR : (j + 1) * PAIR], mixed[half:, j * PAIR : (j + 1) * PAIR]], axis=1
            )
            for j in range(pairs)
        ],
        axis=0,
    )
    zero = jnp.zeros((R, PAIR), F32)
    at_low = jnp.where(low, inv, 0.0)
    at_high = pltpu.roll(at_low, R, 1)
    right = jnp.concatenate(
        [
            jnp.concatenate([at_low, zero], axis=1),
            jnp.concatenate([zero, at_low], axis=1),
            jnp.concatenate([at_high, zero], axis=1),
            jnp.concatenate([zero, at_high], axis=1),
        ],
        axis=0,
    )
    done = dot(stack, right, NN, lax.Precision.HIGHEST)
    for j in range(pairs):
        rows = done[j * half : (j + 1) * half]
        flat_ref[(2 * j) * half : (2 * j + 1) * half, :] = rows[:, :PAIR]
        flat_ref[(2 * j + 1) * half : (2 * j + 2) * half, :] = rows[:, PAIR:]
    for k in range(half):
        out_ref[:, k * PAIR : (k + 1) * PAIR] = flat_ref[pl.ds(k, 2 * pairs, stride=half), :].astype(BF16)


def precondition(cov, keep_mom, recv_mom, total_tokens):
    seqs = 2 * keep_mom.shape[1] // R
    return pl.pallas_call(
        functools.partial(precondition_kernel, total_tokens),
        in_specs=[pl.BlockSpec(memory_space=pltpu.VMEM)] * 3,
        out_specs=pl.BlockSpec(memory_space=pltpu.VMEM),
        out_shape=jax.ShapeDtypeStruct((seqs, R * R), BF16),
        scratch_shapes=[pltpu.VMEM((R, PAIR), F32), pltpu.VMEM((seqs * R // 2, PAIR), F32)],
        compiler_params=pltpu.CompilerParams(vmem_limit_bytes=16 * MIB),
        name="precondition",
    )(cov, keep_mom, recv_mom)


def scores_kernel(core_ref, flat_ref, mine_ref, other_ref, out_ref):
    first = core_ref[0] == 0
    flat = flat_ref[...]
    mine = dot(mine_ref[...], flat, NT)
    other = dot(other_ref[...], flat, NT)
    low = jnp.where(first, mine, other)
    high = jnp.where(first, other, mine)
    groups = []
    for at in range(0, mine.shape[0], 8):
        groups += [low[at : at + 8], high[at : at + 8]]
    out_ref[...] = jnp.concatenate(groups, axis=0).T


def score(core, flat, mine, other):
    queries = mine.shape[0] + other.shape[0]
    return pl.pallas_call(
        scores_kernel,
        in_specs=[pl.BlockSpec(memory_space=pltpu.SMEM)] + [pl.BlockSpec(memory_space=pltpu.VMEM)] * 3,
        out_specs=pl.BlockSpec(memory_space=pltpu.VMEM),
        out_shape=jax.ShapeDtypeStruct((flat.shape[0], queries), F32),
        compiler_params=pltpu.CompilerParams(vmem_limit_bytes=32 * MIB),
        name="scores",
    )(core, flat, mine, other)


def per_device(layer_input, out_grads, in_proj, out_proj, queries):
    local_tokens = layer_input.shape[0]
    chips = lax.axis_size("chip")
    core = lax.axis_index("core").astype(jnp.int32)
    core_arg = core.reshape(1)
    swap = [(0, 1), (1, 0)]
    entries = R * R
    column = lax.all_gather(queries, "chip", axis=0, tiled=True)
    outs = jnp.einsum("mrk,tmk->mrt", out_proj, out_grads, preferred_element_type=F32).astype(BF16)
    keep_cov, send_cov, keep_mom, send_mom = statistics(
        core_arg, layer_input, in_proj.reshape(PAIR, in_proj.shape[2]), outs.reshape(PAIR, local_tokens)
    )
    cov = keep_cov + lax.ppermute(send_cov, "core", swap)
    recv_mom = lax.ppermute(send_mom, "core", swap)
    distance = 1
    while distance < chips:
        cov = cov + lax.ppermute(cov, "chip", [(i, i ^ distance) for i in range(chips)])
        distance *= 2
    flat = precondition(cov, keep_mom, recv_mom, local_tokens * chips * 2)
    mine = lax.dynamic_slice(column, (0, core * entries), (column.shape[0], entries))
    theirs = lax.dynamic_slice(column, (0, (1 - core) * entries), (column.shape[0], entries))
    other = lax.ppermute(theirs, "core", swap)
    partial = score(core_arg, flat, mine, other)
    seqs = local_tokens // LEN
    return partial[:seqs] + lax.ppermute(partial[seqs:], "core", swap)


def solution(mesh):
    parts, dp = mesh.devices.shape
    grid = Mesh(mesh.devices.reshape(parts, dp // 2, 2), ("parts", "chip", "core"))
    split = ("parts", "chip", "core")
    return jax.shard_map(
        per_device,
        mesh=grid,
        in_specs=(P(split, None), P(split, None, None), P(), P(), P(split, None)),
        out_specs=P(split, None),
        check_vma=False,
    )
```

```python
import functools

import jax
import jax.numpy as jnp
from jax import lax
from jax.experimental import pallas as pl
from jax.experimental.pallas import tpu as pltpu
from jax.sharding import PartitionSpec as P

R = 64
LEN = 128
PAIR = 2 * R
DAMPING = 0.1
STEP = 512
BLOCK = 4
GROUP = 4

F32 = jnp.float32
BF16 = jnp.bfloat16
MIB = 1024 * 1024


def dot(a, b, dims, precision=None):
    return lax.dot_general(a, b, (dims, ((), ())), precision=precision, preferred_element_type=F32)


NN = ((1,), (0,))
NT = ((1,), (1,))
TN = ((0,), (0,))


def statistics_kernel(
    core_ref, x_hbm, w_hbm, outs_ref, keep_cov, send_cov, keep_mom, send_mom, x_buf, w_buf, total, x_sem, w_sem
):
    chunks = x_buf.shape[0]

    def x_copy(k):
        columns = pl.ds(pl.multiple_of(k * STEP, STEP), STEP)
        return pltpu.make_async_copy(x_hbm.at[:, columns], x_buf.at[k], x_sem.at[k])

    def w_copy(k):
        columns = pl.ds(pl.multiple_of(k * STEP, STEP), STEP)
        return pltpu.make_async_copy(w_hbm.at[:, columns], w_buf.at[k], w_sem.at[k])

    for k in range(chunks):
        w_copy(k).start()
        x_copy(k).start()
    total[...] = jnp.zeros_like(total)

    @pl.loop(0, chunks)
    def _(k):
        w_copy(k).wait()
        x_copy(k).wait()
        total[...] += dot(x_buf[k], w_buf[k], NT)

    first = core_ref[0] == 0
    acts = total[...].astype(BF16)
    outs = outs_ref[...]
    low = lax.broadcasted_iota(jnp.int32, (R, PAIR), 1) < R
    cov_in = dot(acts, acts, TN)
    cov_out = dot(outs, outs, NT)
    cov0 = jnp.where(low, cov_in[:R], pltpu.roll(cov_out[:R], R, 1))
    cov1 = jnp.where(low, pltpu.roll(cov_in[R:], R, 1), cov_out[R:])
    keep_cov[...] = jnp.where(first, cov0, cov1)
    send_cov[...] = jnp.where(first, cov1, cov0)
    for pair in range(acts.shape[0] // LEN // 2):
        blocks = []
        for seq in (2 * pair, 2 * pair + 1):
            rows = slice(seq * LEN, (seq + 1) * LEN)
            blocks.append(dot(outs[:, rows], acts[rows], NN) * (1.0 / LEN))
        mom0 = jnp.where(low, blocks[0][:R], pltpu.roll(blocks[1][:R], R, 1))
        mom1 = jnp.where(low, pltpu.roll(blocks[0][R:], R, 1), blocks[1][R:])
        lanes = slice(pair * PAIR, (pair + 1) * PAIR)
        keep_mom[:, lanes] = jnp.where(first, mom0, mom1)
        send_mom[:, lanes] = jnp.where(first, mom1, mom0)


def statistics(core, layer_input, in_flat, outs):
    tokens, width = layer_input.shape
    seqs = tokens // LEN
    chunks = width // STEP
    cov = jax.ShapeDtypeStruct((R, PAIR), F32)
    mom = jax.ShapeDtypeStruct((R, seqs * R), F32)
    vmem = pl.BlockSpec(memory_space=pltpu.VMEM)
    return pl.pallas_call(
        statistics_kernel,
        in_specs=[
            pl.BlockSpec(memory_space=pltpu.SMEM),
            pl.BlockSpec(memory_space=pl.ANY),
            pl.BlockSpec(memory_space=pl.ANY),
            vmem,
        ],
        out_specs=[vmem] * 4,
        out_shape=[cov, cov, mom, mom],
        scratch_shapes=[
            pltpu.VMEM((chunks, tokens, STEP), BF16),
            pltpu.VMEM((chunks, PAIR, STEP), BF16),
            pltpu.VMEM((tokens, PAIR), F32),
            pltpu.SemaphoreType.DMA((chunks,)),
            pltpu.SemaphoreType.DMA((chunks,)),
        ],
        compiler_params=pltpu.CompilerParams(vmem_limit_bytes=48 * MIB),
        cost_estimate=pl.CostEstimate(
            flops=2 * tokens * width * PAIR, bytes_accessed=2 * tokens * width, transcendentals=0
        ),
        name="statistics",
    )(core, layer_input, in_flat, outs)


def solve_block(p, rows):
    det = 1.0 / (p[0][0] * p[1][1] - p[0][1] * p[0][1])
    a, b, c = p[1][1] * det, -p[0][1] * det, p[0][0] * det
    t = [[a * p[0][j] + b * p[1][j], b * p[0][j] + c * p[1][j]] for j in (2, 3)]
    s22 = p[2][2] - p[0][2] * t[0][0] - p[1][2] * t[0][1]
    s23 = p[2][3] - p[0][2] * t[1][0] - p[1][2] * t[1][1]
    s33 = p[3][3] - p[0][3] * t[1][0] - p[1][3] * t[1][1]
    det = 1.0 / (s22 * s33 - s23 * s23)
    y0 = a * rows[0] + b * rows[1]
    y1 = b * rows[0] + c * rows[1]
    z2 = rows[2] - p[0][2] * y0 - p[1][2] * y1
    z3 = rows[3] - p[0][3] * y0 - p[1][3] * y1
    x2 = (s33 * z2 - s23 * z3) * det
    x3 = (s22 * z3 - s23 * z2) * det
    return [y0 - t[0][0] * x2 - t[1][0] * x3, y1 - t[0][1] * x2 - t[1][1] * x3, x2, x3]


def invert_pair(matrix):
    lane = lax.broadcasted_iota(jnp.int32, (8, PAIR), 1)
    row = lax.broadcasted_iota(jnp.int32, (8, PAIR), 0)
    column = lane % R
    base = lane - column
    work = [matrix[8 * g : 8 * g + 8] for g in range(R // 8)]
    for k in range(0, R, BLOCK):
        cols = [[jnp.take_along_axis(part, base + (k + j), axis=1) for j in range(BLOCK)] for part in work]
        home, at = k // 8, k % 8
        inside = (column >= k) & (column < k + BLOCK)
        pivots = [[cols[home][j][at + i : at + i + 1] for j in range(BLOCK)] for i in range(BLOCK)]
        rows = [
            jnp.where(
                inside[:1], jnp.where(column[:1] == k + i, 1.0, 0.0), work[home][at + i : at + i + 1]
            )
            for i in range(BLOCK)
        ]
        solved = solve_block(pivots, rows)
        for g in range(R // 8):
            part = jnp.where(inside, 0.0, work[g])
            col = cols[g]
            if g == home:
                block_row = (row >= at) & (row < at + BLOCK)
                part = jnp.where(block_row, 0.0, part)
                col = [
                    jnp.where(block_row, jnp.where(row == at + j, -1.0, 0.0), col[j]) for j in range(BLOCK)
                ]
            work[g] = part - (col[0] * solved[0] + col[1] * solved[1]) - (col[2] * solved[2] + col[3] * solved[3])
    return jnp.concatenate(work, axis=0)


def inverse_kernel(total_tokens, cov_ref, inv_ref):
    row = lax.broadcasted_iota(jnp.int32, (R, PAIR), 0)
    lane = lax.broadcasted_iota(jnp.int32, (R, PAIR), 1)
    low = lane < R
    column = jnp.where(low, lane, lane - R)
    cov = cov_ref[...]
    diagonal = jnp.where(row == column, cov, 0.0)
    trace_in = jnp.sum(jnp.where(low, diagonal, 0.0), keepdims=True)
    trace_out = jnp.sum(jnp.where(low, 0.0, diagonal), keepdims=True)
    scale = R / jnp.where(low, trace_in, trace_out)
    inv_ref[...] = invert_pair(cov * scale + jnp.where(row == column, DAMPING, 0.0)) * (scale * total_tokens)


def inverse(cov, total_tokens):
    vmem = pl.BlockSpec(memory_space=pltpu.VMEM)
    return pl.pallas_call(
        functools.partial(inverse_kernel, total_tokens),
        in_specs=[vmem],
        out_specs=vmem,
        out_shape=jax.ShapeDtypeStruct(cov.shape, F32),
        cost_estimate=pl.CostEstimate(flops=4 * 10**9, bytes_accessed=2**16, transcendentals=0),
        name="inverse",
    )(cov)


def scores_kernel(count, place_ref, inv_ref, *refs):
    moment_refs, shard_refs, (out_ref, flat_ref, part_ref) = refs[:count], refs[count:-3], refs[-3:]
    place = place_ref[0]
    upper = (place >> 1) & 1 == 1
    low = lax.broadcasted_iota(jnp.int32, (R, PAIR), 1) < R
    inv = inv_ref[...]
    tiles = R // 4
    even = [inv_ref[pl.ds(start, tiles, stride=2), :] for start in (0, R // 2)]
    odd = [inv_ref[pl.ds(start + 1, tiles, stride=2), :] for start in (0, R // 2)]
    left = jnp.concatenate([jnp.where(upper, even[1], even[0]), jnp.where(upper, odd[1], odd[0])], axis=0)
    left = pltpu.roll(left, R, 1)[:, :R]
    moments = jnp.concatenate([ref[...] for ref in moment_refs], axis=1)
    mixed = dot(left, moments, NN, lax.Precision.HIGHEST)
    pairs = moments.shape[1] // PAIR
    stack = jnp.concatenate(
        [
            jnp.concatenate(
                [mixed[:tiles, j * PAIR : (j + 1) * PAIR], mixed[tiles:, j * PAIR : (j + 1) * PAIR]], axis=1
            )
            for j in range(pairs)
        ],
        axis=0,
    )
    zero = jnp.zeros((R, PAIR), F32)
    at_low = jnp.where(low, inv, 0.0)
    at_high = pltpu.roll(at_low, R, 1)
    right = jnp.concatenate(
        [
            jnp.concatenate([at_low, zero], axis=1),
            jnp.concatenate([zero, at_low], axis=1),
            jnp.concatenate([at_high, zero], axis=1),
            jnp.concatenate([zero, at_high], axis=1),
        ],
        axis=0,
    )
    done = dot(stack, right, NN, lax.Precision.HIGHEST)
    for j in range(pairs):
        rows = done[j * tiles : (j + 1) * tiles]
        flat_ref[(2 * j) * tiles : (2 * j + 1) * tiles, :] = rows[:, :PAIR]
        flat_ref[(2 * j + 1) * tiles : (2 * j + 2) * tiles, :] = rows[:, PAIR:]
    flat = jnp.concatenate(
        [flat_ref[pl.ds(k, 2 * pairs, stride=tiles), :].astype(BF16) for k in range(tiles)], axis=1
    )
    part = dot(jnp.concatenate([ref[...] for ref in shard_refs], axis=0), flat, NT)
    group = part_ref.shape[1]
    for distance in range(part_ref.shape[0]):
        part_ref[place ^ distance] = part[distance * group : (distance + 1) * group]
    out_ref[...] = part_ref[...].reshape(part.shape).T


def score(place, inv, moments, shards, group):
    seqs = sum(part.shape[1] for part in moments) // R
    queries = sum(shard.shape[0] for shard in shards)
    vmem = pl.BlockSpec(memory_space=pltpu.VMEM)
    return pl.pallas_call(
        functools.partial(scores_kernel, len(moments)),
        in_specs=[pl.BlockSpec(memory_space=pltpu.SMEM), vmem] + [vmem] * (len(moments) + len(shards)),
        out_specs=vmem,
        out_shape=jax.ShapeDtypeStruct((seqs, queries), F32),
        scratch_shapes=[
            pltpu.VMEM((seqs * R // 4, PAIR), F32),
            pltpu.VMEM((queries // group, group, seqs), F32),
        ],
        compiler_params=pltpu.CompilerParams(vmem_limit_bytes=32 * MIB),
        name="scores",
    )(place, inv, *moments, *shards)


def exchange(value, distance):
    return lax.ppermute(value, "dp", [(i, i ^ distance) for i in range(lax.axis_size("dp"))])


def per_device(layer_input, out_grads, in_proj, out_proj, queries):
    local_tokens = layer_input.shape[0]
    local_queries = queries.shape[0]
    devices = lax.axis_size("dp")
    place = lax.axis_index("dp").astype(jnp.int32)
    module = place & 1
    quarter = queries.shape[1] // GROUP

    def block_for(distance):
        target = place ^ distance
        block = ((target & 1) << 1) | ((target >> 1) & 1)
        return lax.dynamic_slice_in_dim(queries, block * quarter, quarter, 1)

    shard = jnp.concatenate(
        [block_for(0)] + [exchange(block_for(distance), distance) for distance in range(1, GROUP)], axis=0
    )
    outs = jnp.einsum("tmk,mrk->tmr", out_grads, out_proj, preferred_element_type=F32).astype(BF16)
    outs = outs.reshape(local_tokens, PAIR).T
    shard, outs = lax.optimization_barrier((shard, outs))
    shards = [shard] + [exchange(shard, distance) for distance in range(GROUP, devices, GROUP)]
    keep_cov, send_cov, keep_mom, send_mom = statistics(
        module.reshape(1), layer_input, in_proj.reshape(PAIR, in_proj.shape[2]), outs
    )
    cov = keep_cov + exchange(send_cov, 1)
    recv_mom = exchange(send_mom, 1)
    cov = cov + exchange(cov, 2)
    moments = [keep_mom, recv_mom, exchange(keep_mom, 2), exchange(recv_mom, 2)]
    cov, shards = lax.optimization_barrier((cov, shards))
    cov = cov + sum(exchange(cov, distance) for distance in range(GROUP, devices, GROUP))
    partial = score(place.reshape(1), inverse(cov, local_tokens * devices), moments, shards, local_queries)
    seqs = local_tokens // LEN
    result = partial[:seqs]
    for distance in range(1, GROUP):
        result = result + exchange(partial[distance * seqs : (distance + 1) * seqs], distance)
    return result


def solution(mesh):
    return jax.shard_map(
        per_device,
        mesh=mesh,
        in_specs=(
            P(("parts", "dp"), None),
            P(("parts", "dp"), None, None),
            P(),
            P(),
            P(("parts", "dp"), None),
        ),
        out_specs=P(("parts", "dp"), None),
        check_vma=False,
    )
```

```python
import functools

import jax
import jax.numpy as jnp
from jax import lax
from jax.experimental import pallas as pl
from jax.experimental.pallas import tpu as pltpu
from jax.sharding import Mesh, PartitionSpec as P

R = 64
LEN = 128
PAIR = 2 * R
DAMPING = 0.1
STEP = 512
BLOCK = 4
GROUP = 4

F32 = jnp.float32
BF16 = jnp.bfloat16
MIB = 1024 * 1024


def dot(a, b, dims, precision=None):
    return lax.dot_general(a, b, (dims, ((), ())), precision=precision, preferred_element_type=F32)


NN = ((1,), (0,))
NT = ((1,), (1,))
TN = ((0,), (0,))


def statistics_kernel(
    x_hbm, g_hbm, w_hbm, v_hbm, cov_ref, mom_ref, x_buf, g_buf, w_buf, v_buf, total, both, x_sem, g_sem, w_sem, v_sem
):
    chunks, tokens, step = x_buf.shape
    seqs = tokens // LEN

    def x_copy(k):
        return pltpu.make_async_copy(x_hbm.at[:, k * step : (k + 1) * step], x_buf.at[k], x_sem.at[k])

    def w_copy(k):
        return pltpu.make_async_copy(w_hbm.at[:, k * step : (k + 1) * step], w_buf.at[k], w_sem.at[k])

    def g_copy(seq):
        return pltpu.make_async_copy(
            g_hbm.at[pl.ds(seq * LEN, LEN)], g_buf.at[pl.ds(seq * LEN, LEN)], g_sem.at[seq]
        )

    v_copy = pltpu.make_async_copy(v_hbm, v_buf, v_sem)
    v_copy.start()
    for seq in range(seqs):
        g_copy(seq).start()
    for k in range(chunks):
        w_copy(k).start()
        x_copy(k).start()
    v_copy.wait()

    @pl.loop(0, seqs)
    def _(seq):
        g_copy(seq).wait()
        rows = pl.ds(pl.multiple_of(seq * LEN, LEN), LEN)
        outs = [dot(g_buf[rows, m, :], v_buf[m], NT) for m in range(2)]
        both[rows, PAIR:] = jnp.concatenate(outs, axis=1).astype(BF16)

    for k in range(chunks):
        w_copy(k).wait()
        x_copy(k).wait()
        term = dot(x_buf[k], w_buf[k], NT)
        if k == 0:
            total[...] = term
        elif k < chunks - 1:
            total[...] += term
        else:
            both[:, :PAIR] = (total[...] + term).astype(BF16)

    low = lax.broadcasted_iota(jnp.int32, (R, PAIR), 1) < R
    products = []
    for seq in range(seqs):
        part = both[seq * LEN : (seq + 1) * LEN, :]
        products.append(dot(part, part, TN))
    for pair in range(seqs // 2):
        blocks = [products[2 * pair + i][PAIR:, :PAIR] * (1.0 / LEN) for i in range(2)]
        lanes = slice(pair * PAIR, (pair + 1) * PAIR)
        mom_ref[0, :, lanes] = jnp.where(low, blocks[0][:R], pltpu.roll(blocks[1][:R], R, 1))
        mom_ref[1, :, lanes] = jnp.where(low, pltpu.roll(blocks[0][R:], R, 1), blocks[1][R:])
    mom_ref[2] = mom_ref[0]
    mom_ref[3] = mom_ref[1]
    cov_in = sum(product[:PAIR, :PAIR] for product in products)
    cov_out = sum(product[PAIR:, PAIR:] for product in products)
    cov0 = jnp.where(low, cov_in[:R], pltpu.roll(cov_out[:R], R, 1))
    cov1 = jnp.where(low, pltpu.roll(cov_in[R:], R, 1), cov_out[R:])
    for group in range(GROUP):
        cov_ref[group] = (cov0, cov1)[group & 1]


def statistics(layer_input, out_grads, in_flat, out_proj):
    tokens, width = layer_input.shape
    seqs = tokens // LEN
    chunks = width // STEP
    vmem = pl.BlockSpec(memory_space=pltpu.VMEM)
    return pl.pallas_call(
        statistics_kernel,
        in_specs=[pl.BlockSpec(memory_space=pl.ANY)] * 4,
        out_specs=[vmem, vmem],
        out_shape=[
            jax.ShapeDtypeStruct((GROUP, R, PAIR), F32),
            jax.ShapeDtypeStruct((GROUP, R, seqs * R), F32),
        ],
        scratch_shapes=[
            pltpu.VMEM((chunks, tokens, STEP), BF16),
            pltpu.VMEM(out_grads.shape, BF16),
            pltpu.VMEM((chunks, PAIR, STEP), BF16),
            pltpu.VMEM(out_proj.shape, BF16),
            pltpu.VMEM((tokens, PAIR), F32),
            pltpu.VMEM((tokens, 2 * PAIR), BF16),
            pltpu.SemaphoreType.DMA((chunks,)),
            pltpu.SemaphoreType.DMA((seqs,)),
            pltpu.SemaphoreType.DMA((chunks,)),
            pltpu.SemaphoreType.DMA,
        ],
        compiler_params=pltpu.CompilerParams(vmem_limit_bytes=48 * MIB),
        cost_estimate=pl.CostEstimate(
            flops=3 * tokens * width * PAIR, bytes_accessed=3 * tokens * width, transcendentals=0
        ),
        name="statistics",
    )(layer_input, out_grads, in_flat, out_proj)


def solve_block(p, rows):
    det = 1.0 / (p[0][0] * p[1][1] - p[0][1] * p[0][1])
    a, b, c = p[1][1] * det, -p[0][1] * det, p[0][0] * det
    t = [[a * p[0][j] + b * p[1][j], b * p[0][j] + c * p[1][j]] for j in (2, 3)]
    s22 = p[2][2] - p[0][2] * t[0][0] - p[1][2] * t[0][1]
    s23 = p[2][3] - p[0][2] * t[1][0] - p[1][2] * t[1][1]
    s33 = p[3][3] - p[0][3] * t[1][0] - p[1][3] * t[1][1]
    det = 1.0 / (s22 * s33 - s23 * s23)
    y0 = a * rows[0] + b * rows[1]
    y1 = b * rows[0] + c * rows[1]
    z2 = rows[2] - p[0][2] * y0 - p[1][2] * y1
    z3 = rows[3] - p[0][3] * y0 - p[1][3] * y1
    x2 = (s33 * z2 - s23 * z3) * det
    x3 = (s22 * z3 - s23 * z2) * det
    return [y0 - t[0][0] * x2 - t[1][0] * x3, y1 - t[0][1] * x2 - t[1][1] * x3, x2, x3]


def invert_pair(matrix):
    lane = lax.broadcasted_iota(jnp.int32, (8, PAIR), 1)
    row = lax.broadcasted_iota(jnp.int32, (8, PAIR), 0)
    column = lane % R
    base = lane - column
    work = [matrix[8 * g : 8 * g + 8] for g in range(R // 8)]
    for k in range(0, R, BLOCK):
        cols = [[jnp.take_along_axis(part, base + (k + j), axis=1) for j in range(BLOCK)] for part in work]
        home, at = k // 8, k % 8
        inside = (column >= k) & (column < k + BLOCK)
        pivots = [[cols[home][j][at + i : at + i + 1] for j in range(BLOCK)] for i in range(BLOCK)]
        rows = [
            jnp.where(
                inside[:1], jnp.where(column[:1] == k + i, 1.0, 0.0), work[home][at + i : at + i + 1]
            )
            for i in range(BLOCK)
        ]
        solved = solve_block(pivots, rows)
        for g in range(R // 8):
            part = jnp.where(inside, 0.0, work[g])
            col = cols[g]
            if g == home:
                block_row = (row >= at) & (row < at + BLOCK)
                part = jnp.where(block_row, 0.0, part)
                col = [
                    jnp.where(block_row, jnp.where(row == at + j, -1.0, 0.0), col[j]) for j in range(BLOCK)
                ]
            work[g] = part - (col[0] * solved[0] + col[1] * solved[1]) - (col[2] * solved[2] + col[3] * solved[3])
    return jnp.concatenate(work, axis=0)


def inverse_kernel(total_tokens, cov_ref, inv_ref):
    row = lax.broadcasted_iota(jnp.int32, (R, PAIR), 0)
    lane = lax.broadcasted_iota(jnp.int32, (R, PAIR), 1)
    low = lane < R
    column = jnp.where(low, lane, lane - R)
    cov = jnp.sum(cov_ref[...], axis=0)
    diagonal = jnp.where(row == column, cov, 0.0)
    trace_in = jnp.sum(jnp.where(low, diagonal, 0.0), keepdims=True)
    trace_out = jnp.sum(jnp.where(low, 0.0, diagonal), keepdims=True)
    scale = R / jnp.where(low, trace_in, trace_out)
    inv_ref[...] = invert_pair(cov * scale + jnp.where(row == column, DAMPING, 0.0)) * (scale * total_tokens)


def inverse(cov, total_tokens):
    vmem = pl.BlockSpec(memory_space=pltpu.VMEM)
    return pl.pallas_call(
        functools.partial(inverse_kernel, total_tokens),
        in_specs=[vmem],
        out_specs=vmem,
        out_shape=jax.ShapeDtypeStruct(cov.shape[1:], F32),
        compiler_params=pltpu.CompilerParams(vmem_limit_bytes=16 * MIB),
        cost_estimate=pl.CostEstimate(flops=4 * 10**9, bytes_accessed=2**16, transcendentals=0),
        name="inverse",
    )(cov)


def scores_kernel(upper_ref, inv_ref, moments_ref, queries_ref, out_ref, flat_ref):
    upper = upper_ref[0] == 1
    low = lax.broadcasted_iota(jnp.int32, (R, PAIR), 1) < R
    inv = inv_ref[...]
    tiles = R // 4
    even = [inv_ref[pl.ds(start, tiles, stride=2), :] for start in (0, R // 2)]
    odd = [inv_ref[pl.ds(start + 1, tiles, stride=2), :] for start in (0, R // 2)]
    left = jnp.concatenate([jnp.where(upper, even[1], even[0]), jnp.where(upper, odd[1], odd[0])], axis=0)
    left = pltpu.roll(left, R, 1)[:, :R]
    moments = jnp.concatenate([moments_ref[group] for group in range(GROUP)], axis=1)
    mixed = dot(left, moments, NN, lax.Precision.HIGHEST)
    pairs = moments.shape[1] // PAIR
    stack = jnp.concatenate(
        [
            jnp.concatenate(
                [mixed[:tiles, j * PAIR : (j + 1) * PAIR], mixed[tiles:, j * PAIR : (j + 1) * PAIR]], axis=1
            )
            for j in range(pairs)
        ],
        axis=0,
    )
    zero = jnp.zeros((R, PAIR), F32)
    at_low = jnp.where(low, inv, 0.0)
    at_high = pltpu.roll(at_low, R, 1)
    right = jnp.concatenate(
        [
            jnp.concatenate([at_low, zero], axis=1),
            jnp.concatenate([zero, at_low], axis=1),
            jnp.concatenate([at_high, zero], axis=1),
            jnp.concatenate([zero, at_high], axis=1),
        ],
        axis=0,
    )
    done = dot(stack, right, NN, lax.Precision.HIGHEST)
    for j in range(pairs):
        rows = done[j * tiles : (j + 1) * tiles]
        flat_ref[(2 * j) * tiles : (2 * j + 1) * tiles, :] = rows[:, :PAIR]
        flat_ref[(2 * j + 1) * tiles : (2 * j + 2) * tiles, :] = rows[:, PAIR:]
    flat = jnp.concatenate(
        [flat_ref[pl.ds(k, 2 * pairs, stride=tiles), :].astype(BF16) for k in range(tiles)], axis=1
    )
    out_ref[...] = dot(flat, queries_ref[...], NT)


def score(upper, inv, moments, queries):
    seqs = GROUP * moments.shape[2] // R
    vmem = pl.BlockSpec(memory_space=pltpu.VMEM)
    return pl.pallas_call(
        scores_kernel,
        in_specs=[pl.BlockSpec(memory_space=pltpu.SMEM), vmem, vmem, vmem],
        out_specs=vmem,
        out_shape=jax.ShapeDtypeStruct((seqs, queries.shape[0]), F32),
        scratch_shapes=[pltpu.VMEM((seqs * R // 4, PAIR), F32)],
        compiler_params=pltpu.CompilerParams(vmem_limit_bytes=16 * MIB),
        name="scores",
    )(upper, inv, moments, queries)


def swap(value, axis):
    return lax.all_to_all(value, axis, 0, 0, tiled=False)


def per_device(layer_input, out_grads, in_proj, out_proj, queries):
    local_tokens = layer_input.shape[0]
    local_queries = queries.shape[0]
    slabs = lax.axis_size("slab")
    upper = (lax.axis_index("group").astype(jnp.int32) >> 1).reshape(1)
    quarter = queries.shape[1] // GROUP
    blocks = [queries[:, block * quarter : (block + 1) * quarter] for block in (0, 2, 1, 3)]
    shard = swap(jnp.stack(blocks), "group").reshape(GROUP * local_queries, quarter)
    every = swap(jnp.broadcast_to(shard, (slabs,) + shard.shape), "slab")
    every = every.reshape(slabs * GROUP * local_queries, quarter)
    cov, moments = statistics(
        layer_input, out_grads, in_proj.reshape(PAIR, in_proj.shape[2]), out_proj
    )
    cov = jnp.sum(swap(cov, "group"), axis=0)
    moments = swap(moments, "group")
    cov = swap(jnp.broadcast_to(cov, (slabs,) + cov.shape), "slab")
    partial = score(upper, inverse(cov, local_tokens * slabs * GROUP), moments, every)
    return jnp.sum(swap(partial.reshape(GROUP, local_tokens // LEN, partial.shape[1]), "group"), axis=0)


def solution(mesh):
    parts, devices = mesh.devices.shape
    grid = Mesh(mesh.devices.reshape(parts, devices // GROUP, GROUP), ("parts", "slab", "group"))
    split = ("parts", "slab", "group")
    return jax.shard_map(
        per_device,
        mesh=grid,
        in_specs=(P(split, None), P(split, None, None), P(), P(), P(split, None)),
        out_specs=P(split, None),
        check_vma=False,
    )
```

```python
import functools

import jax
import jax.numpy as jnp
from jax import lax
from jax.experimental import pallas as pl
from jax.experimental.pallas import tpu as pltpu
from jax.sharding import PartitionSpec as P

R = 64
LEN = 128
PAIR = 2 * R
DAMPING = 0.1
STEP = 512
BLOCK = 4
GROUP = 4

F32 = jnp.float32
BF16 = jnp.bfloat16
MIB = 1024 * 1024


def dot(a, b, dims, precision=None):
    return lax.dot_general(a, b, (dims, ((), ())), precision=precision, preferred_element_type=F32)


NN = ((1,), (0,))
NT = ((1,), (1,))
TN = ((0,), (0,))


def project_kernel(x_hbm, w_hbm, acts_ref, x_buf, w_buf, total, x_sem, w_sem):
    chunks, _, step = x_buf.shape

    def x_copy(k):
        return pltpu.make_async_copy(x_hbm.at[:, k * step : (k + 1) * step], x_buf.at[k], x_sem.at[k])

    def w_copy(k):
        return pltpu.make_async_copy(w_hbm.at[:, k * step : (k + 1) * step], w_buf.at[k], w_sem.at[k])

    for k in range(chunks):
        w_copy(k).start()
        x_copy(k).start()
    for k in range(chunks):
        w_copy(k).wait()
        x_copy(k).wait()
        term = dot(x_buf[k], w_buf[k], NT)
        if k == 0:
            total[...] = term
        elif k < chunks - 1:
            total[...] += term
        else:
            acts_ref[...] = (total[...] + term).astype(BF16)


def project(layer_input, in_flat):
    tokens, width = layer_input.shape
    chunks = width // STEP
    return pl.pallas_call(
        project_kernel,
        in_specs=[pl.BlockSpec(memory_space=pl.ANY)] * 2,
        out_specs=pl.BlockSpec(memory_space=pltpu.VMEM),
        out_shape=jax.ShapeDtypeStruct((tokens, PAIR), BF16),
        scratch_shapes=[
            pltpu.VMEM((chunks, tokens, STEP), BF16),
            pltpu.VMEM((chunks, PAIR, STEP), BF16),
            pltpu.VMEM((tokens, PAIR), F32),
            pltpu.SemaphoreType.DMA((chunks,)),
            pltpu.SemaphoreType.DMA((chunks,)),
        ],
        compiler_params=pltpu.CompilerParams(vmem_limit_bytes=48 * MIB),
        cost_estimate=pl.CostEstimate(
            flops=4 * tokens * width * PAIR, bytes_accessed=2 * tokens * width, transcendentals=0
        ),
        name="project",
    )(layer_input, in_flat)


def statistics_kernel(core_ref, acts_ref, outs_ref, keep_cov, send_cov, keep_mom, send_mom):
    first = core_ref[0] == 0
    acts = acts_ref[...]
    outs = outs_ref[...]
    low = lax.broadcasted_iota(jnp.int32, (R, PAIR), 1) < R
    cov_in = dot(acts, acts, TN)
    cov_out = dot(outs, outs, NT)
    cov0 = jnp.where(low, cov_in[:R], pltpu.roll(cov_out[:R], R, 1))
    cov1 = jnp.where(low, pltpu.roll(cov_in[R:], R, 1), cov_out[R:])
    keep_cov[...] = jnp.where(first, cov0, cov1)
    send_cov[...] = jnp.where(first, cov1, cov0)
    for pair in range(acts.shape[0] // LEN // 2):
        blocks = []
        for seq in (2 * pair, 2 * pair + 1):
            rows = slice(seq * LEN, (seq + 1) * LEN)
            blocks.append(dot(outs[:, rows], acts[rows], NN) * (1.0 / LEN))
        mom0 = jnp.where(low, blocks[0][:R], pltpu.roll(blocks[1][:R], R, 1))
        mom1 = jnp.where(low, pltpu.roll(blocks[0][R:], R, 1), blocks[1][R:])
        lanes = slice(pair * PAIR, (pair + 1) * PAIR)
        keep_mom[:, lanes] = jnp.where(first, mom0, mom1)
        send_mom[:, lanes] = jnp.where(first, mom1, mom0)


def statistics(core, acts, outs):
    seqs = acts.shape[0] // LEN
    cov = jax.ShapeDtypeStruct((R, PAIR), F32)
    mom = jax.ShapeDtypeStruct((R, seqs * R), F32)
    vmem = pl.BlockSpec(memory_space=pltpu.VMEM)
    return pl.pallas_call(
        statistics_kernel,
        in_specs=[pl.BlockSpec(memory_space=pltpu.SMEM), vmem, vmem],
        out_specs=[vmem] * 4,
        out_shape=[cov, cov, mom, mom],
        compiler_params=pltpu.CompilerParams(vmem_limit_bytes=16 * MIB),
        name="statistics",
    )(core, acts, outs)


def solve_block(p, rows):
    det = 1.0 / (p[0][0] * p[1][1] - p[0][1] * p[0][1])
    a, b, c = p[1][1] * det, -p[0][1] * det, p[0][0] * det
    t = [[a * p[0][j] + b * p[1][j], b * p[0][j] + c * p[1][j]] for j in (2, 3)]
    s22 = p[2][2] - p[0][2] * t[0][0] - p[1][2] * t[0][1]
    s23 = p[2][3] - p[0][2] * t[1][0] - p[1][2] * t[1][1]
    s33 = p[3][3] - p[0][3] * t[1][0] - p[1][3] * t[1][1]
    det = 1.0 / (s22 * s33 - s23 * s23)
    y0 = a * rows[0] + b * rows[1]
    y1 = b * rows[0] + c * rows[1]
    z2 = rows[2] - p[0][2] * y0 - p[1][2] * y1
    z3 = rows[3] - p[0][3] * y0 - p[1][3] * y1
    x2 = (s33 * z2 - s23 * z3) * det
    x3 = (s22 * z3 - s23 * z2) * det
    return [y0 - t[0][0] * x2 - t[1][0] * x3, y1 - t[0][1] * x2 - t[1][1] * x3, x2, x3]


def invert_pair(matrix):
    lane = lax.broadcasted_iota(jnp.int32, (8, PAIR), 1)
    row = lax.broadcasted_iota(jnp.int32, (8, PAIR), 0)
    column = lane % R
    base = lane - column
    work = [matrix[8 * g : 8 * g + 8] for g in range(R // 8)]
    for k in range(0, R, BLOCK):
        cols = [[jnp.take_along_axis(part, base + (k + j), axis=1) for j in range(BLOCK)] for part in work]
        home, at = k // 8, k % 8
        inside = (column >= k) & (column < k + BLOCK)
        pivots = [[cols[home][j][at + i : at + i + 1] for j in range(BLOCK)] for i in range(BLOCK)]
        rows = [
            jnp.where(
                inside[:1], jnp.where(column[:1] == k + i, 1.0, 0.0), work[home][at + i : at + i + 1]
            )
            for i in range(BLOCK)
        ]
        solved = solve_block(pivots, rows)
        for g in range(R // 8):
            part = jnp.where(inside, 0.0, work[g])
            col = cols[g]
            if g == home:
                block_row = (row >= at) & (row < at + BLOCK)
                part = jnp.where(block_row, 0.0, part)
                col = [
                    jnp.where(block_row, jnp.where(row == at + j, -1.0, 0.0), col[j]) for j in range(BLOCK)
                ]
            work[g] = part - (col[0] * solved[0] + col[1] * solved[1]) - (col[2] * solved[2] + col[3] * solved[3])
    return jnp.concatenate(work, axis=0)


def inverse_kernel(total_tokens, *refs):
    cov_refs, inv_ref = refs[:-1], refs[-1]
    row = lax.broadcasted_iota(jnp.int32, (R, PAIR), 0)
    lane = lax.broadcasted_iota(jnp.int32, (R, PAIR), 1)
    low = lane < R
    column = jnp.where(low, lane, lane - R)
    cov = sum(ref[...] for ref in cov_refs)
    diagonal = jnp.where(row == column, cov, 0.0)
    trace_in = jnp.sum(jnp.where(low, diagonal, 0.0), keepdims=True)
    trace_out = jnp.sum(jnp.where(low, 0.0, diagonal), keepdims=True)
    scale = R / jnp.where(low, trace_in, trace_out)
    inv_ref[...] = invert_pair(cov * scale + jnp.where(row == column, DAMPING, 0.0)) * (scale * total_tokens)


def inverse(covs, total_tokens):
    vmem = pl.BlockSpec(memory_space=pltpu.VMEM)
    return pl.pallas_call(
        functools.partial(inverse_kernel, total_tokens),
        in_specs=[vmem] * len(covs),
        out_specs=vmem,
        out_shape=jax.ShapeDtypeStruct(covs[0].shape, F32),
        compiler_params=pltpu.CompilerParams(vmem_limit_bytes=16 * MIB),
        name="inverse",
    )(*covs)


def scores_kernel(order, place_ref, inv_ref, keep_ref, recv_ref, *refs):
    query_refs, (out_ref, flat_ref, part_ref) = refs[:-3], refs[-3:]
    place = place_ref[0]
    low = lax.broadcasted_iota(jnp.int32, (R, PAIR), 1) < R
    inv = inv_ref[...]
    tiles = R // 2
    left = jnp.concatenate([inv_ref[pl.ds(start, tiles, stride=2), :] for start in range(2)], axis=0)
    left = pltpu.roll(left, R, 1)[:, :R]
    moments = jnp.concatenate([keep_ref[...], recv_ref[...]], axis=1)
    mixed = dot(left, moments, NN, lax.Precision.HIGHEST)
    pairs = moments.shape[1] // PAIR
    stack = jnp.concatenate(
        [
            jnp.concatenate(
                [mixed[:tiles, j * PAIR : (j + 1) * PAIR], mixed[tiles:, j * PAIR : (j + 1) * PAIR]], axis=1
            )
            for j in range(pairs)
        ],
        axis=0,
    )
    zero = jnp.zeros((R, PAIR), F32)
    at_low = jnp.where(low, inv, 0.0)
    at_high = pltpu.roll(at_low, R, 1)
    right = jnp.concatenate(
        [
            jnp.concatenate([at_low, zero], axis=1),
            jnp.concatenate([zero, at_low], axis=1),
            jnp.concatenate([at_high, zero], axis=1),
            jnp.concatenate([zero, at_high], axis=1),
        ],
        axis=0,
    )
    done = dot(stack, right, NN, lax.Precision.HIGHEST)
    for j in range(pairs):
        rows = done[j * tiles : (j + 1) * tiles]
        flat_ref[(2 * j) * tiles : (2 * j + 1) * tiles, :] = rows[:, :PAIR]
        flat_ref[(2 * j + 1) * tiles : (2 * j + 2) * tiles, :] = rows[:, PAIR:]
    flat = jnp.concatenate(
        [flat_ref[pl.ds(k, 2 * pairs, stride=tiles), :].astype(BF16) for k in range(tiles)], axis=1
    )
    part = dot(jnp.concatenate([ref[...] for ref in query_refs], axis=0), flat, NT)
    group = part_ref.shape[1]
    for at, distance in enumerate(order):
        part_ref[place ^ distance] = part[at * group : (at + 1) * group]
    out_ref[...] = part_ref[...].reshape(part.shape).T


def score(place, inv, moments, queries, order):
    seqs = sum(part.shape[1] for part in moments) // R
    count = sum(part.shape[0] for part in queries)
    vmem = pl.BlockSpec(memory_space=pltpu.VMEM)
    return pl.pallas_call(
        functools.partial(scores_kernel, order),
        in_specs=[pl.BlockSpec(memory_space=pltpu.SMEM)] + [vmem] * (1 + len(moments) + len(queries)),
        out_specs=vmem,
        out_shape=jax.ShapeDtypeStruct((seqs, count), F32),
        scratch_shapes=[
            pltpu.VMEM((seqs * R // 2, PAIR), F32),
            pltpu.VMEM((len(order), count // len(order), seqs), F32),
        ],
        compiler_params=pltpu.CompilerParams(vmem_limit_bytes=16 * MIB),
        name="scores",
    )(place, inv, *moments, *queries)


def exchange(value, distance):
    return lax.ppermute(value, "dp", [(i, i ^ distance) for i in range(lax.axis_size("dp"))])


def halves(values, upper):
    picked = []
    for value in values:
        low, high = jnp.split(value, 2, axis=1)
        picked.append((jnp.where(upper, high, low), jnp.where(upper, low, high)))
    return [jnp.concatenate(side, axis=0) for side in zip(*picked)]


def per_device(layer_input, out_grads, in_proj, out_proj, queries):
    local_tokens = layer_input.shape[0]
    devices = lax.axis_size("dp")
    slabs = devices // GROUP
    place = lax.axis_index("dp").astype(jnp.int32)
    module = place & 1
    column = [queries] + [exchange(queries, slab * GROUP) for slab in range(1, slabs)]
    acts = project(layer_input, in_proj.reshape(PAIR, in_proj.shape[2]))
    acts, out_grads, column[1] = lax.optimization_barrier((acts, out_grads, column[1]))
    near, send_near = halves(column[:2], module == 1)
    outs = jnp.einsum("tmk,mrk->tmr", out_grads, out_proj, preferred_element_type=F32).astype(BF16)
    outs = outs.reshape(local_tokens, PAIR).T
    near = jnp.concatenate([near, exchange(send_near, 1)], axis=0)
    acts, outs, near, column[2] = lax.optimization_barrier((acts, outs, near, column[2]))
    keep_cov, send_cov, keep_mom, send_mom = statistics(module.reshape(1), acts, outs)
    cov = keep_cov + exchange(send_cov, 1)
    moments = [keep_mom, exchange(send_mom, 1)]
    cov, column[3] = lax.optimization_barrier((cov, column[3]))
    cov = cov + exchange(cov, 2)
    far, send_far = halves(column[2:], module == 1)
    far = jnp.concatenate([far, exchange(send_far, 1)], axis=0)
    cov, moments, far = lax.optimization_barrier((cov, moments, far))
    across = exchange(near, 2)
    cov = cov + exchange(cov, GROUP)
    cov, across = lax.optimization_barrier((cov, across))
    distance = 2 * GROUP
    while distance < devices:
        last = exchange(cov, distance)
        if 2 * distance < devices:
            cov = cov + last
        distance *= 2
    inv = inverse([cov, last], local_tokens * devices)
    gathered = [near, across, far, exchange(far, 2)]
    order = [
        slab * GROUP + 2 * over + core
        for part in (range(2), range(2, slabs))
        for over in range(2)
        for core in range(2)
        for slab in part
    ]
    partial = score(place.reshape(1), inv, moments, gathered, order)
    seqs = local_tokens // LEN
    return partial[:seqs] + exchange(partial[seqs:], 1)


def solution(mesh):
    return jax.shard_map(
        per_device,
        mesh=mesh,
        in_specs=(
            P(("parts", "dp"), None),
            P(("parts", "dp"), None, None),
            P(),
            P(),
            P(("parts", "dp"), None),
        ),
        out_specs=P(("parts", "dp"), None),
        check_vma=False,
    )
```

```python
import functools

import jax
import jax.numpy as jnp
from jax import lax
from jax.experimental import pallas as pl
from jax.experimental.pallas import tpu as pltpu
from jax.sharding import PartitionSpec as P

R = 64
LEN = 128
PAIR = 2 * R
DAMPING = 0.1
ROWS = 256
BLOCK = 4
GROUP = 4

F32 = jnp.float32
BF16 = jnp.bfloat16
MIB = 1024 * 1024


def dot(a, b, dims, precision=None):
    return lax.dot_general(a, b, (dims, ((), ())), precision=precision, preferred_element_type=F32)


NN = ((1,), (0,))
NT = ((1,), (1,))


def stage_kernel(core_ref, source_ref, all_ref, keep_ref, send_ref):
    first = core_ref[0] == 0
    values = source_ref[...]
    half = values.shape[1] // 2
    low, high = values[:, :half], values[:, half:]
    all_ref[...] = values
    keep_ref[...] = jnp.where(first, low, high)
    send_ref[...] = jnp.where(first, high, low)


def stage(core, queries):
    rows, entries = queries.shape
    vmem = pl.BlockSpec(memory_space=pltpu.VMEM)
    half = jax.ShapeDtypeStruct((rows, entries // 2), BF16)
    return pl.pallas_call(
        stage_kernel,
        in_specs=[pl.BlockSpec(memory_space=pltpu.SMEM), vmem],
        out_specs=[vmem] * 3,
        out_shape=[jax.ShapeDtypeStruct(queries.shape, BF16), half, half],
        compiler_params=pltpu.CompilerParams(vmem_limit_bytes=16 * MIB),
        cost_estimate=pl.CostEstimate(flops=8 * 10**9, bytes_accessed=2**18, transcendentals=0),
        name="stage",
    )(core, queries)


def project_kernel(x_ref, w_ref, acts_ref):
    tokens = x_ref.shape[0]
    for at in range(0, tokens, ROWS):
        acts_ref[:, at : at + ROWS] = dot(w_ref[...], x_ref[at : at + ROWS], NT).astype(BF16)


def project(layer_input, in_flat):
    tokens, width = layer_input.shape
    vmem = pl.BlockSpec(memory_space=pltpu.VMEM)
    return pl.pallas_call(
        project_kernel,
        in_specs=[vmem, vmem],
        out_specs=vmem,
        out_shape=jax.ShapeDtypeStruct((PAIR, tokens), BF16),
        compiler_params=pltpu.CompilerParams(vmem_limit_bytes=24 * MIB),
        cost_estimate=pl.CostEstimate(
            flops=4 * tokens * width * PAIR, bytes_accessed=2 * tokens * width, transcendentals=0
        ),
        name="project",
    )(layer_input, in_flat)


def statistics_kernel(core_ref, acts_ref, outs_ref, keep_cov, send_cov, keep_mom, send_mom):
    first = core_ref[0] == 0
    acts = acts_ref[...]
    outs = outs_ref[...]
    low = lax.broadcasted_iota(jnp.int32, (R, PAIR), 1) < R
    cov_in = dot(acts, acts, NT)
    cov_out = dot(outs, outs, NT)
    cov0 = jnp.where(low, cov_in[:R], pltpu.roll(cov_out[:R], R, 1))
    cov1 = jnp.where(low, pltpu.roll(cov_in[R:], R, 1), cov_out[R:])
    keep_cov[...] = jnp.where(first, cov0, cov1)
    send_cov[...] = jnp.where(first, cov1, cov0)
    for pair in range(acts.shape[1] // LEN // 2):
        blocks = []
        for seq in (2 * pair, 2 * pair + 1):
            tokens = slice(seq * LEN, (seq + 1) * LEN)
            blocks.append(dot(outs[:, tokens], acts[:, tokens], NT) * (1.0 / LEN))
        mom0 = jnp.where(low, blocks[0][:R], pltpu.roll(blocks[1][:R], R, 1))
        mom1 = jnp.where(low, pltpu.roll(blocks[0][R:], R, 1), blocks[1][R:])
        lanes = slice(pair * PAIR, (pair + 1) * PAIR)
        keep_mom[:, lanes] = jnp.where(first, mom0, mom1)
        send_mom[:, lanes] = jnp.where(first, mom1, mom0)


def statistics(core, acts, outs):
    seqs = acts.shape[1] // LEN
    cov = jax.ShapeDtypeStruct((R, PAIR), F32)
    mom = jax.ShapeDtypeStruct((R, seqs * R), F32)
    vmem = pl.BlockSpec(memory_space=pltpu.VMEM)
    return pl.pallas_call(
        statistics_kernel,
        in_specs=[pl.BlockSpec(memory_space=pltpu.SMEM), vmem, vmem],
        out_specs=[vmem] * 4,
        out_shape=[cov, cov, mom, mom],
        compiler_params=pltpu.CompilerParams(vmem_limit_bytes=16 * MIB),
        name="statistics",
    )(core, acts, outs)


def solve_block(p, rows):
    det = 1.0 / (p[0][0] * p[1][1] - p[0][1] * p[0][1])
    a, b, c = p[1][1] * det, -p[0][1] * det, p[0][0] * det
    t = [[a * p[0][j] + b * p[1][j], b * p[0][j] + c * p[1][j]] for j in (2, 3)]
    s22 = p[2][2] - p[0][2] * t[0][0] - p[1][2] * t[0][1]
    s23 = p[2][3] - p[0][2] * t[1][0] - p[1][2] * t[1][1]
    s33 = p[3][3] - p[0][3] * t[1][0] - p[1][3] * t[1][1]
    det = 1.0 / (s22 * s33 - s23 * s23)
    y0 = a * rows[0] + b * rows[1]
    y1 = b * rows[0] + c * rows[1]
    z2 = rows[2] - p[0][2] * y0 - p[1][2] * y1
    z3 = rows[3] - p[0][3] * y0 - p[1][3] * y1
    x2 = (s33 * z2 - s23 * z3) * det
    x3 = (s22 * z3 - s23 * z2) * det
    return [y0 - t[0][0] * x2 - t[1][0] * x3, y1 - t[0][1] * x2 - t[1][1] * x3, x2, x3]


def invert_pair(matrix):
    lane = lax.broadcasted_iota(jnp.int32, (8, PAIR), 1)
    row = lax.broadcasted_iota(jnp.int32, (8, PAIR), 0)
    column = lane % R
    base = lane - column
    work = [matrix[8 * g : 8 * g + 8] for g in range(R // 8)]
    for k in range(0, R, BLOCK):
        cols = [[jnp.take_along_axis(part, base + (k + j), axis=1) for j in range(BLOCK)] for part in work]
        home, at = k // 8, k % 8
        inside = (column >= k) & (column < k + BLOCK)
        pivots = [[cols[home][j][at + i : at + i + 1] for j in range(BLOCK)] for i in range(BLOCK)]
        rows = [
            jnp.where(
                inside[:1], jnp.where(column[:1] == k + i, 1.0, 0.0), work[home][at + i : at + i + 1]
            )
            for i in range(BLOCK)
        ]
        solved = solve_block(pivots, rows)
        for g in range(R // 8):
            part = jnp.where(inside, 0.0, work[g])
            col = cols[g]
            if g == home:
                block_row = (row >= at) & (row < at + BLOCK)
                part = jnp.where(block_row, 0.0, part)
                col = [
                    jnp.where(block_row, jnp.where(row == at + j, -1.0, 0.0), col[j]) for j in range(BLOCK)
                ]
            work[g] = part - (col[0] * solved[0] + col[1] * solved[1]) - (col[2] * solved[2] + col[3] * solved[3])
    return jnp.concatenate(work, axis=0)


def inverse_kernel(total_tokens, *refs):
    cov_refs, inv_ref = refs[:-1], refs[-1]
    row = lax.broadcasted_iota(jnp.int32, (R, PAIR), 0)
    lane = lax.broadcasted_iota(jnp.int32, (R, PAIR), 1)
    low = lane < R
    column = jnp.where(low, lane, lane - R)
    cov = sum(ref[...] for ref in cov_refs)
    diagonal = jnp.where(row == column, cov, 0.0)
    trace_in = jnp.sum(jnp.where(low, diagonal, 0.0), keepdims=True)
    trace_out = jnp.sum(jnp.where(low, 0.0, diagonal), keepdims=True)
    scale = R / jnp.where(low, trace_in, trace_out)
    inv_ref[...] = invert_pair(cov * scale + jnp.where(row == column, DAMPING, 0.0)) * (scale * total_tokens)


def inverse(covs, total_tokens):
    vmem = pl.BlockSpec(memory_space=pltpu.VMEM)
    return pl.pallas_call(
        functools.partial(inverse_kernel, total_tokens),
        in_specs=[vmem] * len(covs),
        out_specs=vmem,
        out_shape=jax.ShapeDtypeStruct(covs[0].shape, F32),
        compiler_params=pltpu.CompilerParams(vmem_limit_bytes=16 * MIB),
        name="inverse",
    )(*covs)


def scores_kernel(order, place_ref, inv_ref, keep_ref, recv_ref, *refs):
    query_refs, (out_ref, flat_ref, part_ref) = refs[:-3], refs[-3:]
    place = place_ref[0]
    low = lax.broadcasted_iota(jnp.int32, (R, PAIR), 1) < R
    inv = inv_ref[...]
    tiles = R // 2
    left = jnp.concatenate([inv_ref[pl.ds(start, tiles, stride=2), :] for start in range(2)], axis=0)
    left = pltpu.roll(left, R, 1)[:, :R]
    moments = jnp.concatenate([keep_ref[...], recv_ref[...]], axis=1)
    mixed = dot(left, moments, NN, lax.Precision.HIGHEST)
    pairs = moments.shape[1] // PAIR
    stack = jnp.concatenate(
        [
            jnp.concatenate(
                [mixed[:tiles, j * PAIR : (j + 1) * PAIR], mixed[tiles:, j * PAIR : (j + 1) * PAIR]], axis=1
            )
            for j in range(pairs)
        ],
        axis=0,
    )
    zero = jnp.zeros((R, PAIR), F32)
    at_low = jnp.where(low, inv, 0.0)
    at_high = pltpu.roll(at_low, R, 1)
    right = jnp.concatenate(
        [
            jnp.concatenate([at_low, zero], axis=1),
            jnp.concatenate([zero, at_low], axis=1),
            jnp.concatenate([at_high, zero], axis=1),
            jnp.concatenate([zero, at_high], axis=1),
        ],
        axis=0,
    )
    done = dot(stack, right, NN, lax.Precision.HIGHEST)
    for j in range(pairs):
        rows = done[j * tiles : (j + 1) * tiles]
        flat_ref[(2 * j) * tiles : (2 * j + 1) * tiles, :] = rows[:, :PAIR]
        flat_ref[(2 * j + 1) * tiles : (2 * j + 2) * tiles, :] = rows[:, PAIR:]
    flat = jnp.concatenate(
        [flat_ref[pl.ds(k, 2 * pairs, stride=tiles), :].astype(BF16) for k in range(tiles)], axis=1
    )
    part = dot(jnp.concatenate([ref[...] for ref in query_refs], axis=0), flat, NT)
    group = part_ref.shape[1]
    for at, distance in enumerate(order):
        part_ref[place ^ distance] = part[at * group : (at + 1) * group]
    out_ref[...] = part_ref[...].reshape(part.shape).T


def score(place, inv, moments, queries, order):
    seqs = sum(part.shape[1] for part in moments) // R
    count = sum(part.shape[0] for part in queries)
    vmem = pl.BlockSpec(memory_space=pltpu.VMEM)
    return pl.pallas_call(
        functools.partial(scores_kernel, order),
        in_specs=[pl.BlockSpec(memory_space=pltpu.SMEM)] + [vmem] * (1 + len(moments) + len(queries)),
        out_specs=vmem,
        out_shape=jax.ShapeDtypeStruct((seqs, count), F32),
        scratch_shapes=[
            pltpu.VMEM((seqs * R // 2, PAIR), F32),
            pltpu.VMEM((len(order), count // len(order), seqs), F32),
        ],
        compiler_params=pltpu.CompilerParams(vmem_limit_bytes=16 * MIB),
        name="scores",
    )(place, inv, *moments, *queries)


def exchange(value, distance):
    return lax.ppermute(value, "dp", [(i, i ^ distance) for i in range(lax.axis_size("dp"))])


def halves(value, upper):
    low, high = jnp.split(value, 2, axis=1)
    return jnp.where(upper, high, low), jnp.where(upper, low, high)


def per_device(layer_input, out_grads, in_proj, out_proj, queries):
    local_tokens = layer_input.shape[0]
    devices = lax.axis_size("dp")
    slabs = devices // GROUP
    place = lax.axis_index("dp").astype(jnp.int32)
    module = place & 1
    own, near, send_near = stage(module.reshape(1), queries)
    column = [own] + [exchange(own, slab * GROUP) for slab in range(1, slabs)]
    acts = project(layer_input, in_proj.reshape(PAIR, in_proj.shape[2]))
    acts, out_grads, column[1] = lax.optimization_barrier((acts, out_grads, column[1]))
    keep, send = halves(column[1], module == 1)
    near = jnp.concatenate([near, keep], axis=0)
    send_near = jnp.concatenate([send_near, send], axis=0)
    outs = jnp.einsum("tmk,mrk->tmr", out_grads, out_proj, preferred_element_type=F32).astype(BF16)
    outs = outs.reshape(local_tokens, PAIR).T
    near = jnp.concatenate([near, exchange(send_near, 1)], axis=0)
    acts, outs, near = lax.optimization_barrier((acts, outs, near))
    keep_cov, send_cov, keep_mom, send_mom = statistics(module.reshape(1), acts, outs)
    cov = keep_cov + exchange(send_cov, 1)
    moments = [keep_mom, exchange(send_mom, 1)]
    cov, column[2] = lax.optimization_barrier((cov, column[2]))
    cov = cov + exchange(cov, 2)
    far, send_far = zip(*(halves(value, module == 1) for value in column[2:]))
    far, send_far = jnp.concatenate(far, axis=0), jnp.concatenate(send_far, axis=0)
    far = jnp.concatenate([far, exchange(send_far, 1)], axis=0)
    cov, moments, far = lax.optimization_barrier((cov, moments, far))
    across = exchange(near, 2)
    cov = cov + exchange(cov, GROUP)
    distance = 2 * GROUP
    while distance < devices:
        last = exchange(cov, distance)
        if 2 * distance < devices:
            cov = cov + last
        distance *= 2
    cov, last, across = lax.optimization_barrier((cov, last, across))
    inv = inverse([cov, last], local_tokens * devices)
    gathered = [near, across, far, exchange(far, 2)]
    order = [
        slab * GROUP + 2 * over + core
        for part in (range(2), range(2, slabs))
        for over in range(2)
        for core in range(2)
        for slab in part
    ]
    partial = score(place.reshape(1), inv, moments, gathered, order)
    seqs = local_tokens // LEN
    return partial[:seqs] + exchange(partial[seqs:], 1)


def solution(mesh):
    return jax.shard_map(
        per_device,
        mesh=mesh,
        in_specs=(
            P(("parts", "dp"), None),
            P(("parts", "dp"), None, None),
            P(),
            P(),
            P(("parts", "dp"), None),
        ),
        out_specs=P(("parts", "dp"), None),
        check_vma=False,
    )
```

```python
import functools

import jax
import jax.numpy as jnp
from jax import lax
from jax.experimental import pallas as pl
from jax.experimental.pallas import tpu as pltpu
from jax.sharding import PartitionSpec as P

R = 64
LEN = 128
PAIR = 2 * R
DAMPING = 0.1
ROWS = 256
STAGE = 8 * 10**10
BLOCK = 4
GROUP = 4

F32 = jnp.float32
BF16 = jnp.bfloat16
MIB = 1024 * 1024


def dot(a, b, dims, precision=None):
    return lax.dot_general(a, b, (dims, ((), ())), precision=precision, preferred_element_type=F32)


NN = ((1,), (0,))
NT = ((1,), (1,))


def place_kernel(out_ref):
    out_ref[0] = lax.axis_index("dp")


def own_place():
    return pl.pallas_call(
        place_kernel,
        out_specs=pl.BlockSpec(memory_space=pltpu.SMEM),
        out_shape=jax.ShapeDtypeStruct((1,), jnp.int32),
        compiler_params=pltpu.CompilerParams(vmem_limit_bytes=MIB),
        cost_estimate=pl.CostEstimate(flops=STAGE, bytes_accessed=8, transcendentals=0),
        name="own_place",
    )()


def project_kernel(x_ref, w_ref, acts_ref):
    tokens = x_ref.shape[0]
    for at in range(0, tokens, ROWS):
        acts_ref[:, at : at + ROWS] = dot(w_ref[...], x_ref[at : at + ROWS], NT).astype(BF16)


def project(layer_input, in_flat):
    tokens, width = layer_input.shape
    vmem = pl.BlockSpec(memory_space=pltpu.VMEM)
    return pl.pallas_call(
        project_kernel,
        in_specs=[vmem, vmem],
        out_specs=vmem,
        out_shape=jax.ShapeDtypeStruct((PAIR, tokens), BF16),
        compiler_params=pltpu.CompilerParams(vmem_limit_bytes=24 * MIB),
        cost_estimate=pl.CostEstimate(
            flops=4 * tokens * width * PAIR, bytes_accessed=2 * tokens * width, transcendentals=0
        ),
        name="project",
    )(layer_input, in_flat)


def statistics_kernel(place_ref, acts_ref, outs_ref, keep_cov, send_cov, keep_mom, send_mom):
    first = place_ref[0] & 1 == 0
    acts = acts_ref[...]
    outs = outs_ref[...]
    low = lax.broadcasted_iota(jnp.int32, (R, PAIR), 1) < R
    cov_in = dot(acts, acts, NT)
    cov_out = dot(outs, outs, NT)
    cov0 = jnp.where(low, cov_in[:R], pltpu.roll(cov_out[:R], R, 1))
    cov1 = jnp.where(low, pltpu.roll(cov_in[R:], R, 1), cov_out[R:])
    keep_cov[...] = jnp.where(first, cov0, cov1)
    send_cov[...] = jnp.where(first, cov1, cov0)
    for pair in range(acts.shape[1] // LEN // 2):
        blocks = []
        for seq in (2 * pair, 2 * pair + 1):
            tokens = slice(seq * LEN, (seq + 1) * LEN)
            blocks.append(dot(outs[:, tokens], acts[:, tokens], NT) * (1.0 / LEN))
        mom0 = jnp.where(low, blocks[0][:R], pltpu.roll(blocks[1][:R], R, 1))
        mom1 = jnp.where(low, pltpu.roll(blocks[0][R:], R, 1), blocks[1][R:])
        lanes = slice(pair * PAIR, (pair + 1) * PAIR)
        keep_mom[:, lanes] = jnp.where(first, mom0, mom1)
        send_mom[:, lanes] = jnp.where(first, mom1, mom0)


def statistics(place, acts, outs):
    seqs = acts.shape[1] // LEN
    cov = jax.ShapeDtypeStruct((R, PAIR), F32)
    mom = jax.ShapeDtypeStruct((R, seqs * R), F32)
    vmem = pl.BlockSpec(memory_space=pltpu.VMEM)
    return pl.pallas_call(
        statistics_kernel,
        in_specs=[pl.BlockSpec(memory_space=pltpu.SMEM), vmem, vmem],
        out_specs=[vmem] * 4,
        out_shape=[cov, cov, mom, mom],
        compiler_params=pltpu.CompilerParams(vmem_limit_bytes=16 * MIB),
        name="statistics",
    )(place, acts, outs)


def solve_block(p, rows):
    det = 1.0 / (p[0][0] * p[1][1] - p[0][1] * p[0][1])
    a, b, c = p[1][1] * det, -p[0][1] * det, p[0][0] * det
    t = [[a * p[0][j] + b * p[1][j], b * p[0][j] + c * p[1][j]] for j in (2, 3)]
    s22 = p[2][2] - p[0][2] * t[0][0] - p[1][2] * t[0][1]
    s23 = p[2][3] - p[0][2] * t[1][0] - p[1][2] * t[1][1]
    s33 = p[3][3] - p[0][3] * t[1][0] - p[1][3] * t[1][1]
    det = 1.0 / (s22 * s33 - s23 * s23)
    y0 = a * rows[0] + b * rows[1]
    y1 = b * rows[0] + c * rows[1]
    z2 = rows[2] - p[0][2] * y0 - p[1][2] * y1
    z3 = rows[3] - p[0][3] * y0 - p[1][3] * y1
    x2 = (s33 * z2 - s23 * z3) * det
    x3 = (s22 * z3 - s23 * z2) * det
    return [y0 - t[0][0] * x2 - t[1][0] * x3, y1 - t[0][1] * x2 - t[1][1] * x3, x2, x3]


def invert_pair(matrix):
    lane = lax.broadcasted_iota(jnp.int32, (8, PAIR), 1)
    row = lax.broadcasted_iota(jnp.int32, (8, PAIR), 0)
    column = lane % R
    base = lane - column
    work = [matrix[8 * g : 8 * g + 8] for g in range(R // 8)]
    for k in range(0, R, BLOCK):
        cols = [[jnp.take_along_axis(part, base + (k + j), axis=1) for j in range(BLOCK)] for part in work]
        home, at = k // 8, k % 8
        inside = (column >= k) & (column < k + BLOCK)
        pivots = [[cols[home][j][at + i : at + i + 1] for j in range(BLOCK)] for i in range(BLOCK)]
        rows = [
            jnp.where(
                inside[:1], jnp.where(column[:1] == k + i, 1.0, 0.0), work[home][at + i : at + i + 1]
            )
            for i in range(BLOCK)
        ]
        solved = solve_block(pivots, rows)
        for g in range(R // 8):
            part = jnp.where(inside, 0.0, work[g])
            col = cols[g]
            if g == home:
                block_row = (row >= at) & (row < at + BLOCK)
                part = jnp.where(block_row, 0.0, part)
                col = [
                    jnp.where(block_row, jnp.where(row == at + j, -1.0, 0.0), col[j]) for j in range(BLOCK)
                ]
            work[g] = part - (col[0] * solved[0] + col[1] * solved[1]) - (col[2] * solved[2] + col[3] * solved[3])
    return jnp.concatenate(work, axis=0)


def inverse_kernel(total_tokens, *refs):
    cov_refs, inv_ref = refs[:-1], refs[-1]
    row = lax.broadcasted_iota(jnp.int32, (R, PAIR), 0)
    lane = lax.broadcasted_iota(jnp.int32, (R, PAIR), 1)
    low = lane < R
    column = jnp.where(low, lane, lane - R)
    cov = sum(ref[...] for ref in cov_refs)
    diagonal = jnp.where(row == column, cov, 0.0)
    trace_in = jnp.sum(jnp.where(low, diagonal, 0.0), keepdims=True)
    trace_out = jnp.sum(jnp.where(low, 0.0, diagonal), keepdims=True)
    scale = R / jnp.where(low, trace_in, trace_out)
    inv_ref[...] = invert_pair(cov * scale + jnp.where(row == column, DAMPING, 0.0)) * (scale * total_tokens)


def inverse(covs, total_tokens):
    vmem = pl.BlockSpec(memory_space=pltpu.VMEM)
    return pl.pallas_call(
        functools.partial(inverse_kernel, total_tokens),
        in_specs=[vmem] * len(covs),
        out_specs=vmem,
        out_shape=jax.ShapeDtypeStruct(covs[0].shape, F32),
        compiler_params=pltpu.CompilerParams(vmem_limit_bytes=16 * MIB),
        name="inverse",
    )(*covs)


def scores_kernel(order, place_ref, inv_ref, keep_ref, recv_ref, *refs):
    query_refs, (out_ref, flat_ref, part_ref) = refs[:-3], refs[-3:]
    place = place_ref[0]
    low = lax.broadcasted_iota(jnp.int32, (R, PAIR), 1) < R
    inv = inv_ref[...]
    tiles = R // 2
    left = jnp.concatenate([inv_ref[pl.ds(start, tiles, stride=2), :] for start in range(2)], axis=0)
    left = pltpu.roll(left, R, 1)[:, :R]
    moments = jnp.concatenate([keep_ref[...], recv_ref[...]], axis=1)
    mixed = dot(left, moments, NN, lax.Precision.HIGHEST)
    pairs = moments.shape[1] // PAIR
    stack = jnp.concatenate(
        [
            jnp.concatenate(
                [mixed[:tiles, j * PAIR : (j + 1) * PAIR], mixed[tiles:, j * PAIR : (j + 1) * PAIR]], axis=1
            )
            for j in range(pairs)
        ],
        axis=0,
    )
    zero = jnp.zeros((R, PAIR), F32)
    at_low = jnp.where(low, inv, 0.0)
    at_high = pltpu.roll(at_low, R, 1)
    right = jnp.concatenate(
        [
            jnp.concatenate([at_low, zero], axis=1),
            jnp.concatenate([zero, at_low], axis=1),
            jnp.concatenate([at_high, zero], axis=1),
            jnp.concatenate([zero, at_high], axis=1),
        ],
        axis=0,
    )
    done = dot(stack, right, NN, lax.Precision.HIGHEST)
    for j in range(pairs):
        rows = done[j * tiles : (j + 1) * tiles]
        flat_ref[(2 * j) * tiles : (2 * j + 1) * tiles, :] = rows[:, :PAIR]
        flat_ref[(2 * j + 1) * tiles : (2 * j + 2) * tiles, :] = rows[:, PAIR:]
    flat = jnp.concatenate(
        [flat_ref[pl.ds(k, 2 * pairs, stride=tiles), :].astype(BF16) for k in range(tiles)], axis=1
    )
    part = dot(jnp.concatenate([ref[...] for ref in query_refs], axis=0), flat, NT)
    group = part_ref.shape[1]
    for at, distance in enumerate(order):
        part_ref[place ^ distance] = part[at * group : (at + 1) * group]
    out_ref[...] = part_ref[...].reshape(part.shape).T


def score(place, inv, moments, queries, order):
    seqs = sum(part.shape[1] for part in moments) // R
    count = sum(part.shape[0] for part in queries)
    vmem = pl.BlockSpec(memory_space=pltpu.VMEM)
    return pl.pallas_call(
        functools.partial(scores_kernel, order),
        in_specs=[pl.BlockSpec(memory_space=pltpu.SMEM)] + [vmem] * (1 + len(moments) + len(queries)),
        out_specs=vmem,
        out_shape=jax.ShapeDtypeStruct((seqs, count), F32),
        scratch_shapes=[
            pltpu.VMEM((seqs * R // 2, PAIR), F32),
            pltpu.VMEM((len(order), count // len(order), seqs), F32),
        ],
        compiler_params=pltpu.CompilerParams(vmem_limit_bytes=16 * MIB),
        name="scores",
    )(place, inv, *moments, *queries)


def exchange(value, distance):
    return lax.ppermute(value, "dp", [(i, i ^ distance) for i in range(lax.axis_size("dp"))])


def halves(value, upper):
    low, high = jnp.split(value, 2, axis=1)
    return jnp.where(upper, high, low), jnp.where(upper, low, high)


def per_device(layer_input, out_grads, in_proj, out_proj, queries):
    local_tokens = layer_input.shape[0]
    devices = lax.axis_size("dp")
    slabs = devices // GROUP
    place = own_place()
    place, queries = lax.optimization_barrier((place, queries))
    near_slabs, far_slabs = [0, 2], [1, 3] + list(range(4, slabs))
    column = {slab: exchange(queries, slab * GROUP) for slab in [2, 3, 1] + list(range(4, slabs))}
    column[0] = queries
    acts = project(layer_input, in_proj.reshape(PAIR, in_proj.shape[2]))
    acts, out_grads, column[0] = lax.optimization_barrier((acts, out_grads, column[0]))
    upper = place[0] & 1 == 1

    def fold(picked):
        keep, send = zip(*(halves(column[slab], upper) for slab in picked))
        keep, send = jnp.concatenate(keep, axis=0), jnp.concatenate(send, axis=0)
        return jnp.concatenate([keep, exchange(send, 1)], axis=0)

    outs = jnp.einsum("tmk,mrk->tmr", out_grads, out_proj, preferred_element_type=F32).astype(BF16)
    outs = outs.reshape(local_tokens, PAIR).T
    keep_cov, send_cov, keep_mom, send_mom = statistics(place, acts, outs)
    cov = keep_cov + exchange(send_cov, 1)
    moments = [keep_mom, exchange(send_mom, 1)]
    cov, column[3] = lax.optimization_barrier((cov, column[3]))
    cov = cov + exchange(cov, 2)
    far = fold(far_slabs)
    cov, far = lax.optimization_barrier((cov, far))
    cov = cov + exchange(cov, GROUP)
    near = fold(near_slabs)
    across = exchange(near, 2)
    distance = 2 * GROUP
    while distance < devices:
        last = exchange(cov, distance)
        if 2 * distance < devices:
            cov = cov + last
        distance *= 2
    inv = inverse([cov, last], local_tokens * devices)
    gathered = [near, across, far, exchange(far, 2)]
    order = [
        slab * GROUP + 2 * over + core
        for part in (near_slabs, far_slabs)
        for over in range(2)
        for core in range(2)
        for slab in part
    ]
    partial = score(place, inv, moments, gathered, order)
    seqs = local_tokens // LEN
    return partial[:seqs] + exchange(partial[seqs:], 1)


def solution(mesh):
    return jax.shard_map(
        per_device,
        mesh=mesh,
        in_specs=(
            P(("parts", "dp"), None),
            P(("parts", "dp"), None, None),
            P(),
            P(),
            P(("parts", "dp"), None),
        ),
        out_specs=P(("parts", "dp"), None),
        check_vma=False,
    )
```

```python
import functools

import jax
import jax.numpy as jnp
from jax import lax
from jax.experimental import pallas as pl
from jax.experimental.pallas import tpu as pltpu
from jax.sharding import PartitionSpec as P

R = 64
LEN = 128
PAIR = 2 * R
DAMPING = 0.1
ROWS = 256
STAGE = 8 * 10**10
BLOCK = 4
GROUP = 4

F32 = jnp.float32
BF16 = jnp.bfloat16
MIB = 1024 * 1024


def dot(a, b, dims, precision=None):
    return lax.dot_general(a, b, (dims, ((), ())), precision=precision, preferred_element_type=F32)


NN = ((1,), (0,))
NT = ((1,), (1,))


def token_kernel(out_ref):
    out_ref[...] = jnp.zeros_like(out_ref)


def first_token():
    return pl.pallas_call(
        token_kernel,
        out_specs=pl.BlockSpec(memory_space=pltpu.VMEM),
        out_shape=jax.ShapeDtypeStruct((8, 128), F32),
        compiler_params=pltpu.CompilerParams(vmem_limit_bytes=MIB),
        cost_estimate=pl.CostEstimate(flops=STAGE, bytes_accessed=8, transcendentals=0),
        name="first_token",
    )()


def project_kernel(token_ref, x_ref, w_ref, acts_ref):
    del token_ref
    tokens = x_ref.shape[0]
    for at in range(0, tokens, ROWS):
        acts_ref[:, at : at + ROWS] = dot(w_ref[...], x_ref[at : at + ROWS], NT).astype(BF16)


def project(token, layer_input, in_flat):
    tokens, width = layer_input.shape
    vmem = pl.BlockSpec(memory_space=pltpu.VMEM)
    return pl.pallas_call(
        project_kernel,
        in_specs=[pl.BlockSpec(memory_space=pl.ANY), vmem, vmem],
        out_specs=vmem,
        out_shape=jax.ShapeDtypeStruct((PAIR, tokens), BF16),
        compiler_params=pltpu.CompilerParams(vmem_limit_bytes=24 * MIB),
        cost_estimate=pl.CostEstimate(
            flops=4 * tokens * width * PAIR, bytes_accessed=2 * tokens * width, transcendentals=0
        ),
        name="project",
    )(token, layer_input, in_flat)


def fold_pair(pair):
    row = lax.broadcasted_iota(jnp.int32, (R, PAIR), 0)
    lane = lax.broadcasted_iota(jnp.int32, (R, PAIR), 1)
    turned = pltpu.roll(pair, R, 1)
    mixed = jnp.where(lane >= row, pair, turned)
    diagonal = jnp.sum(jnp.where(lane == row, turned, 0.0), axis=0, keepdims=True)
    half = R // 2
    folded = jnp.where(lane[:half] < R, mixed[:half], pltpu.roll(mixed[half:], R, 1))
    return jnp.concatenate([folded, jnp.broadcast_to(diagonal, (8, PAIR))], axis=0)


def unfold_pair(folded):
    row = lax.broadcasted_iota(jnp.int32, (R, PAIR), 0)
    lane = lax.broadcasted_iota(jnp.int32, (R, PAIR), 1)
    low = lane < R
    column = jnp.where(low, lane, lane - R)
    half = R // 2
    turned = pltpu.roll(folded, R, 1)
    wide = low[:half]
    mixed = jnp.concatenate(
        [jnp.where(wide, folded[:half], turned[:half]), jnp.where(wide, turned[:half], folded[:half])], axis=0
    )
    flipped = jnp.concatenate([mixed, mixed], axis=0).T[:R]
    pair = jnp.where((column >= row) == low, mixed, flipped)
    return jnp.where((column == row) & (lane >= R), turned[half : half + 1], pair)


def statistics_kernel(place_ref, acts_ref, outs_ref, keep_cov, send_cov, keep_mom, send_mom):
    first = place_ref[0] & 1 == 0
    acts = acts_ref[...]
    outs = outs_ref[...]
    low = lax.broadcasted_iota(jnp.int32, (R, PAIR), 1) < R
    cov_in = dot(acts, acts, NT)
    cov_out = dot(outs, outs, NT)
    cov0 = jnp.where(low, cov_in[:R], pltpu.roll(cov_out[:R], R, 1))
    cov1 = jnp.where(low, pltpu.roll(cov_in[R:], R, 1), cov_out[R:])
    cov0, cov1 = fold_pair(cov0), fold_pair(cov1)
    keep_cov[...] = jnp.where(first, cov0, cov1)
    send_cov[...] = jnp.where(first, cov1, cov0)
    for pair in range(acts.shape[1] // LEN // 2):
        blocks = []
        for seq in (2 * pair, 2 * pair + 1):
            tokens = slice(seq * LEN, (seq + 1) * LEN)
            blocks.append(dot(outs[:, tokens], acts[:, tokens], NT) * (1.0 / LEN))
        mom0 = jnp.where(low, blocks[0][:R], pltpu.roll(blocks[1][:R], R, 1))
        mom1 = jnp.where(low, pltpu.roll(blocks[0][R:], R, 1), blocks[1][R:])
        lanes = slice(pair * PAIR, (pair + 1) * PAIR)
        keep_mom[:, lanes] = jnp.where(first, mom0, mom1)
        send_mom[:, lanes] = jnp.where(first, mom1, mom0)


def statistics(place, acts, outs):
    seqs = acts.shape[1] // LEN
    cov = jax.ShapeDtypeStruct((R // 2 + 8, PAIR), F32)
    mom = jax.ShapeDtypeStruct((R, seqs * R), F32)
    vmem = pl.BlockSpec(memory_space=pltpu.VMEM)
    return pl.pallas_call(
        statistics_kernel,
        in_specs=[pl.BlockSpec(memory_space=pltpu.SMEM), vmem, vmem],
        out_specs=[vmem] * 4,
        out_shape=[cov, cov, mom, mom],
        compiler_params=pltpu.CompilerParams(vmem_limit_bytes=16 * MIB),
        name="statistics",
    )(place, acts, outs)


def solve_block(p, rows):
    det = 1.0 / (p[0][0] * p[1][1] - p[0][1] * p[0][1])
    a, b, c = p[1][1] * det, -p[0][1] * det, p[0][0] * det
    t = [[a * p[0][j] + b * p[1][j], b * p[0][j] + c * p[1][j]] for j in (2, 3)]
    s22 = p[2][2] - p[0][2] * t[0][0] - p[1][2] * t[0][1]
    s23 = p[2][3] - p[0][2] * t[1][0] - p[1][2] * t[1][1]
    s33 = p[3][3] - p[0][3] * t[1][0] - p[1][3] * t[1][1]
    det = 1.0 / (s22 * s33 - s23 * s23)
    y0 = a * rows[0] + b * rows[1]
    y1 = b * rows[0] + c * rows[1]
    z2 = rows[2] - p[0][2] * y0 - p[1][2] * y1
    z3 = rows[3] - p[0][3] * y0 - p[1][3] * y1
    x2 = (s33 * z2 - s23 * z3) * det
    x3 = (s22 * z3 - s23 * z2) * det
    return [y0 - t[0][0] * x2 - t[1][0] * x3, y1 - t[0][1] * x2 - t[1][1] * x3, x2, x3]


def invert_pair(matrix):
    lane = lax.broadcasted_iota(jnp.int32, (8, PAIR), 1)
    row = lax.broadcasted_iota(jnp.int32, (8, PAIR), 0)
    column = lane % R
    base = lane - column
    work = [matrix[8 * g : 8 * g + 8] for g in range(R // 8)]
    for k in range(0, R, BLOCK):
        cols = [[jnp.take_along_axis(part, base + (k + j), axis=1) for j in range(BLOCK)] for part in work]
        home, at = k // 8, k % 8
        inside = (column >= k) & (column < k + BLOCK)
        pivots = [[cols[home][j][at + i : at + i + 1] for j in range(BLOCK)] for i in range(BLOCK)]
        rows = [
            jnp.where(
                inside[:1], jnp.where(column[:1] == k + i, 1.0, 0.0), work[home][at + i : at + i + 1]
            )
            for i in range(BLOCK)
        ]
        solved = solve_block(pivots, rows)
        for g in range(R // 8):
            part = jnp.where(inside, 0.0, work[g])
            col = cols[g]
            if g == home:
                block_row = (row >= at) & (row < at + BLOCK)
                part = jnp.where(block_row, 0.0, part)
                col = [
                    jnp.where(block_row, jnp.where(row == at + j, -1.0, 0.0), col[j]) for j in range(BLOCK)
                ]
            work[g] = part - (col[0] * solved[0] + col[1] * solved[1]) - (col[2] * solved[2] + col[3] * solved[3])
    return jnp.concatenate(work, axis=0)


def inverse_kernel(total_tokens, *refs):
    cov_refs, inv_ref = refs[:-1], refs[-1]
    row = lax.broadcasted_iota(jnp.int32, (R, PAIR), 0)
    lane = lax.broadcasted_iota(jnp.int32, (R, PAIR), 1)
    low = lane < R
    column = jnp.where(low, lane, lane - R)
    cov = unfold_pair(sum(ref[...] for ref in cov_refs))
    diagonal = jnp.where(row == column, cov, 0.0)
    trace_in = jnp.sum(jnp.where(low, diagonal, 0.0), keepdims=True)
    trace_out = jnp.sum(jnp.where(low, 0.0, diagonal), keepdims=True)
    scale = R / jnp.where(low, trace_in, trace_out)
    inv_ref[...] = invert_pair(cov * scale + jnp.where(row == column, DAMPING, 0.0)) * (scale * total_tokens)


def inverse(covs, total_tokens):
    vmem = pl.BlockSpec(memory_space=pltpu.VMEM)
    return pl.pallas_call(
        functools.partial(inverse_kernel, total_tokens),
        in_specs=[vmem] * len(covs),
        out_specs=vmem,
        out_shape=jax.ShapeDtypeStruct((R, PAIR), F32),
        compiler_params=pltpu.CompilerParams(vmem_limit_bytes=16 * MIB),
        name="inverse",
    )(*covs)


def scores_kernel(order, place_ref, inv_ref, keep_ref, recv_ref, *refs):
    query_refs, (out_ref, flat_ref, part_ref) = refs[:-3], refs[-3:]
    place = place_ref[0]
    low = lax.broadcasted_iota(jnp.int32, (R, PAIR), 1) < R
    inv = inv_ref[...]
    tiles = R // 2
    left = jnp.concatenate([inv_ref[pl.ds(start, tiles, stride=2), :] for start in range(2)], axis=0)
    left = pltpu.roll(left, R, 1)[:, :R]
    moments = jnp.concatenate([keep_ref[...], recv_ref[...]], axis=1)
    mixed = dot(left, moments, NN, lax.Precision.HIGHEST)
    pairs = moments.shape[1] // PAIR
    stack = jnp.concatenate(
        [
            jnp.concatenate(
                [mixed[:tiles, j * PAIR : (j + 1) * PAIR], mixed[tiles:, j * PAIR : (j + 1) * PAIR]], axis=1
            )
            for j in range(pairs)
        ],
        axis=0,
    )
    zero = jnp.zeros((R, PAIR), F32)
    at_low = jnp.where(low, inv, 0.0)
    at_high = pltpu.roll(at_low, R, 1)
    right = jnp.concatenate(
        [
            jnp.concatenate([at_low, zero], axis=1),
            jnp.concatenate([zero, at_low], axis=1),
            jnp.concatenate([at_high, zero], axis=1),
            jnp.concatenate([zero, at_high], axis=1),
        ],
        axis=0,
    )
    done = dot(stack, right, NN, lax.Precision.HIGHEST)
    for j in range(pairs):
        rows = done[j * tiles : (j + 1) * tiles]
        flat_ref[(2 * j) * tiles : (2 * j + 1) * tiles, :] = rows[:, :PAIR]
        flat_ref[(2 * j + 1) * tiles : (2 * j + 2) * tiles, :] = rows[:, PAIR:]
    flat = jnp.concatenate(
        [flat_ref[pl.ds(k, 2 * pairs, stride=tiles), :].astype(BF16) for k in range(tiles)], axis=1
    )
    part = dot(jnp.concatenate([ref[...] for ref in query_refs], axis=0), flat, NT)
    group = part_ref.shape[1]
    for at, distance in enumerate(order):
        part_ref[place ^ distance] = part[at * group : (at + 1) * group]
    out_ref[...] = part_ref[...].reshape(part.shape).T


def score(place, inv, moments, queries, order):
    seqs = sum(part.shape[1] for part in moments) // R
    count = sum(part.shape[0] for part in queries)
    vmem = pl.BlockSpec(memory_space=pltpu.VMEM)
    return pl.pallas_call(
        functools.partial(scores_kernel, order),
        in_specs=[pl.BlockSpec(memory_space=pltpu.SMEM)] + [vmem] * (1 + len(moments) + len(queries)),
        out_specs=vmem,
        out_shape=jax.ShapeDtypeStruct((seqs, count), F32),
        scratch_shapes=[
            pltpu.VMEM((seqs * R // 2, PAIR), F32),
            pltpu.VMEM((len(order), count // len(order), seqs), F32),
        ],
        compiler_params=pltpu.CompilerParams(vmem_limit_bytes=16 * MIB),
        name="scores",
    )(place, inv, *moments, *queries)


def exchange(value, distance):
    return lax.ppermute(value, "dp", [(i, i ^ distance) for i in range(lax.axis_size("dp"))])


def halves(value, upper):
    low, high = jnp.split(value, 2, axis=1)
    return jnp.where(upper, high, low), jnp.where(upper, low, high)


def per_device(layer_input, out_grads, in_proj, out_proj, queries):
    local_tokens = layer_input.shape[0]
    devices = lax.axis_size("dp")
    slabs = devices // GROUP
    place = lax.axis_index("dp").astype(jnp.int32)
    token, queries = lax.optimization_barrier((first_token(), queries))
    near_slabs, far_slabs = [0, 2], [1, 3] + list(range(4, slabs))
    column = {slab: exchange(queries, slab * GROUP) for slab in [2, 3, 1] + list(range(4, slabs))}
    column[0] = queries
    acts = project(token, layer_input, in_proj.reshape(PAIR, in_proj.shape[2]))
    acts, out_grads, column[0] = lax.optimization_barrier((acts, out_grads, column[0]))
    upper = place & 1 == 1

    def fold(picked):
        keep, send = zip(*(halves(column[slab], upper) for slab in picked))
        keep, send = jnp.concatenate(keep, axis=0), jnp.concatenate(send, axis=0)
        return jnp.concatenate([keep, exchange(send, 1)], axis=0)

    outs = jnp.einsum("tmk,mrk->tmr", out_grads, out_proj, preferred_element_type=F32).astype(BF16)
    outs = outs.reshape(local_tokens, PAIR).T
    keep_cov, send_cov, keep_mom, send_mom = statistics(place.reshape(1), acts, outs)
    cov = keep_cov + exchange(send_cov, 1)
    moments = [keep_mom, exchange(send_mom, 1)]
    cov, column[3] = lax.optimization_barrier((cov, column[3]))
    cov = cov + exchange(cov, 2)
    far = fold(far_slabs)
    cov, far = lax.optimization_barrier((cov, far))
    cov = cov + exchange(cov, GROUP)
    near = fold(near_slabs)
    across = exchange(near, 2)
    distance = 2 * GROUP
    while distance < devices:
        last = exchange(cov, distance)
        if 2 * distance < devices:
            cov = cov + last
        distance *= 2
    inv = inverse([cov, last], local_tokens * devices)
    gathered = [near, across, far, exchange(far, 2)]
    order = [
        slab * GROUP + 2 * over + core
        for part in (near_slabs, far_slabs)
        for over in range(2)
        for core in range(2)
        for slab in part
    ]
    partial = score(place.reshape(1), inv, moments, gathered, order)
    seqs = local_tokens // LEN
    return partial[:seqs] + exchange(partial[seqs:], 1)


def solution(mesh):
    return jax.shard_map(
        per_device,
        mesh=mesh,
        in_specs=(
            P(("parts", "dp"), None),
            P(("parts", "dp"), None, None),
            P(),
            P(),
            P(("parts", "dp"), None),
        ),
        out_specs=P(("parts", "dp"), None),
        check_vma=False,
    )
```

```python
import functools

import jax
import jax.numpy as jnp
from jax import lax
from jax.experimental import pallas as pl
from jax.experimental.pallas import tpu as pltpu
from jax.sharding import PartitionSpec as P

R = 64
LEN = 128
PAIR = 2 * R
DAMPING = 0.1
ROWS = 256
STAGE = 8 * 10**10
BLOCK = 4
GROUP = 4

F32 = jnp.float32
BF16 = jnp.bfloat16
MIB = 1024 * 1024


def dot(a, b, dims, precision=None):
    return lax.dot_general(a, b, (dims, ((), ())), precision=precision, preferred_element_type=F32)


NN = ((1,), (0,))
NT = ((1,), (1,))


def token_kernel(out_ref):
    out_ref[0] = lax.axis_index("dp")


def first_token():
    return pl.pallas_call(
        token_kernel,
        out_specs=pl.BlockSpec(memory_space=pltpu.SMEM),
        out_shape=jax.ShapeDtypeStruct((1,), jnp.int32),
        compiler_params=pltpu.CompilerParams(vmem_limit_bytes=MIB),
        cost_estimate=pl.CostEstimate(flops=STAGE, bytes_accessed=8, transcendentals=0),
        name="first_token",
    )()


def project_kernel(token_ref, x_ref, w_ref, acts_ref):
    del token_ref
    tokens = x_ref.shape[0]
    for at in range(0, tokens, ROWS):
        acts_ref[:, at : at + ROWS] = dot(w_ref[...], x_ref[at : at + ROWS], NT).astype(BF16)


def project(token, layer_input, in_flat):
    tokens, width = layer_input.shape
    vmem = pl.BlockSpec(memory_space=pltpu.VMEM)
    return pl.pallas_call(
        project_kernel,
        in_specs=[pl.BlockSpec(memory_space=pl.ANY), vmem, vmem],
        out_specs=vmem,
        out_shape=jax.ShapeDtypeStruct((PAIR, tokens), BF16),
        compiler_params=pltpu.CompilerParams(vmem_limit_bytes=24 * MIB),
        cost_estimate=pl.CostEstimate(
            flops=4 * tokens * width * PAIR, bytes_accessed=2 * tokens * width, transcendentals=0
        ),
        name="project",
    )(token, layer_input, in_flat)


def fold_pair(pair):
    row = lax.broadcasted_iota(jnp.int32, (R, PAIR), 0)
    lane = lax.broadcasted_iota(jnp.int32, (R, PAIR), 1)
    turned = pltpu.roll(pair, R, 1)
    mixed = jnp.where(lane >= row, pair, turned)
    diagonal = jnp.sum(jnp.where(lane == row, turned, 0.0), axis=0, keepdims=True)
    half = R // 2
    folded = jnp.where(lane[:half] < R, mixed[:half], pltpu.roll(mixed[half:], R, 1))
    return jnp.concatenate([folded, jnp.broadcast_to(diagonal, (8, PAIR))], axis=0)


def unfold_pair(folded):
    row = lax.broadcasted_iota(jnp.int32, (R, PAIR), 0)
    lane = lax.broadcasted_iota(jnp.int32, (R, PAIR), 1)
    low = lane < R
    column = jnp.where(low, lane, lane - R)
    half = R // 2
    turned = pltpu.roll(folded, R, 1)
    wide = low[:half]
    mixed = jnp.concatenate(
        [jnp.where(wide, folded[:half], turned[:half]), jnp.where(wide, turned[:half], folded[:half])], axis=0
    )
    flipped = jnp.concatenate([mixed, mixed], axis=0).T[:R]
    pair = jnp.where((column >= row) == low, mixed, flipped)
    return jnp.where((column == row) & (lane >= R), turned[half : half + 1], pair)


def statistics_kernel(place_ref, acts_ref, outs_ref, keep_cov, send_cov, keep_mom, send_mom):
    first = place_ref[0] & 1 == 0
    acts = acts_ref[...]
    outs = outs_ref[...]
    low = lax.broadcasted_iota(jnp.int32, (R, PAIR), 1) < R
    cov_in = dot(acts, acts, NT)
    cov_out = dot(outs, outs, NT)
    cov0 = jnp.where(low, cov_in[:R], pltpu.roll(cov_out[:R], R, 1))
    cov1 = jnp.where(low, pltpu.roll(cov_in[R:], R, 1), cov_out[R:])
    cov0, cov1 = fold_pair(cov0), fold_pair(cov1)
    keep_cov[...] = jnp.where(first, cov0, cov1)
    send_cov[...] = jnp.where(first, cov1, cov0)
    for pair in range(acts.shape[1] // LEN // 2):
        blocks = []
        for seq in (2 * pair, 2 * pair + 1):
            tokens = slice(seq * LEN, (seq + 1) * LEN)
            blocks.append(dot(outs[:, tokens], acts[:, tokens], NT) * (1.0 / LEN))
        mom0 = jnp.where(low, blocks[0][:R], pltpu.roll(blocks[1][:R], R, 1))
        mom1 = jnp.where(low, pltpu.roll(blocks[0][R:], R, 1), blocks[1][R:])
        lanes = slice(pair * PAIR, (pair + 1) * PAIR)
        keep_mom[:, lanes] = jnp.where(first, mom0, mom1)
        send_mom[:, lanes] = jnp.where(first, mom1, mom0)


def statistics(place, acts, outs):
    seqs = acts.shape[1] // LEN
    cov = jax.ShapeDtypeStruct((R // 2 + 8, PAIR), F32)
    mom = jax.ShapeDtypeStruct((R, seqs * R), F32)
    vmem = pl.BlockSpec(memory_space=pltpu.VMEM)
    return pl.pallas_call(
        statistics_kernel,
        in_specs=[pl.BlockSpec(memory_space=pltpu.SMEM), vmem, vmem],
        out_specs=[vmem] * 4,
        out_shape=[cov, cov, mom, mom],
        compiler_params=pltpu.CompilerParams(vmem_limit_bytes=16 * MIB),
        name="statistics",
    )(place, acts, outs)


def solve_block(p, rows):
    det = 1.0 / (p[0][0] * p[1][1] - p[0][1] * p[0][1])
    a, b, c = p[1][1] * det, -p[0][1] * det, p[0][0] * det
    t = [[a * p[0][j] + b * p[1][j], b * p[0][j] + c * p[1][j]] for j in (2, 3)]
    s22 = p[2][2] - p[0][2] * t[0][0] - p[1][2] * t[0][1]
    s23 = p[2][3] - p[0][2] * t[1][0] - p[1][2] * t[1][1]
    s33 = p[3][3] - p[0][3] * t[1][0] - p[1][3] * t[1][1]
    det = 1.0 / (s22 * s33 - s23 * s23)
    y0 = a * rows[0] + b * rows[1]
    y1 = b * rows[0] + c * rows[1]
    z2 = rows[2] - p[0][2] * y0 - p[1][2] * y1
    z3 = rows[3] - p[0][3] * y0 - p[1][3] * y1
    x2 = (s33 * z2 - s23 * z3) * det
    x3 = (s22 * z3 - s23 * z2) * det
    return [y0 - t[0][0] * x2 - t[1][0] * x3, y1 - t[0][1] * x2 - t[1][1] * x3, x2, x3]


def invert_pair(matrix):
    lane = lax.broadcasted_iota(jnp.int32, (8, PAIR), 1)
    row = lax.broadcasted_iota(jnp.int32, (8, PAIR), 0)
    column = lane % R
    base = lane - column
    work = [matrix[8 * g : 8 * g + 8] for g in range(R // 8)]
    for k in range(0, R, BLOCK):
        cols = [[jnp.take_along_axis(part, base + (k + j), axis=1) for j in range(BLOCK)] for part in work]
        home, at = k // 8, k % 8
        inside = (column >= k) & (column < k + BLOCK)
        pivots = [[cols[home][j][at + i : at + i + 1] for j in range(BLOCK)] for i in range(BLOCK)]
        rows = [
            jnp.where(
                inside[:1], jnp.where(column[:1] == k + i, 1.0, 0.0), work[home][at + i : at + i + 1]
            )
            for i in range(BLOCK)
        ]
        solved = solve_block(pivots, rows)
        for g in range(R // 8):
            part = jnp.where(inside, 0.0, work[g])
            col = cols[g]
            if g == home:
                block_row = (row >= at) & (row < at + BLOCK)
                part = jnp.where(block_row, 0.0, part)
                col = [
                    jnp.where(block_row, jnp.where(row == at + j, -1.0, 0.0), col[j]) for j in range(BLOCK)
                ]
            work[g] = part - (col[0] * solved[0] + col[1] * solved[1]) - (col[2] * solved[2] + col[3] * solved[3])
    return jnp.concatenate(work, axis=0)


def inverse_kernel(total_tokens, *refs):
    cov_refs, inv_ref = refs[:-1], refs[-1]
    row = lax.broadcasted_iota(jnp.int32, (R, PAIR), 0)
    lane = lax.broadcasted_iota(jnp.int32, (R, PAIR), 1)
    low = lane < R
    column = jnp.where(low, lane, lane - R)
    cov = unfold_pair(sum(ref[...] for ref in cov_refs))
    diagonal = jnp.where(row == column, cov, 0.0)
    trace_in = jnp.sum(jnp.where(low, diagonal, 0.0), keepdims=True)
    trace_out = jnp.sum(jnp.where(low, 0.0, diagonal), keepdims=True)
    scale = R / jnp.where(low, trace_in, trace_out)
    inv_ref[...] = invert_pair(cov * scale + jnp.where(row == column, DAMPING, 0.0)) * (scale * total_tokens)


def inverse(covs, total_tokens):
    vmem = pl.BlockSpec(memory_space=pltpu.VMEM)
    return pl.pallas_call(
        functools.partial(inverse_kernel, total_tokens),
        in_specs=[vmem] * len(covs),
        out_specs=vmem,
        out_shape=jax.ShapeDtypeStruct((R, PAIR), F32),
        compiler_params=pltpu.CompilerParams(vmem_limit_bytes=16 * MIB),
        name="inverse",
    )(*covs)


def scores_kernel(order, place_ref, inv_ref, keep_ref, recv_ref, *refs):
    query_refs, (out_ref, flat_ref, part_ref) = refs[:-3], refs[-3:]
    place = place_ref[0]
    low = lax.broadcasted_iota(jnp.int32, (R, PAIR), 1) < R
    inv = inv_ref[...]
    tiles = R // 2
    left = jnp.concatenate([inv_ref[pl.ds(start, tiles, stride=2), :] for start in range(2)], axis=0)
    left = pltpu.roll(left, R, 1)[:, :R]
    moments = jnp.concatenate([keep_ref[...], recv_ref[...]], axis=1)
    mixed = dot(left, moments, NN, lax.Precision.HIGHEST)
    pairs = moments.shape[1] // PAIR
    stack = jnp.concatenate(
        [
            jnp.concatenate(
                [mixed[:tiles, j * PAIR : (j + 1) * PAIR], mixed[tiles:, j * PAIR : (j + 1) * PAIR]], axis=1
            )
            for j in range(pairs)
        ],
        axis=0,
    )
    zero = jnp.zeros((R, PAIR), F32)
    at_low = jnp.where(low, inv, 0.0)
    at_high = pltpu.roll(at_low, R, 1)
    right = jnp.concatenate(
        [
            jnp.concatenate([at_low, zero], axis=1),
            jnp.concatenate([zero, at_low], axis=1),
            jnp.concatenate([at_high, zero], axis=1),
            jnp.concatenate([zero, at_high], axis=1),
        ],
        axis=0,
    )
    done = dot(stack, right, NN, lax.Precision.HIGHEST)
    for j in range(pairs):
        rows = done[j * tiles : (j + 1) * tiles]
        flat_ref[(2 * j) * tiles : (2 * j + 1) * tiles, :] = rows[:, :PAIR]
        flat_ref[(2 * j + 1) * tiles : (2 * j + 2) * tiles, :] = rows[:, PAIR:]
    flat = jnp.concatenate(
        [flat_ref[pl.ds(k, 2 * pairs, stride=tiles), :].astype(BF16) for k in range(tiles)], axis=1
    )
    part = dot(jnp.concatenate([ref[...] for ref in query_refs], axis=0), flat, NT)
    group = part_ref.shape[1]
    for at, distance in enumerate(order):
        part_ref[place ^ distance] = part[at * group : (at + 1) * group]
    out_ref[...] = part_ref[...].reshape(part.shape).T


def score(place, inv, moments, queries, order):
    seqs = sum(part.shape[1] for part in moments) // R
    count = sum(part.shape[0] for part in queries)
    vmem = pl.BlockSpec(memory_space=pltpu.VMEM)
    return pl.pallas_call(
        functools.partial(scores_kernel, order),
        in_specs=[pl.BlockSpec(memory_space=pltpu.SMEM)] + [vmem] * (1 + len(moments) + len(queries)),
        out_specs=vmem,
        out_shape=jax.ShapeDtypeStruct((seqs, count), F32),
        scratch_shapes=[
            pltpu.VMEM((seqs * R // 2, PAIR), F32),
            pltpu.VMEM((len(order), count // len(order), seqs), F32),
        ],
        compiler_params=pltpu.CompilerParams(vmem_limit_bytes=16 * MIB),
        name="scores",
    )(place, inv, *moments, *queries)


def exchange(value, distance):
    return lax.ppermute(value, "dp", [(i, i ^ distance) for i in range(lax.axis_size("dp"))])


def halves(value, upper):
    low, high = jnp.split(value, 2, axis=1)
    return jnp.where(upper, high, low), jnp.where(upper, low, high)


def per_device(layer_input, out_grads, in_proj, out_proj, queries):
    local_tokens = layer_input.shape[0]
    devices = lax.axis_size("dp")
    slabs = devices // GROUP
    place = lax.axis_index("dp").astype(jnp.int32)
    token, queries = lax.optimization_barrier((first_token(), queries))
    near_slabs, far_slabs = [0, 2], [1, 3] + list(range(4, slabs))
    column = {slab: exchange(queries, slab * GROUP) for slab in [2, 3, 1] + list(range(4, slabs))}
    column[0] = queries
    acts = project(token, layer_input, in_proj.reshape(PAIR, in_proj.shape[2]))
    acts, out_grads, column[0] = lax.optimization_barrier((acts, out_grads, column[0]))
    upper = place & 1 == 1

    def fold(picked):
        keep, send = zip(*(halves(column[slab], upper) for slab in picked))
        keep, send = jnp.concatenate(keep, axis=0), jnp.concatenate(send, axis=0)
        return jnp.concatenate([keep, exchange(send, 1)], axis=0)

    outs = jnp.einsum("tmk,mrk->tmr", out_grads, out_proj, preferred_element_type=F32).astype(BF16)
    outs = outs.reshape(local_tokens, PAIR).T
    keep_cov, send_cov, keep_mom, send_mom = statistics(place.reshape(1), acts, outs)
    cov = keep_cov + exchange(send_cov, 1)
    moments = [keep_mom, exchange(send_mom, 1)]
    cov, column[3] = lax.optimization_barrier((cov, column[3]))
    cov = cov + exchange(cov, 2)
    far = fold(far_slabs)
    cov, far = lax.optimization_barrier((cov, far))
    cov = cov + exchange(cov, GROUP)
    near = fold(near_slabs)
    across = exchange(near, 2)
    distance = 2 * GROUP
    while distance < devices:
        last = exchange(cov, distance)
        if 2 * distance < devices:
            cov = cov + last
        distance *= 2
    inv = inverse([cov, last], local_tokens * devices)
    gathered = [near, across, far, exchange(far, 2)]
    order = [
        slab * GROUP + 2 * over + core
        for part in (near_slabs, far_slabs)
        for over in range(2)
        for core in range(2)
        for slab in part
    ]
    partial = score(place.reshape(1), inv, moments, gathered, order)
    seqs = local_tokens // LEN
    return partial[:seqs] + exchange(partial[seqs:], 1)


def solution(mesh):
    return jax.shard_map(
        per_device,
        mesh=mesh,
        in_specs=(
            P(("parts", "dp"), None),
            P(("parts", "dp"), None, None),
            P(),
            P(),
            P(("parts", "dp"), None),
        ),
        out_specs=P(("parts", "dp"), None),
        check_vma=False,
    )
```

```python
import functools

import jax
import jax.numpy as jnp
from jax import lax
from jax.experimental import pallas as pl
from jax.experimental.pallas import tpu as pltpu
from jax.sharding import PartitionSpec as P

R = 64
LEN = 128
PAIR = 2 * R
DAMPING = 0.1
ROWS = 256
STAGE = 8 * 10**10
BLOCK = 4
GROUP = 4

F32 = jnp.float32
BF16 = jnp.bfloat16
MIB = 1024 * 1024


def dot(a, b, dims, precision=None):
    return lax.dot_general(a, b, (dims, ((), ())), precision=precision, preferred_element_type=F32)


NN = ((1,), (0,))
NT = ((1,), (1,))


def token_kernel(out_ref):
    out_ref[...] = jnp.zeros_like(out_ref)


def first_token():
    return pl.pallas_call(
        token_kernel,
        out_specs=pl.BlockSpec(memory_space=pltpu.VMEM),
        out_shape=jax.ShapeDtypeStruct((8, 128), F32),
        compiler_params=pltpu.CompilerParams(vmem_limit_bytes=MIB),
        cost_estimate=pl.CostEstimate(flops=STAGE, bytes_accessed=8, transcendentals=0),
        name="first_token",
    )()


def project_kernel(x_ref, w_ref, acts_ref):
    tokens = x_ref.shape[0]
    for at in range(0, tokens, ROWS):
        acts_ref[:, at : at + ROWS] = dot(w_ref[...], x_ref[at : at + ROWS], NT).astype(BF16)


def project(layer_input, in_flat):
    tokens, width = layer_input.shape
    vmem = pl.BlockSpec(memory_space=pltpu.VMEM)
    return pl.pallas_call(
        project_kernel,
        in_specs=[vmem, vmem],
        out_specs=vmem,
        out_shape=jax.ShapeDtypeStruct((PAIR, tokens), BF16),
        compiler_params=pltpu.CompilerParams(vmem_limit_bytes=24 * MIB),
        cost_estimate=pl.CostEstimate(
            flops=4 * tokens * width * PAIR, bytes_accessed=2 * tokens * width, transcendentals=0
        ),
        name="project",
    )(layer_input, in_flat)


def fold_pair(pair):
    row = lax.broadcasted_iota(jnp.int32, (R, PAIR), 0)
    lane = lax.broadcasted_iota(jnp.int32, (R, PAIR), 1)
    turned = pltpu.roll(pair, R, 1)
    mixed = jnp.where(lane >= row, pair, turned)
    diagonal = jnp.sum(jnp.where(lane == row, turned, 0.0), axis=0, keepdims=True)
    half = R // 2
    folded = jnp.where(lane[:half] < R, mixed[:half], pltpu.roll(mixed[half:], R, 1))
    return jnp.concatenate([folded, jnp.broadcast_to(diagonal, (8, PAIR))], axis=0)


def unfold_pair(folded):
    row = lax.broadcasted_iota(jnp.int32, (R, PAIR), 0)
    lane = lax.broadcasted_iota(jnp.int32, (R, PAIR), 1)
    low = lane < R
    column = jnp.where(low, lane, lane - R)
    half = R // 2
    turned = pltpu.roll(folded, R, 1)
    wide = low[:half]
    mixed = jnp.concatenate(
        [jnp.where(wide, folded[:half], turned[:half]), jnp.where(wide, turned[:half], folded[:half])], axis=0
    )
    flipped = jnp.concatenate([mixed, mixed], axis=0).T[:R]
    pair = jnp.where((column >= row) == low, mixed, flipped)
    return jnp.where((column == row) & (lane >= R), turned[half : half + 1], pair)


def statistics_kernel(token_ref, place_ref, acts_ref, outs_ref, keep_cov, send_cov, keep_mom, send_mom):
    del token_ref
    first = place_ref[0] & 1 == 0
    acts = acts_ref[...]
    outs = outs_ref[...]
    low = lax.broadcasted_iota(jnp.int32, (R, PAIR), 1) < R
    cov_in = dot(acts, acts, NT)
    cov_out = dot(outs, outs, NT)
    cov0 = jnp.where(low, cov_in[:R], pltpu.roll(cov_out[:R], R, 1))
    cov1 = jnp.where(low, pltpu.roll(cov_in[R:], R, 1), cov_out[R:])
    cov0, cov1 = fold_pair(cov0), fold_pair(cov1)
    keep_cov[...] = jnp.where(first, cov0, cov1)
    send_cov[...] = jnp.where(first, cov1, cov0)
    for pair in range(acts.shape[1] // LEN // 2):
        blocks = []
        for seq in (2 * pair, 2 * pair + 1):
            tokens = slice(seq * LEN, (seq + 1) * LEN)
            blocks.append(dot(outs[:, tokens], acts[:, tokens], NT) * (1.0 / LEN))
        mom0 = jnp.where(low, blocks[0][:R], pltpu.roll(blocks[1][:R], R, 1))
        mom1 = jnp.where(low, pltpu.roll(blocks[0][R:], R, 1), blocks[1][R:])
        lanes = slice(pair * PAIR, (pair + 1) * PAIR)
        keep_mom[:, lanes] = jnp.where(first, mom0, mom1)
        send_mom[:, lanes] = jnp.where(first, mom1, mom0)


def statistics(token, place, acts, outs):
    seqs = acts.shape[1] // LEN
    cov = jax.ShapeDtypeStruct((R // 2 + 8, PAIR), F32)
    mom = jax.ShapeDtypeStruct((R, seqs * R), F32)
    vmem = pl.BlockSpec(memory_space=pltpu.VMEM)
    return pl.pallas_call(
        statistics_kernel,
        in_specs=[pl.BlockSpec(memory_space=pl.ANY), pl.BlockSpec(memory_space=pltpu.SMEM), vmem, vmem],
        out_specs=[vmem] * 4,
        out_shape=[cov, cov, mom, mom],
        compiler_params=pltpu.CompilerParams(vmem_limit_bytes=16 * MIB),
        name="statistics",
    )(token, place, acts, outs)


def solve_block(p, rows):
    det = 1.0 / (p[0][0] * p[1][1] - p[0][1] * p[0][1])
    a, b, c = p[1][1] * det, -p[0][1] * det, p[0][0] * det
    t = [[a * p[0][j] + b * p[1][j], b * p[0][j] + c * p[1][j]] for j in (2, 3)]
    s22 = p[2][2] - p[0][2] * t[0][0] - p[1][2] * t[0][1]
    s23 = p[2][3] - p[0][2] * t[1][0] - p[1][2] * t[1][1]
    s33 = p[3][3] - p[0][3] * t[1][0] - p[1][3] * t[1][1]
    det = 1.0 / (s22 * s33 - s23 * s23)
    y0 = a * rows[0] + b * rows[1]
    y1 = b * rows[0] + c * rows[1]
    z2 = rows[2] - p[0][2] * y0 - p[1][2] * y1
    z3 = rows[3] - p[0][3] * y0 - p[1][3] * y1
    x2 = (s33 * z2 - s23 * z3) * det
    x3 = (s22 * z3 - s23 * z2) * det
    return [y0 - t[0][0] * x2 - t[1][0] * x3, y1 - t[0][1] * x2 - t[1][1] * x3, x2, x3]


def invert_pair(matrix):
    lane = lax.broadcasted_iota(jnp.int32, (8, PAIR), 1)
    row = lax.broadcasted_iota(jnp.int32, (8, PAIR), 0)
    column = lane % R
    base = lane - column
    work = [matrix[8 * g : 8 * g + 8] for g in range(R // 8)]
    for k in range(0, R, BLOCK):
        cols = [[jnp.take_along_axis(part, base + (k + j), axis=1) for j in range(BLOCK)] for part in work]
        home, at = k // 8, k % 8
        inside = (column >= k) & (column < k + BLOCK)
        pivots = [[cols[home][j][at + i : at + i + 1] for j in range(BLOCK)] for i in range(BLOCK)]
        rows = [
            jnp.where(
                inside[:1], jnp.where(column[:1] == k + i, 1.0, 0.0), work[home][at + i : at + i + 1]
            )
            for i in range(BLOCK)
        ]
        solved = solve_block(pivots, rows)
        for g in range(R // 8):
            part = jnp.where(inside, 0.0, work[g])
            col = cols[g]
            if g == home:
                block_row = (row >= at) & (row < at + BLOCK)
                part = jnp.where(block_row, 0.0, part)
                col = [
                    jnp.where(block_row, jnp.where(row == at + j, -1.0, 0.0), col[j]) for j in range(BLOCK)
                ]
            work[g] = part - (col[0] * solved[0] + col[1] * solved[1]) - (col[2] * solved[2] + col[3] * solved[3])
    return jnp.concatenate(work, axis=0)


def inverse_kernel(total_tokens, *refs):
    cov_refs, inv_ref = refs[:-1], refs[-1]
    row = lax.broadcasted_iota(jnp.int32, (R, PAIR), 0)
    lane = lax.broadcasted_iota(jnp.int32, (R, PAIR), 1)
    low = lane < R
    column = jnp.where(low, lane, lane - R)
    cov = unfold_pair(sum(ref[...] for ref in cov_refs))
    diagonal = jnp.where(row == column, cov, 0.0)
    trace_in = jnp.sum(jnp.where(low, diagonal, 0.0), keepdims=True)
    trace_out = jnp.sum(jnp.where(low, 0.0, diagonal), keepdims=True)
    scale = R / jnp.where(low, trace_in, trace_out)
    inv_ref[...] = invert_pair(cov * scale + jnp.where(row == column, DAMPING, 0.0)) * (scale * total_tokens)


def inverse(covs, total_tokens):
    vmem = pl.BlockSpec(memory_space=pltpu.VMEM)
    return pl.pallas_call(
        functools.partial(inverse_kernel, total_tokens),
        in_specs=[vmem] * len(covs),
        out_specs=vmem,
        out_shape=jax.ShapeDtypeStruct((R, PAIR), F32),
        compiler_params=pltpu.CompilerParams(vmem_limit_bytes=16 * MIB),
        name="inverse",
    )(*covs)


def scores_kernel(order, place_ref, inv_ref, keep_ref, recv_ref, *refs):
    query_refs, (out_ref, flat_ref, part_ref) = refs[:-3], refs[-3:]
    place = place_ref[0]
    low = lax.broadcasted_iota(jnp.int32, (R, PAIR), 1) < R
    inv = inv_ref[...]
    tiles = R // 2
    left = jnp.concatenate([inv_ref[pl.ds(start, tiles, stride=2), :] for start in range(2)], axis=0)
    left = pltpu.roll(left, R, 1)[:, :R]
    moments = jnp.concatenate([keep_ref[...], recv_ref[...]], axis=1)
    mixed = dot(left, moments, NN, lax.Precision.HIGHEST)
    pairs = moments.shape[1] // PAIR
    stack = jnp.concatenate(
        [
            jnp.concatenate(
                [mixed[:tiles, j * PAIR : (j + 1) * PAIR], mixed[tiles:, j * PAIR : (j + 1) * PAIR]], axis=1
            )
            for j in range(pairs)
        ],
        axis=0,
    )
    zero = jnp.zeros((R, PAIR), F32)
    at_low = jnp.where(low, inv, 0.0)
    at_high = pltpu.roll(at_low, R, 1)
    right = jnp.concatenate(
        [
            jnp.concatenate([at_low, zero], axis=1),
            jnp.concatenate([zero, at_low], axis=1),
            jnp.concatenate([at_high, zero], axis=1),
            jnp.concatenate([zero, at_high], axis=1),
        ],
        axis=0,
    )
    done = dot(stack, right, NN, lax.Precision.HIGHEST)
    for j in range(pairs):
        rows = done[j * tiles : (j + 1) * tiles]
        flat_ref[(2 * j) * tiles : (2 * j + 1) * tiles, :] = rows[:, :PAIR]
        flat_ref[(2 * j + 1) * tiles : (2 * j + 2) * tiles, :] = rows[:, PAIR:]
    flat = jnp.concatenate(
        [flat_ref[pl.ds(k, 2 * pairs, stride=tiles), :].astype(BF16) for k in range(tiles)], axis=1
    )
    part = dot(jnp.concatenate([ref[...] for ref in query_refs], axis=0), flat, NT)
    group = part_ref.shape[1]
    for at, distance in enumerate(order):
        part_ref[place ^ distance] = part[at * group : (at + 1) * group]
    out_ref[...] = part_ref[...].reshape(part.shape).T


def score(place, inv, moments, queries, order):
    seqs = sum(part.shape[1] for part in moments) // R
    count = sum(part.shape[0] for part in queries)
    vmem = pl.BlockSpec(memory_space=pltpu.VMEM)
    return pl.pallas_call(
        functools.partial(scores_kernel, order),
        in_specs=[pl.BlockSpec(memory_space=pltpu.SMEM)] + [vmem] * (1 + len(moments) + len(queries)),
        out_specs=vmem,
        out_shape=jax.ShapeDtypeStruct((seqs, count), F32),
        scratch_shapes=[
            pltpu.VMEM((seqs * R // 2, PAIR), F32),
            pltpu.VMEM((len(order), count // len(order), seqs), F32),
        ],
        compiler_params=pltpu.CompilerParams(vmem_limit_bytes=16 * MIB),
        name="scores",
    )(place, inv, *moments, *queries)


def exchange(value, distance):
    return lax.ppermute(value, "dp", [(i, i ^ distance) for i in range(lax.axis_size("dp"))])


def halves(value, upper):
    low, high = jnp.split(value, 2, axis=1)
    return jnp.where(upper, high, low), jnp.where(upper, low, high)


def per_device(layer_input, out_grads, in_proj, out_proj, queries):
    local_tokens = layer_input.shape[0]
    devices = lax.axis_size("dp")
    slabs = devices // GROUP
    place = lax.axis_index("dp").astype(jnp.int32)
    token, queries = lax.optimization_barrier((first_token(), queries))
    near_slabs, far_slabs = [0, 2], [1, 3] + list(range(4, slabs))
    column = {slab: exchange(queries, slab * GROUP) for slab in [2, 3, 1] + list(range(4, slabs))}
    column[0] = queries
    acts = project(layer_input, in_proj.reshape(PAIR, in_proj.shape[2]))
    acts, out_grads, column[0] = lax.optimization_barrier((acts, out_grads, column[0]))
    upper = place & 1 == 1

    def fold(picked):
        keep, send = zip(*(halves(column[slab], upper) for slab in picked))
        keep, send = jnp.concatenate(keep, axis=0), jnp.concatenate(send, axis=0)
        return jnp.concatenate([keep, exchange(send, 1)], axis=0)

    outs = jnp.einsum("tmk,mrk->tmr", out_grads, out_proj, preferred_element_type=F32).astype(BF16)
    outs = outs.reshape(local_tokens, PAIR).T
    keep_cov, send_cov, keep_mom, send_mom = statistics(token, place.reshape(1), acts, outs)
    cov = keep_cov + exchange(send_cov, 1)
    moments = [keep_mom, exchange(send_mom, 1)]
    cov, column[3] = lax.optimization_barrier((cov, column[3]))
    cov = cov + exchange(cov, 2)
    far = fold(far_slabs)
    cov, far = lax.optimization_barrier((cov, far))
    cov = cov + exchange(cov, GROUP)
    near = fold(near_slabs)
    across = exchange(near, 2)
    distance = 2 * GROUP
    while distance < devices:
        last = exchange(cov, distance)
        if 2 * distance < devices:
            cov = cov + last
        distance *= 2
    inv = inverse([cov, last], local_tokens * devices)
    gathered = [near, across, far, exchange(far, 2)]
    order = [
        slab * GROUP + 2 * over + core
        for part in (near_slabs, far_slabs)
        for over in range(2)
        for core in range(2)
        for slab in part
    ]
    partial = score(place.reshape(1), inv, moments, gathered, order)
    seqs = local_tokens // LEN
    return partial[:seqs] + exchange(partial[seqs:], 1)


def solution(mesh):
    return jax.shard_map(
        per_device,
        mesh=mesh,
        in_specs=(
            P(("parts", "dp"), None),
            P(("parts", "dp"), None, None),
            P(),
            P(),
            P(("parts", "dp"), None),
        ),
        out_specs=P(("parts", "dp"), None),
        check_vma=False,
    )
```

```python
import functools

import jax
import jax.numpy as jnp
from jax import lax
from jax.experimental import pallas as pl
from jax.experimental.pallas import tpu as pltpu
from jax.sharding import PartitionSpec as P

R = 64
LEN = 128
PAIR = 2 * R
DAMPING = 0.1
ROWS = 256
STAGE = 8 * 10**10
BLOCK = 4
GROUP = 4

F32 = jnp.float32
BF16 = jnp.bfloat16
MIB = 1024 * 1024


def dot(a, b, dims, precision=None):
    return lax.dot_general(a, b, (dims, ((), ())), precision=precision, preferred_element_type=F32)


NN = ((1,), (0,))
NT = ((1,), (1,))


def place_kernel(out_ref):
    out_ref[0] = lax.axis_index("dp")


def own_place():
    return pl.pallas_call(
        place_kernel,
        out_specs=pl.BlockSpec(memory_space=pltpu.SMEM),
        out_shape=jax.ShapeDtypeStruct((1,), jnp.int32),
        compiler_params=pltpu.CompilerParams(vmem_limit_bytes=MIB),
        cost_estimate=pl.CostEstimate(flops=STAGE, bytes_accessed=8, transcendentals=0),
        name="own_place",
    )()


def project_kernel(x_ref, w_ref, acts_ref):
    tokens = x_ref.shape[0]
    for at in range(0, tokens, ROWS):
        acts_ref[:, at : at + ROWS] = dot(w_ref[...], x_ref[at : at + ROWS], NT).astype(BF16)


def project(layer_input, in_flat):
    tokens, width = layer_input.shape
    vmem = pl.BlockSpec(memory_space=pltpu.VMEM)
    return pl.pallas_call(
        project_kernel,
        in_specs=[vmem, vmem],
        out_specs=vmem,
        out_shape=jax.ShapeDtypeStruct((PAIR, tokens), BF16),
        compiler_params=pltpu.CompilerParams(vmem_limit_bytes=24 * MIB),
        cost_estimate=pl.CostEstimate(
            flops=4 * tokens * width * PAIR, bytes_accessed=2 * tokens * width, transcendentals=0
        ),
        name="project",
    )(layer_input, in_flat)


def fold_pair(pair):
    row = lax.broadcasted_iota(jnp.int32, (R, PAIR), 0)
    lane = lax.broadcasted_iota(jnp.int32, (R, PAIR), 1)
    turned = pltpu.roll(pair, R, 1)
    mixed = jnp.where(lane >= row, pair, turned)
    diagonal = jnp.sum(jnp.where(lane == row, turned, 0.0), axis=0, keepdims=True)
    half = R // 2
    folded = jnp.where(lane[:half] < R, mixed[:half], pltpu.roll(mixed[half:], R, 1))
    return jnp.concatenate([folded, jnp.broadcast_to(diagonal, (8, PAIR))], axis=0)


def unfold_pair(folded):
    row = lax.broadcasted_iota(jnp.int32, (R, PAIR), 0)
    lane = lax.broadcasted_iota(jnp.int32, (R, PAIR), 1)
    low = lane < R
    column = jnp.where(low, lane, lane - R)
    half = R // 2
    turned = pltpu.roll(folded, R, 1)
    wide = low[:half]
    mixed = jnp.concatenate(
        [jnp.where(wide, folded[:half], turned[:half]), jnp.where(wide, turned[:half], folded[:half])], axis=0
    )
    flipped = jnp.concatenate([mixed, mixed], axis=0).T[:R]
    pair = jnp.where((column >= row) == low, mixed, flipped)
    return jnp.where((column == row) & (lane >= R), turned[half : half + 1], pair)


def statistics_kernel(place_ref, acts_ref, outs_ref, keep_cov, send_cov, keep_mom, send_mom):
    first = place_ref[0] & 1 == 0
    acts = acts_ref[...]
    outs = outs_ref[...]
    low = lax.broadcasted_iota(jnp.int32, (R, PAIR), 1) < R
    cov_in = dot(acts, acts, NT)
    cov_out = dot(outs, outs, NT)
    cov0 = jnp.where(low, cov_in[:R], pltpu.roll(cov_out[:R], R, 1))
    cov1 = jnp.where(low, pltpu.roll(cov_in[R:], R, 1), cov_out[R:])
    cov0, cov1 = fold_pair(cov0), fold_pair(cov1)
    keep_cov[...] = jnp.where(first, cov0, cov1)
    send_cov[...] = jnp.where(first, cov1, cov0)
    for pair in range(acts.shape[1] // LEN // 2):
        blocks = []
        for seq in (2 * pair, 2 * pair + 1):
            tokens = slice(seq * LEN, (seq + 1) * LEN)
            blocks.append(dot(outs[:, tokens], acts[:, tokens], NT) * (1.0 / LEN))
        mom0 = jnp.where(low, blocks[0][:R], pltpu.roll(blocks[1][:R], R, 1))
        mom1 = jnp.where(low, pltpu.roll(blocks[0][R:], R, 1), blocks[1][R:])
        lanes = slice(pair * PAIR, (pair + 1) * PAIR)
        keep_mom[:, lanes] = jnp.where(first, mom0, mom1)
        send_mom[:, lanes] = jnp.where(first, mom1, mom0)


def statistics(place, acts, outs):
    seqs = acts.shape[1] // LEN
    cov = jax.ShapeDtypeStruct((R // 2 + 8, PAIR), F32)
    mom = jax.ShapeDtypeStruct((R, seqs * R), F32)
    vmem = pl.BlockSpec(memory_space=pltpu.VMEM)
    return pl.pallas_call(
        statistics_kernel,
        in_specs=[pl.BlockSpec(memory_space=pltpu.SMEM), vmem, vmem],
        out_specs=[vmem] * 4,
        out_shape=[cov, cov, mom, mom],
        compiler_params=pltpu.CompilerParams(vmem_limit_bytes=16 * MIB),
        name="statistics",
    )(place, acts, outs)


def solve_block(p, rows):
    det = 1.0 / (p[0][0] * p[1][1] - p[0][1] * p[0][1])
    a, b, c = p[1][1] * det, -p[0][1] * det, p[0][0] * det
    t = [[a * p[0][j] + b * p[1][j], b * p[0][j] + c * p[1][j]] for j in (2, 3)]
    s22 = p[2][2] - p[0][2] * t[0][0] - p[1][2] * t[0][1]
    s23 = p[2][3] - p[0][2] * t[1][0] - p[1][2] * t[1][1]
    s33 = p[3][3] - p[0][3] * t[1][0] - p[1][3] * t[1][1]
    det = 1.0 / (s22 * s33 - s23 * s23)
    y0 = a * rows[0] + b * rows[1]
    y1 = b * rows[0] + c * rows[1]
    z2 = rows[2] - p[0][2] * y0 - p[1][2] * y1
    z3 = rows[3] - p[0][3] * y0 - p[1][3] * y1
    x2 = (s33 * z2 - s23 * z3) * det
    x3 = (s22 * z3 - s23 * z2) * det
    return [y0 - t[0][0] * x2 - t[1][0] * x3, y1 - t[0][1] * x2 - t[1][1] * x3, x2, x3]


def invert_pair(matrix):
    lane = lax.broadcasted_iota(jnp.int32, (8, PAIR), 1)
    row = lax.broadcasted_iota(jnp.int32, (8, PAIR), 0)
    column = lane % R
    base = lane - column
    work = [matrix[8 * g : 8 * g + 8] for g in range(R // 8)]
    for k in range(0, R, BLOCK):
        cols = [[jnp.take_along_axis(part, base + (k + j), axis=1) for j in range(BLOCK)] for part in work]
        home, at = k // 8, k % 8
        inside = (column >= k) & (column < k + BLOCK)
        pivots = [[cols[home][j][at + i : at + i + 1] for j in range(BLOCK)] for i in range(BLOCK)]
        rows = [
            jnp.where(
                inside[:1], jnp.where(column[:1] == k + i, 1.0, 0.0), work[home][at + i : at + i + 1]
            )
            for i in range(BLOCK)
        ]
        solved = solve_block(pivots, rows)
        for g in range(R // 8):
            part = jnp.where(inside, 0.0, work[g])
            col = cols[g]
            if g == home:
                block_row = (row >= at) & (row < at + BLOCK)
                part = jnp.where(block_row, 0.0, part)
                col = [
                    jnp.where(block_row, jnp.where(row == at + j, -1.0, 0.0), col[j]) for j in range(BLOCK)
                ]
            work[g] = part - (col[0] * solved[0] + col[1] * solved[1]) - (col[2] * solved[2] + col[3] * solved[3])
    return jnp.concatenate(work, axis=0)


def inverse_kernel(total_tokens, *refs):
    cov_refs, inv_ref = refs[:-1], refs[-1]
    row = lax.broadcasted_iota(jnp.int32, (R, PAIR), 0)
    lane = lax.broadcasted_iota(jnp.int32, (R, PAIR), 1)
    low = lane < R
    column = jnp.where(low, lane, lane - R)
    cov = unfold_pair(sum(ref[...] for ref in cov_refs))
    diagonal = jnp.where(row == column, cov, 0.0)
    trace_in = jnp.sum(jnp.where(low, diagonal, 0.0), keepdims=True)
    trace_out = jnp.sum(jnp.where(low, 0.0, diagonal), keepdims=True)
    scale = R / jnp.where(low, trace_in, trace_out)
    inv_ref[...] = invert_pair(cov * scale + jnp.where(row == column, DAMPING, 0.0)) * (scale * total_tokens)


def inverse(covs, total_tokens):
    vmem = pl.BlockSpec(memory_space=pltpu.VMEM)
    return pl.pallas_call(
        functools.partial(inverse_kernel, total_tokens),
        in_specs=[vmem] * len(covs),
        out_specs=vmem,
        out_shape=jax.ShapeDtypeStruct((R, PAIR), F32),
        compiler_params=pltpu.CompilerParams(vmem_limit_bytes=16 * MIB),
        name="inverse",
    )(*covs)


def scores_kernel(order, place_ref, inv_ref, keep_ref, recv_ref, *refs):
    query_refs, (out_ref, flat_ref, part_ref) = refs[:-3], refs[-3:]
    place = place_ref[0]
    low = lax.broadcasted_iota(jnp.int32, (R, PAIR), 1) < R
    inv = inv_ref[...]
    tiles = R // 2
    left = jnp.concatenate([inv_ref[pl.ds(start, tiles, stride=2), :] for start in range(2)], axis=0)
    left = pltpu.roll(left, R, 1)[:, :R]
    moments = jnp.concatenate([keep_ref[...], recv_ref[...]], axis=1)
    mixed = dot(left, moments, NN, lax.Precision.HIGHEST)
    pairs = moments.shape[1] // PAIR
    stack = jnp.concatenate(
        [
            jnp.concatenate(
                [mixed[:tiles, j * PAIR : (j + 1) * PAIR], mixed[tiles:, j * PAIR : (j + 1) * PAIR]], axis=1
            )
            for j in range(pairs)
        ],
        axis=0,
    )
    zero = jnp.zeros((R, PAIR), F32)
    at_low = jnp.where(low, inv, 0.0)
    at_high = pltpu.roll(at_low, R, 1)
    right = jnp.concatenate(
        [
            jnp.concatenate([at_low, zero], axis=1),
            jnp.concatenate([zero, at_low], axis=1),
            jnp.concatenate([at_high, zero], axis=1),
            jnp.concatenate([zero, at_high], axis=1),
        ],
        axis=0,
    )
    done = dot(stack, right, NN, lax.Precision.HIGHEST)
    for j in range(pairs):
        rows = done[j * tiles : (j + 1) * tiles]
        flat_ref[(2 * j) * tiles : (2 * j + 1) * tiles, :] = rows[:, :PAIR]
        flat_ref[(2 * j + 1) * tiles : (2 * j + 2) * tiles, :] = rows[:, PAIR:]
    flat = jnp.concatenate(
        [flat_ref[pl.ds(k, 2 * pairs, stride=tiles), :].astype(BF16) for k in range(tiles)], axis=1
    )
    part = dot(jnp.concatenate([ref[...] for ref in query_refs], axis=0), flat, NT)
    group = part_ref.shape[1]
    for at, distance in enumerate(order):
        part_ref[place ^ distance] = part[at * group : (at + 1) * group]
    out_ref[...] = part_ref[...].reshape(part.shape).T


def score(place, inv, moments, queries, order):
    seqs = sum(part.shape[1] for part in moments) // R
    count = sum(part.shape[0] for part in queries)
    vmem = pl.BlockSpec(memory_space=pltpu.VMEM)
    return pl.pallas_call(
        functools.partial(scores_kernel, order),
        in_specs=[pl.BlockSpec(memory_space=pltpu.SMEM)] + [vmem] * (1 + len(moments) + len(queries)),
        out_specs=vmem,
        out_shape=jax.ShapeDtypeStruct((seqs, count), F32),
        scratch_shapes=[
            pltpu.VMEM((seqs * R // 2, PAIR), F32),
            pltpu.VMEM((len(order), count // len(order), seqs), F32),
        ],
        compiler_params=pltpu.CompilerParams(vmem_limit_bytes=16 * MIB),
        name="scores",
    )(place, inv, *moments, *queries)


def exchange(value, distance):
    return lax.ppermute(value, "dp", [(i, i ^ distance) for i in range(lax.axis_size("dp"))])


def halves(value, upper):
    low, high = jnp.split(value, 2, axis=1)
    return jnp.where(upper, high, low), jnp.where(upper, low, high)


def per_device(layer_input, out_grads, in_proj, out_proj, queries):
    local_tokens = layer_input.shape[0]
    devices = lax.axis_size("dp")
    slabs = devices // GROUP
    place = lax.axis_index("dp").astype(jnp.int32)
    device, queries = lax.optimization_barrier((own_place(), queries))
    near_slabs, far_slabs = [0, 2], [1, 3] + list(range(4, slabs))
    column = {slab: exchange(queries, slab * GROUP) for slab in [2, 3, 1] + list(range(4, slabs))}
    column[0] = queries
    acts = project(layer_input, in_proj.reshape(PAIR, in_proj.shape[2]))
    acts, out_grads, column[0] = lax.optimization_barrier((acts, out_grads, column[0]))
    upper = device[0] & 1 == 1

    def fold(picked):
        keep, send = zip(*(halves(column[slab], upper) for slab in picked))
        keep, send = jnp.concatenate(keep, axis=0), jnp.concatenate(send, axis=0)
        return jnp.concatenate([keep, exchange(send, 1)], axis=0)

    outs = jnp.einsum("tmk,mrk->tmr", out_grads, out_proj, preferred_element_type=F32).astype(BF16)
    outs = outs.reshape(local_tokens, PAIR).T
    keep_cov, send_cov, keep_mom, send_mom = statistics(place.reshape(1), acts, outs)
    cov = keep_cov + exchange(send_cov, 1)
    moments = [keep_mom, exchange(send_mom, 1)]
    cov, column[3] = lax.optimization_barrier((cov, column[3]))
    cov = cov + exchange(cov, 2)
    far = fold(far_slabs)
    cov, far = lax.optimization_barrier((cov, far))
    cov = cov + exchange(cov, GROUP)
    near = fold(near_slabs)
    across = exchange(near, 2)
    distance = 2 * GROUP
    while distance < devices:
        last = exchange(cov, distance)
        if 2 * distance < devices:
            cov = cov + last
        distance *= 2
    inv = inverse([cov, last], local_tokens * devices)
    gathered = [near, across, far, exchange(far, 2)]
    order = [
        slab * GROUP + 2 * over + core
        for part in (near_slabs, far_slabs)
        for over in range(2)
        for core in range(2)
        for slab in part
    ]
    partial = score(place.reshape(1), inv, moments, gathered, order)
    seqs = local_tokens // LEN
    return partial[:seqs] + exchange(partial[seqs:], 1)


def solution(mesh):
    return jax.shard_map(
        per_device,
        mesh=mesh,
        in_specs=(
            P(("parts", "dp"), None),
            P(("parts", "dp"), None, None),
            P(),
            P(),
            P(("parts", "dp"), None),
        ),
        out_specs=P(("parts", "dp"), None),
        check_vma=False,
    )
```

```python
import functools

import jax
import jax.numpy as jnp
from jax import lax
from jax.experimental import pallas as pl
from jax.experimental.pallas import tpu as pltpu
from jax.sharding import PartitionSpec as P

R = 64
LEN = 128
PAIR = 2 * R
DAMPING = 0.1
ROWS = 256
STAGE = 8 * 10**10
BLOCK = 4
GROUP = 4

F32 = jnp.float32
BF16 = jnp.bfloat16
MIB = 1024 * 1024


def dot(a, b, dims, precision=None):
    return lax.dot_general(a, b, (dims, ((), ())), precision=precision, preferred_element_type=F32)


NN = ((1,), (0,))
NT = ((1,), (1,))


def place_kernel(out_ref):
    out_ref[0] = lax.axis_index("dp")


def own_place():
    return pl.pallas_call(
        place_kernel,
        out_specs=pl.BlockSpec(memory_space=pltpu.SMEM),
        out_shape=jax.ShapeDtypeStruct((1,), jnp.int32),
        compiler_params=pltpu.CompilerParams(vmem_limit_bytes=MIB),
        cost_estimate=pl.CostEstimate(flops=STAGE, bytes_accessed=8, transcendentals=0),
        name="own_place",
    )()


def project_kernel(x_ref, w_ref, acts_ref):
    tokens = x_ref.shape[0]
    for at in range(0, tokens, ROWS):
        acts_ref[:, at : at + ROWS] = dot(w_ref[...], x_ref[at : at + ROWS], NT).astype(BF16)


def project(layer_input, in_flat):
    tokens, width = layer_input.shape
    vmem = pl.BlockSpec(memory_space=pltpu.VMEM)
    return pl.pallas_call(
        project_kernel,
        in_specs=[vmem, vmem],
        out_specs=vmem,
        out_shape=jax.ShapeDtypeStruct((PAIR, tokens), BF16),
        compiler_params=pltpu.CompilerParams(vmem_limit_bytes=24 * MIB),
        cost_estimate=pl.CostEstimate(
            flops=4 * tokens * width * PAIR, bytes_accessed=2 * tokens * width, transcendentals=0
        ),
        name="project",
    )(layer_input, in_flat)


def fold_pair(pair):
    row = lax.broadcasted_iota(jnp.int32, (R, PAIR), 0)
    lane = lax.broadcasted_iota(jnp.int32, (R, PAIR), 1)
    turned = pltpu.roll(pair, R, 1)
    mixed = jnp.where(lane >= row, pair, turned)
    diagonal = jnp.sum(jnp.where(lane == row, turned, 0.0), axis=0, keepdims=True)
    half = R // 2
    folded = jnp.where(lane[:half] < R, mixed[:half], pltpu.roll(mixed[half:], R, 1))
    return jnp.concatenate([folded, jnp.broadcast_to(diagonal, (8, PAIR))], axis=0)


def unfold_pair(folded):
    row = lax.broadcasted_iota(jnp.int32, (R, PAIR), 0)
    lane = lax.broadcasted_iota(jnp.int32, (R, PAIR), 1)
    low = lane < R
    column = jnp.where(low, lane, lane - R)
    half = R // 2
    turned = pltpu.roll(folded, R, 1)
    wide = low[:half]
    mixed = jnp.concatenate(
        [jnp.where(wide, folded[:half], turned[:half]), jnp.where(wide, turned[:half], folded[:half])], axis=0
    )
    flipped = jnp.concatenate([mixed, mixed], axis=0).T[:R]
    pair = jnp.where((column >= row) == low, mixed, flipped)
    return jnp.where((column == row) & (lane >= R), turned[half : half + 1], pair)


def statistics_kernel(acts_ref, outs_ref, keep_cov, send_cov, keep_mom, send_mom):
    first = lax.axis_index("dp") & 1 == 0
    acts = acts_ref[...]
    outs = outs_ref[...]
    low = lax.broadcasted_iota(jnp.int32, (R, PAIR), 1) < R
    cov_in = dot(acts, acts, NT)
    cov_out = dot(outs, outs, NT)
    cov0 = jnp.where(low, cov_in[:R], pltpu.roll(cov_out[:R], R, 1))
    cov1 = jnp.where(low, pltpu.roll(cov_in[R:], R, 1), cov_out[R:])
    cov0, cov1 = fold_pair(cov0), fold_pair(cov1)
    keep_cov[...] = jnp.where(first, cov0, cov1)
    send_cov[...] = jnp.where(first, cov1, cov0)
    for pair in range(acts.shape[1] // LEN // 2):
        blocks = []
        for seq in (2 * pair, 2 * pair + 1):
            tokens = slice(seq * LEN, (seq + 1) * LEN)
            blocks.append(dot(outs[:, tokens], acts[:, tokens], NT) * (1.0 / LEN))
        mom0 = jnp.where(low, blocks[0][:R], pltpu.roll(blocks[1][:R], R, 1))
        mom1 = jnp.where(low, pltpu.roll(blocks[0][R:], R, 1), blocks[1][R:])
        lanes = slice(pair * PAIR, (pair + 1) * PAIR)
        keep_mom[:, lanes] = jnp.where(first, mom0, mom1)
        send_mom[:, lanes] = jnp.where(first, mom1, mom0)


def statistics(acts, outs):
    seqs = acts.shape[1] // LEN
    cov = jax.ShapeDtypeStruct((R // 2 + 8, PAIR), F32)
    mom = jax.ShapeDtypeStruct((R, seqs * R), F32)
    vmem = pl.BlockSpec(memory_space=pltpu.VMEM)
    return pl.pallas_call(
        statistics_kernel,
        in_specs=[vmem, vmem],
        out_specs=[vmem] * 4,
        out_shape=[cov, cov, mom, mom],
        compiler_params=pltpu.CompilerParams(vmem_limit_bytes=16 * MIB),
        name="statistics",
    )(acts, outs)


def solve_block(p, rows):
    det = 1.0 / (p[0][0] * p[1][1] - p[0][1] * p[0][1])
    a, b, c = p[1][1] * det, -p[0][1] * det, p[0][0] * det
    t = [[a * p[0][j] + b * p[1][j], b * p[0][j] + c * p[1][j]] for j in (2, 3)]
    s22 = p[2][2] - p[0][2] * t[0][0] - p[1][2] * t[0][1]
    s23 = p[2][3] - p[0][2] * t[1][0] - p[1][2] * t[1][1]
    s33 = p[3][3] - p[0][3] * t[1][0] - p[1][3] * t[1][1]
    det = 1.0 / (s22 * s33 - s23 * s23)
    y0 = a * rows[0] + b * rows[1]
    y1 = b * rows[0] + c * rows[1]
    z2 = rows[2] - p[0][2] * y0 - p[1][2] * y1
    z3 = rows[3] - p[0][3] * y0 - p[1][3] * y1
    x2 = (s33 * z2 - s23 * z3) * det
    x3 = (s22 * z3 - s23 * z2) * det
    return [y0 - t[0][0] * x2 - t[1][0] * x3, y1 - t[0][1] * x2 - t[1][1] * x3, x2, x3]


def invert_pair(matrix):
    lane = lax.broadcasted_iota(jnp.int32, (8, PAIR), 1)
    row = lax.broadcasted_iota(jnp.int32, (8, PAIR), 0)
    column = lane % R
    base = lane - column
    work = [matrix[8 * g : 8 * g + 8] for g in range(R // 8)]
    for k in range(0, R, BLOCK):
        cols = [[jnp.take_along_axis(part, base + (k + j), axis=1) for j in range(BLOCK)] for part in work]
        home, at = k // 8, k % 8
        inside = (column >= k) & (column < k + BLOCK)
        pivots = [[cols[home][j][at + i : at + i + 1] for j in range(BLOCK)] for i in range(BLOCK)]
        rows = [
            jnp.where(
                inside[:1], jnp.where(column[:1] == k + i, 1.0, 0.0), work[home][at + i : at + i + 1]
            )
            for i in range(BLOCK)
        ]
        solved = solve_block(pivots, rows)
        for g in range(R // 8):
            part = jnp.where(inside, 0.0, work[g])
            col = cols[g]
            if g == home:
                block_row = (row >= at) & (row < at + BLOCK)
                part = jnp.where(block_row, 0.0, part)
                col = [
                    jnp.where(block_row, jnp.where(row == at + j, -1.0, 0.0), col[j]) for j in range(BLOCK)
                ]
            work[g] = part - (col[0] * solved[0] + col[1] * solved[1]) - (col[2] * solved[2] + col[3] * solved[3])
    return jnp.concatenate(work, axis=0)


def inverse_kernel(total_tokens, *refs):
    cov_refs, inv_ref = refs[:-1], refs[-1]
    row = lax.broadcasted_iota(jnp.int32, (R, PAIR), 0)
    lane = lax.broadcasted_iota(jnp.int32, (R, PAIR), 1)
    low = lane < R
    column = jnp.where(low, lane, lane - R)
    cov = unfold_pair(sum(ref[...] for ref in cov_refs))
    diagonal = jnp.where(row == column, cov, 0.0)
    trace_in = jnp.sum(jnp.where(low, diagonal, 0.0), keepdims=True)
    trace_out = jnp.sum(jnp.where(low, 0.0, diagonal), keepdims=True)
    scale = R / jnp.where(low, trace_in, trace_out)
    inv_ref[...] = invert_pair(cov * scale + jnp.where(row == column, DAMPING, 0.0)) * (scale * total_tokens)


def inverse(covs, total_tokens):
    vmem = pl.BlockSpec(memory_space=pltpu.VMEM)
    return pl.pallas_call(
        functools.partial(inverse_kernel, total_tokens),
        in_specs=[vmem] * len(covs),
        out_specs=vmem,
        out_shape=jax.ShapeDtypeStruct((R, PAIR), F32),
        compiler_params=pltpu.CompilerParams(vmem_limit_bytes=16 * MIB),
        name="inverse",
    )(*covs)


def scores_kernel(order, inv_ref, keep_ref, recv_ref, *refs):
    query_refs, (out_ref, flat_ref, part_ref) = refs[:-3], refs[-3:]
    place = lax.axis_index("dp")
    low = lax.broadcasted_iota(jnp.int32, (R, PAIR), 1) < R
    inv = inv_ref[...]
    tiles = R // 2
    left = jnp.concatenate([inv_ref[pl.ds(start, tiles, stride=2), :] for start in range(2)], axis=0)
    left = pltpu.roll(left, R, 1)[:, :R]
    moments = jnp.concatenate([keep_ref[...], recv_ref[...]], axis=1)
    mixed = dot(left, moments, NN, lax.Precision.HIGHEST)
    pairs = moments.shape[1] // PAIR
    stack = jnp.concatenate(
        [
            jnp.concatenate(
                [mixed[:tiles, j * PAIR : (j + 1) * PAIR], mixed[tiles:, j * PAIR : (j + 1) * PAIR]], axis=1
            )
            for j in range(pairs)
        ],
        axis=0,
    )
    zero = jnp.zeros((R, PAIR), F32)
    at_low = jnp.where(low, inv, 0.0)
    at_high = pltpu.roll(at_low, R, 1)
    right = jnp.concatenate(
        [
            jnp.concatenate([at_low, zero], axis=1),
            jnp.concatenate([zero, at_low], axis=1),
            jnp.concatenate([at_high, zero], axis=1),
            jnp.concatenate([zero, at_high], axis=1),
        ],
        axis=0,
    )
    done = dot(stack, right, NN, lax.Precision.HIGHEST)
    for j in range(pairs):
        rows = done[j * tiles : (j + 1) * tiles]
        flat_ref[(2 * j) * tiles : (2 * j + 1) * tiles, :] = rows[:, :PAIR]
        flat_ref[(2 * j + 1) * tiles : (2 * j + 2) * tiles, :] = rows[:, PAIR:]
    flat = jnp.concatenate(
        [flat_ref[pl.ds(k, 2 * pairs, stride=tiles), :].astype(BF16) for k in range(tiles)], axis=1
    )
    part = dot(jnp.concatenate([ref[...] for ref in query_refs], axis=0), flat, NT)
    group = part_ref.shape[1]
    for at, distance in enumerate(order):
        part_ref[place ^ distance] = part[at * group : (at + 1) * group]
    out_ref[...] = part_ref[...].reshape(part.shape).T


def score(inv, moments, queries, order):
    seqs = sum(part.shape[1] for part in moments) // R
    count = sum(part.shape[0] for part in queries)
    vmem = pl.BlockSpec(memory_space=pltpu.VMEM)
    return pl.pallas_call(
        functools.partial(scores_kernel, order),
        in_specs=[vmem] * (1 + len(moments) + len(queries)),
        out_specs=vmem,
        out_shape=jax.ShapeDtypeStruct((seqs, count), F32),
        scratch_shapes=[
            pltpu.VMEM((seqs * R // 2, PAIR), F32),
            pltpu.VMEM((len(order), count // len(order), seqs), F32),
        ],
        compiler_params=pltpu.CompilerParams(vmem_limit_bytes=16 * MIB),
        name="scores",
    )(inv, *moments, *queries)


def exchange(value, distance):
    return lax.ppermute(value, "dp", [(i, i ^ distance) for i in range(lax.axis_size("dp"))])


def halves(value, upper):
    low, high = jnp.split(value, 2, axis=1)
    return jnp.where(upper, high, low), jnp.where(upper, low, high)


def per_device(layer_input, out_grads, in_proj, out_proj, queries):
    local_tokens = layer_input.shape[0]
    devices = lax.axis_size("dp")
    slabs = devices // GROUP
    device, queries = lax.optimization_barrier((own_place(), queries))
    near_slabs, far_slabs = [0, 2], [1, 3] + list(range(4, slabs))
    column = {slab: exchange(queries, slab * GROUP) for slab in [2, 3, 1] + list(range(4, slabs))}
    column[0] = queries
    acts = project(layer_input, in_proj.reshape(PAIR, in_proj.shape[2]))
    acts, out_grads, column[0] = lax.optimization_barrier((acts, out_grads, column[0]))
    upper = device[0] & 1 == 1

    def fold(picked):
        keep, send = zip(*(halves(column[slab], upper) for slab in picked))
        keep, send = jnp.concatenate(keep, axis=0), jnp.concatenate(send, axis=0)
        return jnp.concatenate([keep, exchange(send, 1)], axis=0)

    outs = jnp.einsum("tmk,mrk->tmr", out_grads, out_proj, preferred_element_type=F32).astype(BF16)
    outs = outs.reshape(local_tokens, PAIR).T
    keep_cov, send_cov, keep_mom, send_mom = statistics(acts, outs)
    cov = keep_cov + exchange(send_cov, 1)
    moments = [keep_mom, exchange(send_mom, 1)]
    cov, column[3] = lax.optimization_barrier((cov, column[3]))
    cov = cov + exchange(cov, 2)
    far = fold(far_slabs)
    cov, far = lax.optimization_barrier((cov, far))
    cov = cov + exchange(cov, GROUP)
    near = fold(near_slabs)
    across = exchange(near, 2)
    distance = 2 * GROUP
    while distance < devices:
        last = exchange(cov, distance)
        if 2 * distance < devices:
            cov = cov + last
        distance *= 2
    inv = inverse([cov, last], local_tokens * devices)
    gathered = [near, across, far, exchange(far, 2)]
    order = [
        slab * GROUP + 2 * over + core
        for part in (near_slabs, far_slabs)
        for over in range(2)
        for core in range(2)
        for slab in part
    ]
    partial = score(inv, moments, gathered, order)
    seqs = local_tokens // LEN
    return partial[:seqs] + exchange(partial[seqs:], 1)


def solution(mesh):
    return jax.shard_map(
        per_device,
        mesh=mesh,
        in_specs=(
            P(("parts", "dp"), None),
            P(("parts", "dp"), None, None),
            P(),
            P(),
            P(("parts", "dp"), None),
        ),
        out_specs=P(("parts", "dp"), None),
        check_vma=False,
    )
```

```python
import functools

import jax
import jax.numpy as jnp
from jax import lax
from jax.experimental import pallas as pl
from jax.experimental.pallas import tpu as pltpu
from jax.sharding import PartitionSpec as P

R = 64
LEN = 128
PAIR = 2 * R
DAMPING = 0.1
ROWS = 256
STAGE = 8 * 10**10
BLOCK = 4
GROUP = 4

F32 = jnp.float32
BF16 = jnp.bfloat16
MIB = 1024 * 1024


def dot(a, b, dims, precision=None):
    return lax.dot_general(a, b, (dims, ((), ())), precision=precision, preferred_element_type=F32)


NN = ((1,), (0,))
NT = ((1,), (1,))


def place_kernel(out_ref):
    out_ref[0] = lax.axis_index("dp")


def own_place():
    return pl.pallas_call(
        place_kernel,
        out_specs=pl.BlockSpec(memory_space=pltpu.SMEM),
        out_shape=jax.ShapeDtypeStruct((1,), jnp.int32),
        compiler_params=pltpu.CompilerParams(vmem_limit_bytes=MIB),
        cost_estimate=pl.CostEstimate(flops=STAGE, bytes_accessed=8, transcendentals=0),
        name="own_place",
    )()


def project_kernel(x_ref, w_ref, acts_ref):
    tokens = x_ref.shape[0]
    for at in range(0, tokens, ROWS):
        acts_ref[:, at : at + ROWS] = dot(w_ref[...], x_ref[at : at + ROWS], NT).astype(BF16)


def project(layer_input, in_flat):
    tokens, width = layer_input.shape
    vmem = pl.BlockSpec(memory_space=pltpu.VMEM)
    return pl.pallas_call(
        project_kernel,
        in_specs=[vmem, vmem],
        out_specs=vmem,
        out_shape=jax.ShapeDtypeStruct((PAIR, tokens), BF16),
        compiler_params=pltpu.CompilerParams(vmem_limit_bytes=24 * MIB),
        cost_estimate=pl.CostEstimate(
            flops=4 * tokens * width * PAIR, bytes_accessed=2 * tokens * width, transcendentals=0
        ),
        name="project",
    )(layer_input, in_flat)


def fold_pair(pair):
    row = lax.broadcasted_iota(jnp.int32, (R, PAIR), 0)
    lane = lax.broadcasted_iota(jnp.int32, (R, PAIR), 1)
    turned = pltpu.roll(pair, R, 1)
    mixed = jnp.where(lane >= row, pair, turned)
    diagonal = jnp.sum(jnp.where(lane == row, turned, 0.0), axis=0, keepdims=True)
    half = R // 2
    folded = jnp.where(lane[:half] < R, mixed[:half], pltpu.roll(mixed[half:], R, 1))
    return jnp.concatenate([folded, jnp.broadcast_to(diagonal, (8, PAIR))], axis=0)


def unfold_pair(folded):
    row = lax.broadcasted_iota(jnp.int32, (R, PAIR), 0)
    lane = lax.broadcasted_iota(jnp.int32, (R, PAIR), 1)
    low = lane < R
    column = jnp.where(low, lane, lane - R)
    half = R // 2
    turned = pltpu.roll(folded, R, 1)
    wide = low[:half]
    mixed = jnp.concatenate(
        [jnp.where(wide, folded[:half], turned[:half]), jnp.where(wide, turned[:half], folded[:half])], axis=0
    )
    flipped = jnp.concatenate([mixed, mixed], axis=0).T[:R]
    pair = jnp.where((column >= row) == low, mixed, flipped)
    return jnp.where((column == row) & (lane >= R), turned[half : half + 1], pair)


def statistics_kernel(acts_ref, outs_ref, keep_cov, send_cov, keep_mom, send_mom):
    first = lax.axis_index("dp") & 1 == 0
    acts = acts_ref[...]
    outs = outs_ref[...]
    low = lax.broadcasted_iota(jnp.int32, (R, PAIR), 1) < R
    cov_in = dot(acts, acts, NT)
    cov_out = dot(outs, outs, NT)
    cov0 = jnp.where(low, cov_in[:R], pltpu.roll(cov_out[:R], R, 1))
    cov1 = jnp.where(low, pltpu.roll(cov_in[R:], R, 1), cov_out[R:])
    cov0, cov1 = fold_pair(cov0), fold_pair(cov1)
    keep_cov[...] = jnp.where(first, cov0, cov1)
    send_cov[...] = jnp.where(first, cov1, cov0)
    for pair in range(acts.shape[1] // LEN // 2):
        blocks = []
        for seq in (2 * pair, 2 * pair + 1):
            tokens = slice(seq * LEN, (seq + 1) * LEN)
            blocks.append(dot(outs[:, tokens], acts[:, tokens], NT) * (1.0 / LEN))
        mom0 = jnp.where(low, blocks[0][:R], pltpu.roll(blocks[1][:R], R, 1))
        mom1 = jnp.where(low, pltpu.roll(blocks[0][R:], R, 1), blocks[1][R:])
        lanes = slice(pair * PAIR, (pair + 1) * PAIR)
        keep_mom[:, lanes] = jnp.where(first, mom0, mom1)
        send_mom[:, lanes] = jnp.where(first, mom1, mom0)


def statistics(acts, outs):
    seqs = acts.shape[1] // LEN
    cov = jax.ShapeDtypeStruct((R // 2 + 8, PAIR), F32)
    mom = jax.ShapeDtypeStruct((R, seqs * R), F32)
    vmem = pl.BlockSpec(memory_space=pltpu.VMEM)
    return pl.pallas_call(
        statistics_kernel,
        in_specs=[vmem, vmem],
        out_specs=[vmem] * 4,
        out_shape=[cov, cov, mom, mom],
        compiler_params=pltpu.CompilerParams(vmem_limit_bytes=16 * MIB),
        name="statistics",
    )(acts, outs)


def solve_block(p, rows):
    det = 1.0 / (p[0][0] * p[1][1] - p[0][1] * p[0][1])
    a, b, c = p[1][1] * det, -p[0][1] * det, p[0][0] * det
    t = [[a * p[0][j] + b * p[1][j], b * p[0][j] + c * p[1][j]] for j in (2, 3)]
    s22 = p[2][2] - p[0][2] * t[0][0] - p[1][2] * t[0][1]
    s23 = p[2][3] - p[0][2] * t[1][0] - p[1][2] * t[1][1]
    s33 = p[3][3] - p[0][3] * t[1][0] - p[1][3] * t[1][1]
    det = 1.0 / (s22 * s33 - s23 * s23)
    y0 = a * rows[0] + b * rows[1]
    y1 = b * rows[0] + c * rows[1]
    z2 = rows[2] - p[0][2] * y0 - p[1][2] * y1
    z3 = rows[3] - p[0][3] * y0 - p[1][3] * y1
    x2 = (s33 * z2 - s23 * z3) * det
    x3 = (s22 * z3 - s23 * z2) * det
    return [y0 - t[0][0] * x2 - t[1][0] * x3, y1 - t[0][1] * x2 - t[1][1] * x3, x2, x3]


def invert_pair(matrix):
    lane = lax.broadcasted_iota(jnp.int32, (8, PAIR), 1)
    row = lax.broadcasted_iota(jnp.int32, (8, PAIR), 0)
    column = lane % R
    base = lane - column
    work = [matrix[8 * g : 8 * g + 8] for g in range(R // 8)]
    for k in range(0, R, BLOCK):
        cols = [[jnp.take_along_axis(part, base + (k + j), axis=1) for j in range(BLOCK)] for part in work]
        home, at = k // 8, k % 8
        inside = (column >= k) & (column < k + BLOCK)
        pivots = [[cols[home][j][at + i : at + i + 1] for j in range(BLOCK)] for i in range(BLOCK)]
        rows = [
            jnp.where(
                inside[:1], jnp.where(column[:1] == k + i, 1.0, 0.0), work[home][at + i : at + i + 1]
            )
            for i in range(BLOCK)
        ]
        solved = solve_block(pivots, rows)
        for g in range(R // 8):
            part = jnp.where(inside, 0.0, work[g])
            col = cols[g]
            if g == home:
                block_row = (row >= at) & (row < at + BLOCK)
                part = jnp.where(block_row, 0.0, part)
                col = [
                    jnp.where(block_row, jnp.where(row == at + j, -1.0, 0.0), col[j]) for j in range(BLOCK)
                ]
            work[g] = part - (col[0] * solved[0] + col[1] * solved[1]) - (col[2] * solved[2] + col[3] * solved[3])
    return jnp.concatenate(work, axis=0)


def inverse_kernel(total_tokens, *refs):
    cov_refs, inv_ref = refs[:-1], refs[-1]
    row = lax.broadcasted_iota(jnp.int32, (R, PAIR), 0)
    lane = lax.broadcasted_iota(jnp.int32, (R, PAIR), 1)
    low = lane < R
    column = jnp.where(low, lane, lane - R)
    cov = unfold_pair(sum(ref[...] for ref in cov_refs))
    diagonal = jnp.where(row == column, cov, 0.0)
    trace_in = jnp.sum(jnp.where(low, diagonal, 0.0), keepdims=True)
    trace_out = jnp.sum(jnp.where(low, 0.0, diagonal), keepdims=True)
    scale = R / jnp.where(low, trace_in, trace_out)
    inv_ref[...] = invert_pair(cov * scale + jnp.where(row == column, DAMPING, 0.0)) * (scale * total_tokens)


def inverse(covs, total_tokens):
    vmem = pl.BlockSpec(memory_space=pltpu.VMEM)
    return pl.pallas_call(
        functools.partial(inverse_kernel, total_tokens),
        in_specs=[vmem] * len(covs),
        out_specs=vmem,
        out_shape=jax.ShapeDtypeStruct((R, PAIR), F32),
        compiler_params=pltpu.CompilerParams(vmem_limit_bytes=16 * MIB),
        name="inverse",
    )(*covs)


def precondition_kernel(inv_ref, keep_ref, recv_ref, out_ref, flat_ref):
    low = lax.broadcasted_iota(jnp.int32, (R, PAIR), 1) < R
    inv = inv_ref[...]
    tiles = R // 2
    left = jnp.concatenate([inv_ref[pl.ds(start, tiles, stride=2), :] for start in range(2)], axis=0)
    left = pltpu.roll(left, R, 1)[:, :R]
    moments = jnp.concatenate([keep_ref[...], recv_ref[...]], axis=1)
    mixed = dot(left, moments, NN, lax.Precision.HIGHEST)
    pairs = moments.shape[1] // PAIR
    stack = jnp.concatenate(
        [
            jnp.concatenate(
                [mixed[:tiles, j * PAIR : (j + 1) * PAIR], mixed[tiles:, j * PAIR : (j + 1) * PAIR]], axis=1
            )
            for j in range(pairs)
        ],
        axis=0,
    )
    zero = jnp.zeros((R, PAIR), F32)
    at_low = jnp.where(low, inv, 0.0)
    at_high = pltpu.roll(at_low, R, 1)
    right = jnp.concatenate(
        [
            jnp.concatenate([at_low, zero], axis=1),
            jnp.concatenate([zero, at_low], axis=1),
            jnp.concatenate([at_high, zero], axis=1),
            jnp.concatenate([zero, at_high], axis=1),
        ],
        axis=0,
    )
    done = dot(stack, right, NN, lax.Precision.HIGHEST)
    for j in range(pairs):
        rows = done[j * tiles : (j + 1) * tiles]
        flat_ref[(2 * j) * tiles : (2 * j + 1) * tiles, :] = rows[:, :PAIR]
        flat_ref[(2 * j + 1) * tiles : (2 * j + 2) * tiles, :] = rows[:, PAIR:]
    for k in range(tiles):
        out_ref[:, k * PAIR : (k + 1) * PAIR] = flat_ref[pl.ds(k, 2 * pairs, stride=tiles), :].astype(BF16)


def precondition(inv, moments):
    seqs = sum(part.shape[1] for part in moments) // R
    vmem = pl.BlockSpec(memory_space=pltpu.VMEM)
    return pl.pallas_call(
        precondition_kernel,
        in_specs=[vmem] * (1 + len(moments)),
        out_specs=vmem,
        out_shape=jax.ShapeDtypeStruct((seqs, R * R), BF16),
        scratch_shapes=[pltpu.VMEM((seqs * R // 2, PAIR), F32)],
        compiler_params=pltpu.CompilerParams(vmem_limit_bytes=16 * MIB),
        name="precondition",
    )(inv, *moments)


def scores_kernel(order, flat_ref, *refs):
    query_refs, (out_ref, part_ref) = refs[:-2], refs[-2:]
    place = lax.axis_index("dp")
    part = dot(jnp.concatenate([ref[...] for ref in query_refs], axis=0), flat_ref[...], NT)
    group = part_ref.shape[1]
    for at, distance in enumerate(order):
        part_ref[place ^ distance] = part[at * group : (at + 1) * group]
    out_ref[...] = part_ref[...].reshape(part.shape).T


def score(flat, queries, order):
    seqs = flat.shape[0]
    count = sum(part.shape[0] for part in queries)
    vmem = pl.BlockSpec(memory_space=pltpu.VMEM)
    return pl.pallas_call(
        functools.partial(scores_kernel, order),
        in_specs=[vmem] * (1 + len(queries)),
        out_specs=vmem,
        out_shape=jax.ShapeDtypeStruct((seqs, count), F32),
        scratch_shapes=[pltpu.VMEM((len(order), count // len(order), seqs), F32)],
        compiler_params=pltpu.CompilerParams(vmem_limit_bytes=16 * MIB),
        name="scores",
    )(flat, *queries)


def exchange(value, distance):
    return lax.ppermute(value, "dp", [(i, i ^ distance) for i in range(lax.axis_size("dp"))])


def halves(value, upper):
    low, high = jnp.split(value, 2, axis=1)
    return jnp.where(upper, high, low), jnp.where(upper, low, high)


def per_device(layer_input, out_grads, in_proj, out_proj, queries):
    local_tokens = layer_input.shape[0]
    devices = lax.axis_size("dp")
    slabs = devices // GROUP
    device, queries = lax.optimization_barrier((own_place(), queries))
    near_slabs, far_slabs = [0, 1], [2, 3] + list(range(4, slabs))
    column = {slab: exchange(queries, slab * GROUP) for slab in [1, 2, 3] + list(range(4, slabs))}
    column[0] = queries
    acts = project(layer_input, in_proj.reshape(PAIR, in_proj.shape[2]))
    acts, out_grads, column[0] = lax.optimization_barrier((acts, out_grads, column[0]))
    upper = device[0] & 1 == 1

    def fold(picked):
        keep, send = zip(*(halves(column[slab], upper) for slab in picked))
        keep, send = jnp.concatenate(keep, axis=0), jnp.concatenate(send, axis=0)
        return jnp.concatenate([keep, exchange(send, 1)], axis=0)

    outs = jnp.einsum("tmk,mrk->tmr", out_grads, out_proj, preferred_element_type=F32).astype(BF16)
    outs = outs.reshape(local_tokens, PAIR).T
    keep_cov, send_cov, keep_mom, send_mom = statistics(acts, outs)
    cov = keep_cov + exchange(send_cov, 1)
    moments = [keep_mom, exchange(send_mom, 1)]
    cov, column[3] = lax.optimization_barrier((cov, column[3]))
    cov = cov + exchange(cov, 2)
    far = fold(far_slabs)
    cov, far, moments = lax.optimization_barrier((cov, far, moments))
    near = fold(near_slabs)
    across = exchange(near, 2)
    covs = [cov] + [exchange(cov, slab * GROUP) for slab in range(1, slabs)]
    covs, across = lax.optimization_barrier((covs, across))
    inv = inverse(covs, local_tokens * devices)
    gathered = [near, across, far, exchange(far, 2)]
    order = [
        slab * GROUP + 2 * over + core
        for part in (near_slabs, far_slabs)
        for over in range(2)
        for core in range(2)
        for slab in part
    ]
    partial = score(precondition(inv, moments), gathered, order)
    seqs = local_tokens // LEN
    return partial[:seqs] + exchange(partial[seqs:], 1)


def solution(mesh):
    return jax.shard_map(
        per_device,
        mesh=mesh,
        in_specs=(
            P(("parts", "dp"), None),
            P(("parts", "dp"), None, None),
            P(),
            P(),
            P(("parts", "dp"), None),
        ),
        out_specs=P(("parts", "dp"), None),
        check_vma=False,
    )
```

```python
import functools

import jax
import jax.numpy as jnp
from jax import lax
from jax.experimental import pallas as pl
from jax.experimental.pallas import tpu as pltpu
from jax.sharding import PartitionSpec as P

R = 64
LEN = 128
PAIR = 2 * R
DAMPING = 0.1
ROWS = 256
STAGE = 8 * 10**10
BLOCK = 4
GROUP = 4

F32 = jnp.float32
BF16 = jnp.bfloat16
MIB = 1024 * 1024


def dot(a, b, dims, precision=None):
    return lax.dot_general(a, b, (dims, ((), ())), precision=precision, preferred_element_type=F32)


NN = ((1,), (0,))
NT = ((1,), (1,))


def place_kernel(out_ref):
    out_ref[0] = lax.axis_index("dp")


def own_place():
    return pl.pallas_call(
        place_kernel,
        out_specs=pl.BlockSpec(memory_space=pltpu.SMEM),
        out_shape=jax.ShapeDtypeStruct((1,), jnp.int32),
        compiler_params=pltpu.CompilerParams(vmem_limit_bytes=MIB),
        cost_estimate=pl.CostEstimate(flops=STAGE, bytes_accessed=8, transcendentals=0),
        name="own_place",
    )()


def project_kernel(x_ref, w_ref, acts_ref):
    tokens = x_ref.shape[0]
    for at in range(0, tokens, ROWS):
        acts_ref[:, at : at + ROWS] = dot(w_ref[...], x_ref[at : at + ROWS], NT).astype(BF16)


def project(layer_input, in_flat):
    tokens, width = layer_input.shape
    vmem = pl.BlockSpec(memory_space=pltpu.VMEM)
    return pl.pallas_call(
        project_kernel,
        in_specs=[vmem, vmem],
        out_specs=vmem,
        out_shape=jax.ShapeDtypeStruct((PAIR, tokens), BF16),
        compiler_params=pltpu.CompilerParams(vmem_limit_bytes=24 * MIB),
        cost_estimate=pl.CostEstimate(
            flops=4 * tokens * width * PAIR, bytes_accessed=2 * tokens * width, transcendentals=0
        ),
        name="project",
    )(layer_input, in_flat)


def fold_pair(pair):
    row = lax.broadcasted_iota(jnp.int32, (R, PAIR), 0)
    lane = lax.broadcasted_iota(jnp.int32, (R, PAIR), 1)
    turned = pltpu.roll(pair, R, 1)
    mixed = jnp.where(lane >= row, pair, turned)
    diagonal = jnp.sum(jnp.where(lane == row, turned, 0.0), axis=0, keepdims=True)
    half = R // 2
    folded = jnp.where(lane[:half] < R, mixed[:half], pltpu.roll(mixed[half:], R, 1))
    return jnp.concatenate([folded, jnp.broadcast_to(diagonal, (8, PAIR))], axis=0)


def unfold_pair(folded):
    row = lax.broadcasted_iota(jnp.int32, (R, PAIR), 0)
    lane = lax.broadcasted_iota(jnp.int32, (R, PAIR), 1)
    low = lane < R
    column = jnp.where(low, lane, lane - R)
    half = R // 2
    turned = pltpu.roll(folded, R, 1)
    wide = low[:half]
    mixed = jnp.concatenate(
        [jnp.where(wide, folded[:half], turned[:half]), jnp.where(wide, turned[:half], folded[:half])], axis=0
    )
    flipped = jnp.concatenate([mixed, mixed], axis=0).T[:R]
    pair = jnp.where((column >= row) == low, mixed, flipped)
    return jnp.where((column == row) & (lane >= R), turned[half : half + 1], pair)


def statistics_kernel(acts_ref, outs_ref, keep_cov, send_cov, keep_mom, send_mom):
    first = lax.axis_index("dp") & 1 == 0
    acts = acts_ref[...]
    outs = outs_ref[...]
    low = lax.broadcasted_iota(jnp.int32, (R, PAIR), 1) < R
    cov_in = dot(acts, acts, NT)
    cov_out = dot(outs, outs, NT)
    cov0 = jnp.where(low, cov_in[:R], pltpu.roll(cov_out[:R], R, 1))
    cov1 = jnp.where(low, pltpu.roll(cov_in[R:], R, 1), cov_out[R:])
    cov0, cov1 = fold_pair(cov0), fold_pair(cov1)
    keep_cov[...] = jnp.where(first, cov0, cov1)
    send_cov[...] = jnp.where(first, cov1, cov0)
    for pair in range(acts.shape[1] // LEN // 2):
        blocks = []
        for seq in (2 * pair, 2 * pair + 1):
            tokens = slice(seq * LEN, (seq + 1) * LEN)
            blocks.append(dot(outs[:, tokens], acts[:, tokens], NT) * (1.0 / LEN))
        mom0 = jnp.where(low, blocks[0][:R], pltpu.roll(blocks[1][:R], R, 1))
        mom1 = jnp.where(low, pltpu.roll(blocks[0][R:], R, 1), blocks[1][R:])
        lanes = slice(pair * PAIR, (pair + 1) * PAIR)
        keep_mom[:, lanes] = jnp.where(first, mom0, mom1)
        send_mom[:, lanes] = jnp.where(first, mom1, mom0)


def statistics(acts, outs):
    seqs = acts.shape[1] // LEN
    cov = jax.ShapeDtypeStruct((R // 2 + 8, PAIR), F32)
    mom = jax.ShapeDtypeStruct((R, seqs * R), F32)
    vmem = pl.BlockSpec(memory_space=pltpu.VMEM)
    return pl.pallas_call(
        statistics_kernel,
        in_specs=[vmem, vmem],
        out_specs=[vmem] * 4,
        out_shape=[cov, cov, mom, mom],
        compiler_params=pltpu.CompilerParams(vmem_limit_bytes=16 * MIB),
        name="statistics",
    )(acts, outs)


def solve_block(p, rows):
    det = 1.0 / (p[0][0] * p[1][1] - p[0][1] * p[0][1])
    a, b, c = p[1][1] * det, -p[0][1] * det, p[0][0] * det
    t = [[a * p[0][j] + b * p[1][j], b * p[0][j] + c * p[1][j]] for j in (2, 3)]
    s22 = p[2][2] - p[0][2] * t[0][0] - p[1][2] * t[0][1]
    s23 = p[2][3] - p[0][2] * t[1][0] - p[1][2] * t[1][1]
    s33 = p[3][3] - p[0][3] * t[1][0] - p[1][3] * t[1][1]
    det = 1.0 / (s22 * s33 - s23 * s23)
    y0 = a * rows[0] + b * rows[1]
    y1 = b * rows[0] + c * rows[1]
    z2 = rows[2] - p[0][2] * y0 - p[1][2] * y1
    z3 = rows[3] - p[0][3] * y0 - p[1][3] * y1
    x2 = (s33 * z2 - s23 * z3) * det
    x3 = (s22 * z3 - s23 * z2) * det
    return [y0 - t[0][0] * x2 - t[1][0] * x3, y1 - t[0][1] * x2 - t[1][1] * x3, x2, x3]


def invert_pair(matrix):
    lane = lax.broadcasted_iota(jnp.int32, (8, PAIR), 1)
    row = lax.broadcasted_iota(jnp.int32, (8, PAIR), 0)
    column = lane % R
    base = lane - column
    work = [matrix[8 * g : 8 * g + 8] for g in range(R // 8)]
    for k in range(0, R, BLOCK):
        cols = [[jnp.take_along_axis(part, base + (k + j), axis=1) for j in range(BLOCK)] for part in work]
        home, at = k // 8, k % 8
        inside = (column >= k) & (column < k + BLOCK)
        pivots = [[cols[home][j][at + i : at + i + 1] for j in range(BLOCK)] for i in range(BLOCK)]
        rows = [
            jnp.where(
                inside[:1], jnp.where(column[:1] == k + i, 1.0, 0.0), work[home][at + i : at + i + 1]
            )
            for i in range(BLOCK)
        ]
        solved = solve_block(pivots, rows)
        for g in range(R // 8):
            part = jnp.where(inside, 0.0, work[g])
            col = cols[g]
            if g == home:
                block_row = (row >= at) & (row < at + BLOCK)
                part = jnp.where(block_row, 0.0, part)
                col = [
                    jnp.where(block_row, jnp.where(row == at + j, -1.0, 0.0), col[j]) for j in range(BLOCK)
                ]
            work[g] = part - (col[0] * solved[0] + col[1] * solved[1]) - (col[2] * solved[2] + col[3] * solved[3])
    return jnp.concatenate(work, axis=0)


def inverse_kernel(total_tokens, *refs):
    cov_refs, inv_ref = refs[:-1], refs[-1]
    row = lax.broadcasted_iota(jnp.int32, (R, PAIR), 0)
    lane = lax.broadcasted_iota(jnp.int32, (R, PAIR), 1)
    low = lane < R
    column = jnp.where(low, lane, lane - R)
    cov = unfold_pair(sum(ref[...] for ref in cov_refs))
    diagonal = jnp.where(row == column, cov, 0.0)
    trace_in = jnp.sum(jnp.where(low, diagonal, 0.0), keepdims=True)
    trace_out = jnp.sum(jnp.where(low, 0.0, diagonal), keepdims=True)
    scale = R / jnp.where(low, trace_in, trace_out)
    inv_ref[...] = invert_pair(cov * scale + jnp.where(row == column, DAMPING, 0.0)) * (scale * total_tokens)


def inverse(covs, total_tokens):
    vmem = pl.BlockSpec(memory_space=pltpu.VMEM)
    return pl.pallas_call(
        functools.partial(inverse_kernel, total_tokens),
        in_specs=[vmem] * len(covs),
        out_specs=vmem,
        out_shape=jax.ShapeDtypeStruct((R, PAIR), F32),
        compiler_params=pltpu.CompilerParams(vmem_limit_bytes=16 * MIB),
        name="inverse",
    )(*covs)


def precondition_kernel(inv_ref, keep_ref, recv_ref, out_ref, flat_ref):
    low = lax.broadcasted_iota(jnp.int32, (R, PAIR), 1) < R
    inv = inv_ref[...]
    tiles = R // 2
    left = jnp.concatenate([inv_ref[pl.ds(start, tiles, stride=2), :] for start in range(2)], axis=0)
    left = pltpu.roll(left, R, 1)[:, :R]
    moments = jnp.concatenate([keep_ref[...], recv_ref[...]], axis=1)
    mixed = dot(left, moments, NN, lax.Precision.HIGHEST)
    pairs = moments.shape[1] // PAIR
    stack = jnp.concatenate(
        [
            jnp.concatenate(
                [mixed[:tiles, j * PAIR : (j + 1) * PAIR], mixed[tiles:, j * PAIR : (j + 1) * PAIR]], axis=1
            )
            for j in range(pairs)
        ],
        axis=0,
    )
    zero = jnp.zeros((R, PAIR), F32)
    at_low = jnp.where(low, inv, 0.0)
    at_high = pltpu.roll(at_low, R, 1)
    right = jnp.concatenate(
        [
            jnp.concatenate([at_low, zero], axis=1),
            jnp.concatenate([zero, at_low], axis=1),
            jnp.concatenate([at_high, zero], axis=1),
            jnp.concatenate([zero, at_high], axis=1),
        ],
        axis=0,
    )
    done = dot(stack, right, NN, lax.Precision.HIGHEST)
    for j in range(pairs):
        rows = done[j * tiles : (j + 1) * tiles]
        flat_ref[(2 * j) * tiles : (2 * j + 1) * tiles, :] = rows[:, :PAIR]
        flat_ref[(2 * j + 1) * tiles : (2 * j + 2) * tiles, :] = rows[:, PAIR:]
    for k in range(tiles):
        out_ref[:, k * PAIR : (k + 1) * PAIR] = flat_ref[pl.ds(k, 2 * pairs, stride=tiles), :].astype(BF16)


def precondition(inv, moments):
    seqs = sum(part.shape[1] for part in moments) // R
    vmem = pl.BlockSpec(memory_space=pltpu.VMEM)
    return pl.pallas_call(
        precondition_kernel,
        in_specs=[vmem] * (1 + len(moments)),
        out_specs=vmem,
        out_shape=jax.ShapeDtypeStruct((seqs, R * R), BF16),
        scratch_shapes=[pltpu.VMEM((seqs * R // 2, PAIR), F32)],
        compiler_params=pltpu.CompilerParams(vmem_limit_bytes=16 * MIB),
        name="precondition",
    )(inv, *moments)


def scores_kernel(order, flat_ref, *refs):
    query_refs, (out_ref, part_ref) = refs[:-2], refs[-2:]
    place = lax.axis_index("dp")
    part = dot(jnp.concatenate([ref[...] for ref in query_refs], axis=0), flat_ref[...], NT)
    group = part_ref.shape[1]
    for at, distance in enumerate(order):
        part_ref[place ^ distance] = part[at * group : (at + 1) * group]
    out_ref[...] = part_ref[...].reshape(part.shape).T


def score(flat, queries, order):
    seqs = flat.shape[0]
    count = sum(part.shape[0] for part in queries)
    vmem = pl.BlockSpec(memory_space=pltpu.VMEM)
    return pl.pallas_call(
        functools.partial(scores_kernel, order),
        in_specs=[vmem] * (1 + len(queries)),
        out_specs=vmem,
        out_shape=jax.ShapeDtypeStruct((seqs, count), F32),
        scratch_shapes=[pltpu.VMEM((len(order), count // len(order), seqs), F32)],
        compiler_params=pltpu.CompilerParams(vmem_limit_bytes=16 * MIB),
        name="scores",
    )(flat, *queries)


def exchange(value, distance):
    return lax.ppermute(value, "dp", [(i, i ^ distance) for i in range(lax.axis_size("dp"))])


def halves(value, upper):
    low, high = jnp.split(value, 2, axis=1)
    return jnp.where(upper, high, low), jnp.where(upper, low, high)


def per_device(layer_input, out_grads, in_proj, out_proj, queries):
    local_tokens = layer_input.shape[0]
    devices = lax.axis_size("dp")
    slabs = devices // GROUP
    device, queries = lax.optimization_barrier((own_place(), queries))
    near_slabs, far_slabs = [0, 1], [2, 3] + list(range(4, slabs))
    column = {slab: exchange(queries, slab * GROUP) for slab in [1, 2, 3] + list(range(4, slabs))}
    column[0] = queries
    acts = project(layer_input, in_proj.reshape(PAIR, in_proj.shape[2]))
    acts, out_grads, column[0] = lax.optimization_barrier((acts, out_grads, column[0]))
    upper = device[0] & 1 == 1

    def fold(picked):
        keep, send = zip(*(halves(column[slab], upper) for slab in picked))
        keep, send = jnp.concatenate(keep, axis=0), jnp.concatenate(send, axis=0)
        return jnp.concatenate([keep, exchange(send, 1)], axis=0)

    outs = jnp.einsum("tmk,mrk->tmr", out_grads, out_proj, preferred_element_type=F32).astype(BF16)
    outs = outs.reshape(local_tokens, PAIR).T
    keep_cov, send_cov, keep_mom, send_mom = statistics(acts, outs)
    cov = keep_cov + exchange(send_cov, 1)
    moments = [keep_mom, exchange(send_mom, 1)]
    cov, column[3] = lax.optimization_barrier((cov, column[3]))
    cov = cov + exchange(cov, 2)
    far = fold(far_slabs)
    cov, far, moments = lax.optimization_barrier((cov, far, moments))
    near = fold(near_slabs)
    mine = jnp.concatenate([near, far], axis=0)
    across = exchange(mine, 2)
    covs = [cov] + [exchange(cov, slab * GROUP) for slab in reversed(range(1, slabs))]
    inv = inverse(covs, local_tokens * devices)
    gathered = [mine, across]
    order = [
        slab * GROUP + 2 * over + core
        for over in range(2)
        for part in (near_slabs, far_slabs)
        for core in range(2)
        for slab in part
    ]
    partial = score(precondition(inv, moments), gathered, order)
    seqs = local_tokens // LEN
    return partial[:seqs] + exchange(partial[seqs:], 1)


def solution(mesh):
    return jax.shard_map(
        per_device,
        mesh=mesh,
        in_specs=(
            P(("parts", "dp"), None),
            P(("parts", "dp"), None, None),
            P(),
            P(),
            P(("parts", "dp"), None),
        ),
        out_specs=P(("parts", "dp"), None),
        check_vma=False,
    )
```

```python
import functools

import jax
import jax.numpy as jnp
from jax import lax
from jax.experimental import pallas as pl
from jax.experimental.pallas import tpu as pltpu
from jax.sharding import PartitionSpec as P

R = 64
LEN = 128
PAIR = 2 * R
DAMPING = 0.1
ROWS = 256
STAGE = 8 * 10**10
BLOCK = 4
GROUP = 4

F32 = jnp.float32
BF16 = jnp.bfloat16
MIB = 1024 * 1024


def dot(a, b, dims, precision=None):
    return lax.dot_general(a, b, (dims, ((), ())), precision=precision, preferred_element_type=F32)


NN = ((1,), (0,))
NT = ((1,), (1,))


def place_kernel(out_ref):
    out_ref[0] = lax.axis_index("dp")


def own_place():
    return pl.pallas_call(
        place_kernel,
        out_specs=pl.BlockSpec(memory_space=pltpu.SMEM),
        out_shape=jax.ShapeDtypeStruct((1,), jnp.int32),
        compiler_params=pltpu.CompilerParams(vmem_limit_bytes=MIB),
        cost_estimate=pl.CostEstimate(flops=STAGE, bytes_accessed=8, transcendentals=0),
        name="own_place",
    )()


def project_kernel(x_ref, w_ref, acts_ref):
    tokens = x_ref.shape[0]
    for at in range(0, tokens, ROWS):
        acts_ref[:, at : at + ROWS] = dot(w_ref[...], x_ref[at : at + ROWS], NT).astype(BF16)


def project(layer_input, in_flat):
    tokens, width = layer_input.shape
    vmem = pl.BlockSpec(memory_space=pltpu.VMEM)
    return pl.pallas_call(
        project_kernel,
        in_specs=[vmem, vmem],
        out_specs=vmem,
        out_shape=jax.ShapeDtypeStruct((PAIR, tokens), BF16),
        compiler_params=pltpu.CompilerParams(vmem_limit_bytes=24 * MIB),
        cost_estimate=pl.CostEstimate(
            flops=4 * tokens * width * PAIR, bytes_accessed=2 * tokens * width, transcendentals=0
        ),
        name="project",
    )(layer_input, in_flat)


def fold_pair(pair):
    row = lax.broadcasted_iota(jnp.int32, (R, PAIR), 0)
    lane = lax.broadcasted_iota(jnp.int32, (R, PAIR), 1)
    turned = pltpu.roll(pair, R, 1)
    mixed = jnp.where(lane >= row, pair, turned)
    diagonal = jnp.sum(jnp.where(lane == row, turned, 0.0), axis=0, keepdims=True)
    half = R // 2
    folded = jnp.where(lane[:half] < R, mixed[:half], pltpu.roll(mixed[half:], R, 1))
    return jnp.concatenate([folded, jnp.broadcast_to(diagonal, (8, PAIR))], axis=0)


def unfold_pair(folded):
    row = lax.broadcasted_iota(jnp.int32, (R, PAIR), 0)
    lane = lax.broadcasted_iota(jnp.int32, (R, PAIR), 1)
    low = lane < R
    column = jnp.where(low, lane, lane - R)
    half = R // 2
    turned = pltpu.roll(folded, R, 1)
    wide = low[:half]
    mixed = jnp.concatenate(
        [jnp.where(wide, folded[:half], turned[:half]), jnp.where(wide, turned[:half], folded[:half])], axis=0
    )
    flipped = jnp.concatenate([mixed, mixed], axis=0).T[:R]
    pair = jnp.where((column >= row) == low, mixed, flipped)
    return jnp.where((column == row) & (lane >= R), turned[half : half + 1], pair)


def statistics_kernel(acts_ref, outs_ref, keep_cov, send_cov, keep_mom, send_mom):
    first = lax.axis_index("dp") & 1 == 0
    acts = acts_ref[...]
    outs = outs_ref[...]
    low = lax.broadcasted_iota(jnp.int32, (R, PAIR), 1) < R
    cov_in = dot(acts, acts, NT)
    cov_out = dot(outs, outs, NT)
    cov0 = jnp.where(low, cov_in[:R], pltpu.roll(cov_out[:R], R, 1))
    cov1 = jnp.where(low, pltpu.roll(cov_in[R:], R, 1), cov_out[R:])
    cov0, cov1 = fold_pair(cov0), fold_pair(cov1)
    keep_cov[...] = jnp.where(first, cov0, cov1)
    send_cov[...] = jnp.where(first, cov1, cov0)
    for pair in range(acts.shape[1] // LEN // 2):
        blocks = []
        for seq in (2 * pair, 2 * pair + 1):
            tokens = slice(seq * LEN, (seq + 1) * LEN)
            blocks.append(dot(outs[:, tokens], acts[:, tokens], NT) * (1.0 / LEN))
        mom0 = jnp.where(low, blocks[0][:R], pltpu.roll(blocks[1][:R], R, 1))
        mom1 = jnp.where(low, pltpu.roll(blocks[0][R:], R, 1), blocks[1][R:])
        lanes = slice(pair * PAIR, (pair + 1) * PAIR)
        keep_mom[:, lanes] = jnp.where(first, mom0, mom1)
        send_mom[:, lanes] = jnp.where(first, mom1, mom0)


def statistics(acts, outs):
    seqs = acts.shape[1] // LEN
    cov = jax.ShapeDtypeStruct((R // 2 + 8, PAIR), F32)
    mom = jax.ShapeDtypeStruct((R, seqs * R), F32)
    vmem = pl.BlockSpec(memory_space=pltpu.VMEM)
    return pl.pallas_call(
        statistics_kernel,
        in_specs=[vmem, vmem],
        out_specs=[vmem] * 4,
        out_shape=[cov, cov, mom, mom],
        compiler_params=pltpu.CompilerParams(vmem_limit_bytes=16 * MIB),
        name="statistics",
    )(acts, outs)


def solve_block(p, rows):
    det = 1.0 / (p[0][0] * p[1][1] - p[0][1] * p[0][1])
    a, b, c = p[1][1] * det, -p[0][1] * det, p[0][0] * det
    t = [[a * p[0][j] + b * p[1][j], b * p[0][j] + c * p[1][j]] for j in (2, 3)]
    s22 = p[2][2] - p[0][2] * t[0][0] - p[1][2] * t[0][1]
    s23 = p[2][3] - p[0][2] * t[1][0] - p[1][2] * t[1][1]
    s33 = p[3][3] - p[0][3] * t[1][0] - p[1][3] * t[1][1]
    det = 1.0 / (s22 * s33 - s23 * s23)
    y0 = a * rows[0] + b * rows[1]
    y1 = b * rows[0] + c * rows[1]
    z2 = rows[2] - p[0][2] * y0 - p[1][2] * y1
    z3 = rows[3] - p[0][3] * y0 - p[1][3] * y1
    x2 = (s33 * z2 - s23 * z3) * det
    x3 = (s22 * z3 - s23 * z2) * det
    return [y0 - t[0][0] * x2 - t[1][0] * x3, y1 - t[0][1] * x2 - t[1][1] * x3, x2, x3]


def invert_pair(matrix):
    lane = lax.broadcasted_iota(jnp.int32, (8, PAIR), 1)
    row = lax.broadcasted_iota(jnp.int32, (8, PAIR), 0)
    column = lane % R
    base = lane - column
    work = [matrix[8 * g : 8 * g + 8] for g in range(R // 8)]
    for k in range(0, R, BLOCK):
        cols = [[jnp.take_along_axis(part, base + (k + j), axis=1) for j in range(BLOCK)] for part in work]
        home, at = k // 8, k % 8
        inside = (column >= k) & (column < k + BLOCK)
        pivots = [[cols[home][j][at + i : at + i + 1] for j in range(BLOCK)] for i in range(BLOCK)]
        rows = [
            jnp.where(
                inside[:1], jnp.where(column[:1] == k + i, 1.0, 0.0), work[home][at + i : at + i + 1]
            )
            for i in range(BLOCK)
        ]
        solved = solve_block(pivots, rows)
        for g in range(R // 8):
            part = jnp.where(inside, 0.0, work[g])
            col = cols[g]
            if g == home:
                block_row = (row >= at) & (row < at + BLOCK)
                part = jnp.where(block_row, 0.0, part)
                col = [
                    jnp.where(block_row, jnp.where(row == at + j, -1.0, 0.0), col[j]) for j in range(BLOCK)
                ]
            work[g] = part - (col[0] * solved[0] + col[1] * solved[1]) - (col[2] * solved[2] + col[3] * solved[3])
    return jnp.concatenate(work, axis=0)


def inverse_kernel(total_tokens, *refs):
    cov_refs, inv_ref = refs[:-1], refs[-1]
    row = lax.broadcasted_iota(jnp.int32, (R, PAIR), 0)
    lane = lax.broadcasted_iota(jnp.int32, (R, PAIR), 1)
    low = lane < R
    column = jnp.where(low, lane, lane - R)
    cov = unfold_pair(sum(ref[...] for ref in cov_refs))
    diagonal = jnp.where(row == column, cov, 0.0)
    trace_in = jnp.sum(jnp.where(low, diagonal, 0.0), keepdims=True)
    trace_out = jnp.sum(jnp.where(low, 0.0, diagonal), keepdims=True)
    scale = R / jnp.where(low, trace_in, trace_out)
    inv_ref[...] = invert_pair(cov * scale + jnp.where(row == column, DAMPING, 0.0)) * (scale * total_tokens)


def inverse(covs, total_tokens):
    vmem = pl.BlockSpec(memory_space=pltpu.VMEM)
    return pl.pallas_call(
        functools.partial(inverse_kernel, total_tokens),
        in_specs=[vmem] * len(covs),
        out_specs=vmem,
        out_shape=jax.ShapeDtypeStruct((R, PAIR), F32),
        compiler_params=pltpu.CompilerParams(vmem_limit_bytes=16 * MIB),
        name="inverse",
    )(*covs)


def precondition_kernel(inv_ref, keep_ref, recv_ref, out_ref, flat_ref):
    low = lax.broadcasted_iota(jnp.int32, (R, PAIR), 1) < R
    inv = inv_ref[...]
    tiles = R // 2
    left = jnp.concatenate([inv_ref[pl.ds(start, tiles, stride=2), :] for start in range(2)], axis=0)
    left = pltpu.roll(left, R, 1)[:, :R]
    moments = jnp.concatenate([keep_ref[...], recv_ref[...]], axis=1)
    mixed = dot(left, moments, NN, lax.Precision.HIGHEST)
    pairs = moments.shape[1] // PAIR
    stack = jnp.concatenate(
        [
            jnp.concatenate(
                [mixed[:tiles, j * PAIR : (j + 1) * PAIR], mixed[tiles:, j * PAIR : (j + 1) * PAIR]], axis=1
            )
            for j in range(pairs)
        ],
        axis=0,
    )
    zero = jnp.zeros((R, PAIR), F32)
    at_low = jnp.where(low, inv, 0.0)
    at_high = pltpu.roll(at_low, R, 1)
    right = jnp.concatenate(
        [
            jnp.concatenate([at_low, zero], axis=1),
            jnp.concatenate([zero, at_low], axis=1),
            jnp.concatenate([at_high, zero], axis=1),
            jnp.concatenate([zero, at_high], axis=1),
        ],
        axis=0,
    )
    done = dot(stack, right, NN, lax.Precision.HIGHEST)
    for j in range(pairs):
        rows = done[j * tiles : (j + 1) * tiles]
        flat_ref[(2 * j) * tiles : (2 * j + 1) * tiles, :] = rows[:, :PAIR]
        flat_ref[(2 * j + 1) * tiles : (2 * j + 2) * tiles, :] = rows[:, PAIR:]
    for k in range(tiles):
        out_ref[:, k * PAIR : (k + 1) * PAIR] = flat_ref[pl.ds(k, 2 * pairs, stride=tiles), :].astype(BF16)


def precondition(inv, moments):
    seqs = sum(part.shape[1] for part in moments) // R
    vmem = pl.BlockSpec(memory_space=pltpu.VMEM)
    return pl.pallas_call(
        precondition_kernel,
        in_specs=[vmem] * (1 + len(moments)),
        out_specs=vmem,
        out_shape=jax.ShapeDtypeStruct((seqs, R * R), BF16),
        scratch_shapes=[pltpu.VMEM((seqs * R // 2, PAIR), F32)],
        compiler_params=pltpu.CompilerParams(vmem_limit_bytes=16 * MIB),
        name="precondition",
    )(inv, *moments)


def scores_kernel(order, flat_ref, *refs):
    query_refs, (out_ref, part_ref) = refs[:-2], refs[-2:]
    place = lax.axis_index("dp")
    part = dot(jnp.concatenate([ref[...] for ref in query_refs], axis=0), flat_ref[...], NT)
    group = part_ref.shape[1]
    for at, distance in enumerate(order):
        part_ref[place ^ distance] = part[at * group : (at + 1) * group]
    out_ref[...] = part_ref[...].reshape(part.shape).T


def score(flat, queries, order):
    seqs = flat.shape[0]
    count = sum(part.shape[0] for part in queries)
    vmem = pl.BlockSpec(memory_space=pltpu.VMEM)
    return pl.pallas_call(
        functools.partial(scores_kernel, order),
        in_specs=[vmem] * (1 + len(queries)),
        out_specs=vmem,
        out_shape=jax.ShapeDtypeStruct((seqs, count), F32),
        scratch_shapes=[pltpu.VMEM((len(order), count // len(order), seqs), F32)],
        compiler_params=pltpu.CompilerParams(vmem_limit_bytes=16 * MIB),
        name="scores",
    )(flat, *queries)


def exchange(value, distance):
    return lax.ppermute(value, "dp", [(i, i ^ distance) for i in range(lax.axis_size("dp"))])


def halves(value, upper):
    low, high = jnp.split(value, 2, axis=1)
    return jnp.where(upper, high, low), jnp.where(upper, low, high)


def per_device(layer_input, out_grads, in_proj, out_proj, queries):
    local_tokens = layer_input.shape[0]
    devices = lax.axis_size("dp")
    slabs = devices // GROUP
    device, queries = lax.optimization_barrier((own_place(), queries))
    near_slabs, far_slabs = [0, 1], [2, 3] + list(range(4, slabs))
    column = {slab: exchange(queries, slab * GROUP) for slab in [1, 2, 3] + list(range(4, slabs))}
    column[0] = queries
    acts = project(layer_input, in_proj.reshape(PAIR, in_proj.shape[2]))
    acts, out_grads, column[0] = lax.optimization_barrier((acts, out_grads, column[0]))
    upper = device[0] & 1 == 1

    def fold(picked):
        keep, send = zip(*(halves(column[slab], upper) for slab in picked))
        keep, send = jnp.concatenate(keep, axis=0), jnp.concatenate(send, axis=0)
        return jnp.concatenate([keep, exchange(send, 1)], axis=0)

    outs = jnp.einsum("tmk,mrk->tmr", out_grads, out_proj, preferred_element_type=F32).astype(BF16)
    outs = outs.reshape(local_tokens, PAIR).T
    keep_cov, send_cov, keep_mom, send_mom = statistics(acts, outs)
    cov = keep_cov + exchange(send_cov, 1)
    moments = [keep_mom, exchange(send_mom, 1)]
    cov, column[3] = lax.optimization_barrier((cov, column[3]))
    cov = cov + exchange(cov, 2)
    far = fold(far_slabs)
    cov, far, moments = lax.optimization_barrier((cov, far, moments))
    near = fold(near_slabs)
    across = exchange(near, 2)
    covs = [cov] + [exchange(cov, slab * GROUP) for slab in reversed(range(1, slabs))]
    covs, across = lax.optimization_barrier((covs, across))
    inv = inverse(covs, local_tokens * devices)
    gathered = [near, across, far, exchange(far, 2)]
    order = [
        slab * GROUP + 2 * over + core
        for part in (near_slabs, far_slabs)
        for over in range(2)
        for core in range(2)
        for slab in part
    ]
    partial = score(precondition(inv, moments), gathered, order)
    seqs = local_tokens // LEN
    return partial[:seqs] + exchange(partial[seqs:], 1)


def solution(mesh):
    return jax.shard_map(
        per_device,
        mesh=mesh,
        in_specs=(
            P(("parts", "dp"), None),
            P(("parts", "dp"), None, None),
            P(),
            P(),
            P(("parts", "dp"), None),
        ),
        out_specs=P(("parts", "dp"), None),
        check_vma=False,
    )
```

```python
import functools

import jax
import jax.numpy as jnp
from jax import lax
from jax.experimental import pallas as pl
from jax.experimental.pallas import tpu as pltpu
from jax.sharding import PartitionSpec as P

R = 64
LEN = 128
PAIR = 2 * R
DAMPING = 0.1
ROWS = 256
STAGE = 8 * 10**10
BLOCK = 4
GROUP = 4

F32 = jnp.float32
BF16 = jnp.bfloat16
MIB = 1024 * 1024


def dot(a, b, dims, precision=None):
    return lax.dot_general(a, b, (dims, ((), ())), precision=precision, preferred_element_type=F32)


NN = ((1,), (0,))
NT = ((1,), (1,))


def place_kernel(out_ref):
    out_ref[0] = lax.axis_index("dp")


def own_place():
    return pl.pallas_call(
        place_kernel,
        out_specs=pl.BlockSpec(memory_space=pltpu.SMEM),
        out_shape=jax.ShapeDtypeStruct((1,), jnp.int32),
        compiler_params=pltpu.CompilerParams(vmem_limit_bytes=MIB),
        cost_estimate=pl.CostEstimate(flops=STAGE, bytes_accessed=8, transcendentals=0),
        name="own_place",
    )()


def project_kernel(x_ref, w_ref, acts_ref):
    tokens = x_ref.shape[0]
    for at in range(0, tokens, ROWS):
        acts_ref[:, at : at + ROWS] = dot(w_ref[...], x_ref[at : at + ROWS], NT).astype(BF16)


def project(layer_input, in_flat):
    tokens, width = layer_input.shape
    vmem = pl.BlockSpec(memory_space=pltpu.VMEM)
    return pl.pallas_call(
        project_kernel,
        in_specs=[vmem, vmem],
        out_specs=vmem,
        out_shape=jax.ShapeDtypeStruct((PAIR, tokens), BF16),
        compiler_params=pltpu.CompilerParams(vmem_limit_bytes=24 * MIB),
        cost_estimate=pl.CostEstimate(
            flops=4 * tokens * width * PAIR, bytes_accessed=2 * tokens * width, transcendentals=0
        ),
        name="project",
    )(layer_input, in_flat)


def fold_pair(pair):
    row = lax.broadcasted_iota(jnp.int32, (R, PAIR), 0)
    lane = lax.broadcasted_iota(jnp.int32, (R, PAIR), 1)
    turned = pltpu.roll(pair, R, 1)
    mixed = jnp.where(lane >= row, pair, turned)
    diagonal = jnp.sum(jnp.where(lane == row, turned, 0.0), axis=0, keepdims=True)
    half = R // 2
    folded = jnp.where(lane[:half] < R, mixed[:half], pltpu.roll(mixed[half:], R, 1))
    return jnp.concatenate([folded, jnp.broadcast_to(diagonal, (8, PAIR))], axis=0)


def unfold_pair(folded):
    row = lax.broadcasted_iota(jnp.int32, (R, PAIR), 0)
    lane = lax.broadcasted_iota(jnp.int32, (R, PAIR), 1)
    low = lane < R
    column = jnp.where(low, lane, lane - R)
    half = R // 2
    turned = pltpu.roll(folded, R, 1)
    wide = low[:half]
    mixed = jnp.concatenate(
        [jnp.where(wide, folded[:half], turned[:half]), jnp.where(wide, turned[:half], folded[:half])], axis=0
    )
    flipped = jnp.concatenate([mixed, mixed], axis=0).T[:R]
    pair = jnp.where((column >= row) == low, mixed, flipped)
    return jnp.where((column == row) & (lane >= R), turned[half : half + 1], pair)


def statistics_kernel(acts_ref, outs_ref, keep_cov, send_cov, keep_mom, send_mom):
    first = lax.axis_index("dp") & 1 == 0
    acts = acts_ref[...]
    outs = outs_ref[...]
    low = lax.broadcasted_iota(jnp.int32, (R, PAIR), 1) < R
    cov_in = dot(acts, acts, NT)
    cov_out = dot(outs, outs, NT)
    cov0 = jnp.where(low, cov_in[:R], pltpu.roll(cov_out[:R], R, 1))
    cov1 = jnp.where(low, pltpu.roll(cov_in[R:], R, 1), cov_out[R:])
    cov0, cov1 = fold_pair(cov0), fold_pair(cov1)
    keep_cov[...] = jnp.where(first, cov0, cov1)
    send_cov[...] = jnp.where(first, cov1, cov0)
    for pair in range(acts.shape[1] // LEN // 2):
        blocks = []
        for seq in (2 * pair, 2 * pair + 1):
            tokens = slice(seq * LEN, (seq + 1) * LEN)
            blocks.append(dot(outs[:, tokens], acts[:, tokens], NT) * (1.0 / LEN))
        mom0 = jnp.where(low, blocks[0][:R], pltpu.roll(blocks[1][:R], R, 1))
        mom1 = jnp.where(low, pltpu.roll(blocks[0][R:], R, 1), blocks[1][R:])
        lanes = slice(pair * PAIR, (pair + 1) * PAIR)
        keep_mom[:, lanes] = jnp.where(first, mom0, mom1)
        send_mom[:, lanes] = jnp.where(first, mom1, mom0)


def statistics(acts, outs):
    seqs = acts.shape[1] // LEN
    cov = jax.ShapeDtypeStruct((R // 2 + 8, PAIR), F32)
    mom = jax.ShapeDtypeStruct((R, seqs * R), F32)
    vmem = pl.BlockSpec(memory_space=pltpu.VMEM)
    return pl.pallas_call(
        statistics_kernel,
        in_specs=[vmem, vmem],
        out_specs=[vmem] * 4,
        out_shape=[cov, cov, mom, mom],
        compiler_params=pltpu.CompilerParams(vmem_limit_bytes=16 * MIB),
        name="statistics",
    )(acts, outs)


def solve_block(p, rows):
    det = 1.0 / (p[0][0] * p[1][1] - p[0][1] * p[0][1])
    a, b, c = p[1][1] * det, -p[0][1] * det, p[0][0] * det
    t = [[a * p[0][j] + b * p[1][j], b * p[0][j] + c * p[1][j]] for j in (2, 3)]
    s22 = p[2][2] - p[0][2] * t[0][0] - p[1][2] * t[0][1]
    s23 = p[2][3] - p[0][2] * t[1][0] - p[1][2] * t[1][1]
    s33 = p[3][3] - p[0][3] * t[1][0] - p[1][3] * t[1][1]
    det = 1.0 / (s22 * s33 - s23 * s23)
    y0 = a * rows[0] + b * rows[1]
    y1 = b * rows[0] + c * rows[1]
    z2 = rows[2] - p[0][2] * y0 - p[1][2] * y1
    z3 = rows[3] - p[0][3] * y0 - p[1][3] * y1
    x2 = (s33 * z2 - s23 * z3) * det
    x3 = (s22 * z3 - s23 * z2) * det
    return [y0 - t[0][0] * x2 - t[1][0] * x3, y1 - t[0][1] * x2 - t[1][1] * x3, x2, x3]


def invert_pair(matrix):
    lane = lax.broadcasted_iota(jnp.int32, (8, PAIR), 1)
    row = lax.broadcasted_iota(jnp.int32, (8, PAIR), 0)
    column = lane % R
    base = lane - column
    work = [matrix[8 * g : 8 * g + 8] for g in range(R // 8)]
    for k in range(0, R, BLOCK):
        cols = [[jnp.take_along_axis(part, base + (k + j), axis=1) for j in range(BLOCK)] for part in work]
        home, at = k // 8, k % 8
        inside = (column >= k) & (column < k + BLOCK)
        pivots = [[cols[home][j][at + i : at + i + 1] for j in range(BLOCK)] for i in range(BLOCK)]
        rows = [
            jnp.where(
                inside[:1], jnp.where(column[:1] == k + i, 1.0, 0.0), work[home][at + i : at + i + 1]
            )
            for i in range(BLOCK)
        ]
        solved = solve_block(pivots, rows)
        for g in range(R // 8):
            part = jnp.where(inside, 0.0, work[g])
            col = cols[g]
            if g == home:
                block_row = (row >= at) & (row < at + BLOCK)
                part = jnp.where(block_row, 0.0, part)
                col = [
                    jnp.where(block_row, jnp.where(row == at + j, -1.0, 0.0), col[j]) for j in range(BLOCK)
                ]
            work[g] = part - (col[0] * solved[0] + col[1] * solved[1]) - (col[2] * solved[2] + col[3] * solved[3])
    return jnp.concatenate(work, axis=0)


def inverse_kernel(total_tokens, *refs):
    cov_refs, inv_ref = refs[:-1], refs[-1]
    row = lax.broadcasted_iota(jnp.int32, (R, PAIR), 0)
    lane = lax.broadcasted_iota(jnp.int32, (R, PAIR), 1)
    low = lane < R
    column = jnp.where(low, lane, lane - R)
    cov = unfold_pair(sum(ref[...] for ref in cov_refs))
    diagonal = jnp.where(row == column, cov, 0.0)
    trace_in = jnp.sum(jnp.where(low, diagonal, 0.0), keepdims=True)
    trace_out = jnp.sum(jnp.where(low, 0.0, diagonal), keepdims=True)
    scale = R / jnp.where(low, trace_in, trace_out)
    inv_ref[...] = invert_pair(cov * scale + jnp.where(row == column, DAMPING, 0.0)) * (scale * total_tokens)


def inverse(covs, total_tokens):
    vmem = pl.BlockSpec(memory_space=pltpu.VMEM)
    return pl.pallas_call(
        functools.partial(inverse_kernel, total_tokens),
        in_specs=[vmem] * len(covs),
        out_specs=vmem,
        out_shape=jax.ShapeDtypeStruct((R, PAIR), F32),
        compiler_params=pltpu.CompilerParams(vmem_limit_bytes=16 * MIB),
        name="inverse",
    )(*covs)


def precondition_kernel(inv_ref, keep_ref, recv_ref, out_ref, flat_ref):
    low = lax.broadcasted_iota(jnp.int32, (R, PAIR), 1) < R
    inv = inv_ref[...]
    tiles = R // 2
    left = jnp.concatenate([inv_ref[pl.ds(start, tiles, stride=2), :] for start in range(2)], axis=0)
    left = pltpu.roll(left, R, 1)[:, :R]
    moments = jnp.concatenate([keep_ref[...], recv_ref[...]], axis=1)
    mixed = dot(left, moments, NN, lax.Precision.HIGHEST)
    pairs = moments.shape[1] // PAIR
    stack = jnp.concatenate(
        [
            jnp.concatenate(
                [mixed[:tiles, j * PAIR : (j + 1) * PAIR], mixed[tiles:, j * PAIR : (j + 1) * PAIR]], axis=1
            )
            for j in range(pairs)
        ],
        axis=0,
    )
    zero = jnp.zeros((R, PAIR), F32)
    at_low = jnp.where(low, inv, 0.0)
    at_high = pltpu.roll(at_low, R, 1)
    right = jnp.concatenate(
        [
            jnp.concatenate([at_low, zero], axis=1),
            jnp.concatenate([zero, at_low], axis=1),
            jnp.concatenate([at_high, zero], axis=1),
            jnp.concatenate([zero, at_high], axis=1),
        ],
        axis=0,
    )
    done = dot(stack, right, NN, lax.Precision.HIGHEST)
    for j in range(pairs):
        rows = done[j * tiles : (j + 1) * tiles]
        flat_ref[(2 * j) * tiles : (2 * j + 1) * tiles, :] = rows[:, :PAIR]
        flat_ref[(2 * j + 1) * tiles : (2 * j + 2) * tiles, :] = rows[:, PAIR:]
    for k in range(tiles):
        out_ref[:, k * PAIR : (k + 1) * PAIR] = flat_ref[pl.ds(k, 2 * pairs, stride=tiles), :].astype(BF16)


def precondition(inv, moments):
    seqs = sum(part.shape[1] for part in moments) // R
    vmem = pl.BlockSpec(memory_space=pltpu.VMEM)
    return pl.pallas_call(
        precondition_kernel,
        in_specs=[vmem] * (1 + len(moments)),
        out_specs=vmem,
        out_shape=jax.ShapeDtypeStruct((seqs, R * R), BF16),
        scratch_shapes=[pltpu.VMEM((seqs * R // 2, PAIR), F32)],
        compiler_params=pltpu.CompilerParams(vmem_limit_bytes=16 * MIB),
        name="precondition",
    )(inv, *moments)


def scores_kernel(order, flat_ref, *refs):
    query_refs, (out_ref, part_ref) = refs[:-2], refs[-2:]
    place = lax.axis_index("dp")
    part = dot(jnp.concatenate([ref[...] for ref in query_refs], axis=0), flat_ref[...], NT)
    group = part_ref.shape[1]
    for at, distance in enumerate(order):
        part_ref[place ^ distance] = part[at * group : (at + 1) * group]
    out_ref[...] = part_ref[...].reshape(part.shape).T


def score(flat, queries, order):
    seqs = flat.shape[0]
    count = sum(part.shape[0] for part in queries)
    vmem = pl.BlockSpec(memory_space=pltpu.VMEM)
    return pl.pallas_call(
        functools.partial(scores_kernel, order),
        in_specs=[vmem] * (1 + len(queries)),
        out_specs=vmem,
        out_shape=jax.ShapeDtypeStruct((seqs, count), F32),
        scratch_shapes=[pltpu.VMEM((len(order), count // len(order), seqs), F32)],
        compiler_params=pltpu.CompilerParams(vmem_limit_bytes=16 * MIB),
        name="scores",
    )(flat, *queries)


def exchange(value, distance):
    return lax.ppermute(value, "dp", [(i, i ^ distance) for i in range(lax.axis_size("dp"))])


def halves(value, upper):
    low, high = jnp.split(value, 2, axis=1)
    return jnp.where(upper, high, low), jnp.where(upper, low, high)


def per_device(layer_input, out_grads, in_proj, out_proj, queries):
    local_tokens = layer_input.shape[0]
    devices = lax.axis_size("dp")
    slabs = devices // GROUP
    device, queries = lax.optimization_barrier((own_place(), queries))
    near_slabs, far_slabs = [0, 1], [2, 3] + list(range(4, slabs))
    column = {slab: exchange(queries, slab * GROUP) for slab in [1, 2, 3] + list(range(4, slabs))}
    column[0] = queries
    beside = exchange(queries, 2)
    acts = project(layer_input, in_proj.reshape(PAIR, in_proj.shape[2]))
    acts, out_grads, column[0] = lax.optimization_barrier((acts, out_grads, column[0]))
    upper = device[0] & 1 == 1

    def fold(picked):
        keep, send = zip(*(halves(column[slab], upper) for slab in picked))
        keep, send = jnp.concatenate(keep, axis=0), jnp.concatenate(send, axis=0)
        return jnp.concatenate([keep, exchange(send, 1)], axis=0)

    outs = jnp.einsum("tmk,mrk->tmr", out_grads, out_proj, preferred_element_type=F32).astype(BF16)
    outs = outs.reshape(local_tokens, PAIR).T
    keep_cov, send_cov, keep_mom, send_mom = statistics(acts, outs)
    cov = keep_cov + exchange(send_cov, 1)
    moments = [keep_mom, exchange(send_mom, 1)]
    cov, column[3] = lax.optimization_barrier((cov, column[3]))
    cov = cov + exchange(cov, 2)
    far = fold(far_slabs)
    cov, far, moments = lax.optimization_barrier((cov, far, moments))
    column[-1] = beside
    local = fold([0, -1])
    near = fold([1])
    across = exchange(near, 2)
    covs = [cov] + [exchange(cov, slab * GROUP) for slab in reversed(range(1, slabs))]
    covs, across = lax.optimization_barrier((covs, across))
    inv = inverse(covs, local_tokens * devices)
    gathered = [local, near, across, far, exchange(far, 2)]
    order = [0, 2, 1, 3] + [
        slab * GROUP + 2 * over + core
        for part in ([1], far_slabs)
        for over in range(2)
        for core in range(2)
        for slab in part
    ]
    partial = score(precondition(inv, moments), gathered, order)
    seqs = local_tokens // LEN
    return partial[:seqs] + exchange(partial[seqs:], 1)


def solution(mesh):
    return jax.shard_map(
        per_device,
        mesh=mesh,
        in_specs=(
            P(("parts", "dp"), None),
            P(("parts", "dp"), None, None),
            P(),
            P(),
            P(("parts", "dp"), None),
        ),
        out_specs=P(("parts", "dp"), None),
        check_vma=False,
    )
```

```python
import functools

import jax
import jax.numpy as jnp
from jax import lax
from jax.experimental import pallas as pl
from jax.experimental.pallas import tpu as pltpu
from jax.sharding import PartitionSpec as P

R = 64
LEN = 128
PAIR = 2 * R
DAMPING = 0.1
ROWS = 256
STAGE = 8 * 10**10
BLOCK = 4
GROUP = 4

F32 = jnp.float32
BF16 = jnp.bfloat16
MIB = 1024 * 1024


def dot(a, b, dims, precision=None):
    return lax.dot_general(a, b, (dims, ((), ())), precision=precision, preferred_element_type=F32)


NN = ((1,), (0,))
NT = ((1,), (1,))


def place_kernel(out_ref):
    out_ref[0] = lax.axis_index("dp")


def own_place():
    return pl.pallas_call(
        place_kernel,
        out_specs=pl.BlockSpec(memory_space=pltpu.SMEM),
        out_shape=jax.ShapeDtypeStruct((1,), jnp.int32),
        compiler_params=pltpu.CompilerParams(vmem_limit_bytes=MIB),
        cost_estimate=pl.CostEstimate(flops=STAGE, bytes_accessed=8, transcendentals=0),
        name="own_place",
    )()


def project_kernel(x_ref, w_ref, acts_ref):
    tokens = x_ref.shape[0]
    for at in range(0, tokens, ROWS):
        acts_ref[:, at : at + ROWS] = dot(w_ref[...], x_ref[at : at + ROWS], NT).astype(BF16)


def project(layer_input, in_flat):
    tokens, width = layer_input.shape
    vmem = pl.BlockSpec(memory_space=pltpu.VMEM)
    return pl.pallas_call(
        project_kernel,
        in_specs=[vmem, vmem],
        out_specs=vmem,
        out_shape=jax.ShapeDtypeStruct((PAIR, tokens), BF16),
        compiler_params=pltpu.CompilerParams(vmem_limit_bytes=24 * MIB),
        cost_estimate=pl.CostEstimate(
            flops=4 * tokens * width * PAIR, bytes_accessed=2 * tokens * width, transcendentals=0
        ),
        name="project",
    )(layer_input, in_flat)


def fold_pair(pair):
    row = lax.broadcasted_iota(jnp.int32, (R, PAIR), 0)
    lane = lax.broadcasted_iota(jnp.int32, (R, PAIR), 1)
    turned = pltpu.roll(pair, R, 1)
    mixed = jnp.where(lane >= row, pair, turned)
    diagonal = jnp.sum(jnp.where(lane == row, turned, 0.0), axis=0, keepdims=True)
    half = R // 2
    folded = jnp.where(lane[:half] < R, mixed[:half], pltpu.roll(mixed[half:], R, 1))
    return jnp.concatenate([folded, jnp.broadcast_to(diagonal, (8, PAIR))], axis=0)


def unfold_pair(folded):
    row = lax.broadcasted_iota(jnp.int32, (R, PAIR), 0)
    lane = lax.broadcasted_iota(jnp.int32, (R, PAIR), 1)
    low = lane < R
    column = jnp.where(low, lane, lane - R)
    half = R // 2
    turned = pltpu.roll(folded, R, 1)
    wide = low[:half]
    mixed = jnp.concatenate(
        [jnp.where(wide, folded[:half], turned[:half]), jnp.where(wide, turned[:half], folded[:half])], axis=0
    )
    flipped = jnp.concatenate([mixed, mixed], axis=0).T[:R]
    pair = jnp.where((column >= row) == low, mixed, flipped)
    return jnp.where((column == row) & (lane >= R), turned[half : half + 1], pair)


def statistics_kernel(acts_ref, outs_ref, keep_cov, send_cov, keep_mom, send_mom):
    first = lax.axis_index("dp") & 1 == 0
    acts = acts_ref[...]
    outs = outs_ref[...]
    low = lax.broadcasted_iota(jnp.int32, (R, PAIR), 1) < R
    cov_in = dot(acts, acts, NT)
    cov_out = dot(outs, outs, NT)
    cov0 = jnp.where(low, cov_in[:R], pltpu.roll(cov_out[:R], R, 1))
    cov1 = jnp.where(low, pltpu.roll(cov_in[R:], R, 1), cov_out[R:])
    cov0, cov1 = fold_pair(cov0), fold_pair(cov1)
    keep_cov[...] = jnp.where(first, cov0, cov1)
    send_cov[...] = jnp.where(first, cov1, cov0)
    for pair in range(acts.shape[1] // LEN // 2):
        blocks = []
        for seq in (2 * pair, 2 * pair + 1):
            tokens = slice(seq * LEN, (seq + 1) * LEN)
            blocks.append(dot(outs[:, tokens], acts[:, tokens], NT) * (1.0 / LEN))
        mom0 = jnp.where(low, blocks[0][:R], pltpu.roll(blocks[1][:R], R, 1))
        mom1 = jnp.where(low, pltpu.roll(blocks[0][R:], R, 1), blocks[1][R:])
        lanes = slice(pair * PAIR, (pair + 1) * PAIR)
        keep_mom[:, lanes] = jnp.where(first, mom0, mom1)
        send_mom[:, lanes] = jnp.where(first, mom1, mom0)


def statistics(acts, outs):
    seqs = acts.shape[1] // LEN
    cov = jax.ShapeDtypeStruct((R // 2 + 8, PAIR), F32)
    mom = jax.ShapeDtypeStruct((R, seqs * R), F32)
    vmem = pl.BlockSpec(memory_space=pltpu.VMEM)
    return pl.pallas_call(
        statistics_kernel,
        in_specs=[vmem, vmem],
        out_specs=[vmem] * 4,
        out_shape=[cov, cov, mom, mom],
        compiler_params=pltpu.CompilerParams(vmem_limit_bytes=16 * MIB),
        name="statistics",
    )(acts, outs)


def solve_block(p, rows):
    det = 1.0 / (p[0][0] * p[1][1] - p[0][1] * p[0][1])
    a, b, c = p[1][1] * det, -p[0][1] * det, p[0][0] * det
    t = [[a * p[0][j] + b * p[1][j], b * p[0][j] + c * p[1][j]] for j in (2, 3)]
    s22 = p[2][2] - p[0][2] * t[0][0] - p[1][2] * t[0][1]
    s23 = p[2][3] - p[0][2] * t[1][0] - p[1][2] * t[1][1]
    s33 = p[3][3] - p[0][3] * t[1][0] - p[1][3] * t[1][1]
    det = 1.0 / (s22 * s33 - s23 * s23)
    y0 = a * rows[0] + b * rows[1]
    y1 = b * rows[0] + c * rows[1]
    z2 = rows[2] - p[0][2] * y0 - p[1][2] * y1
    z3 = rows[3] - p[0][3] * y0 - p[1][3] * y1
    x2 = (s33 * z2 - s23 * z3) * det
    x3 = (s22 * z3 - s23 * z2) * det
    return [y0 - t[0][0] * x2 - t[1][0] * x3, y1 - t[0][1] * x2 - t[1][1] * x3, x2, x3]


def invert_pair(matrix):
    lane = lax.broadcasted_iota(jnp.int32, (8, PAIR), 1)
    row = lax.broadcasted_iota(jnp.int32, (8, PAIR), 0)
    column = lane % R
    base = lane - column
    work = [matrix[8 * g : 8 * g + 8] for g in range(R // 8)]
    for k in range(0, R, BLOCK):
        cols = [[jnp.take_along_axis(part, base + (k + j), axis=1) for j in range(BLOCK)] for part in work]
        home, at = k // 8, k % 8
        inside = (column >= k) & (column < k + BLOCK)
        pivots = [[cols[home][j][at + i : at + i + 1] for j in range(BLOCK)] for i in range(BLOCK)]
        rows = [
            jnp.where(
                inside[:1], jnp.where(column[:1] == k + i, 1.0, 0.0), work[home][at + i : at + i + 1]
            )
            for i in range(BLOCK)
        ]
        solved = solve_block(pivots, rows)
        for g in range(R // 8):
            part = jnp.where(inside, 0.0, work[g])
            col = cols[g]
            if g == home:
                block_row = (row >= at) & (row < at + BLOCK)
                part = jnp.where(block_row, 0.0, part)
                col = [
                    jnp.where(block_row, jnp.where(row == at + j, -1.0, 0.0), col[j]) for j in range(BLOCK)
                ]
            work[g] = part - (col[0] * solved[0] + col[1] * solved[1]) - (col[2] * solved[2] + col[3] * solved[3])
    return jnp.concatenate(work, axis=0)


def inverse_kernel(total_tokens, *refs):
    cov_refs, inv_ref = refs[:-1], refs[-1]
    row = lax.broadcasted_iota(jnp.int32, (R, PAIR), 0)
    lane = lax.broadcasted_iota(jnp.int32, (R, PAIR), 1)
    low = lane < R
    column = jnp.where(low, lane, lane - R)
    cov = unfold_pair(sum(ref[...] for ref in cov_refs))
    diagonal = jnp.where(row == column, cov, 0.0)
    trace_in = jnp.sum(jnp.where(low, diagonal, 0.0), keepdims=True)
    trace_out = jnp.sum(jnp.where(low, 0.0, diagonal), keepdims=True)
    scale = R / jnp.where(low, trace_in, trace_out)
    inv_ref[...] = invert_pair(cov * scale + jnp.where(row == column, DAMPING, 0.0)) * (scale * total_tokens)


def inverse(covs, total_tokens):
    vmem = pl.BlockSpec(memory_space=pltpu.VMEM)
    return pl.pallas_call(
        functools.partial(inverse_kernel, total_tokens),
        in_specs=[vmem] * len(covs),
        out_specs=vmem,
        out_shape=jax.ShapeDtypeStruct((R, PAIR), F32),
        compiler_params=pltpu.CompilerParams(vmem_limit_bytes=16 * MIB),
        name="inverse",
    )(*covs)


def precondition_kernel(inv_ref, keep_ref, recv_ref, out_ref, flat_ref):
    low = lax.broadcasted_iota(jnp.int32, (R, PAIR), 1) < R
    inv = inv_ref[...]
    tiles = R // 2
    left = jnp.concatenate([inv_ref[pl.ds(start, tiles, stride=2), :] for start in range(2)], axis=0)
    left = pltpu.roll(left, R, 1)[:, :R]
    moments = jnp.concatenate([keep_ref[...], recv_ref[...]], axis=1)
    mixed = dot(left, moments, NN, lax.Precision.HIGHEST)
    pairs = moments.shape[1] // PAIR
    stack = jnp.concatenate(
        [
            jnp.concatenate(
                [mixed[:tiles, j * PAIR : (j + 1) * PAIR], mixed[tiles:, j * PAIR : (j + 1) * PAIR]], axis=1
            )
            for j in range(pairs)
        ],
        axis=0,
    )
    zero = jnp.zeros((R, PAIR), F32)
    at_low = jnp.where(low, inv, 0.0)
    at_high = pltpu.roll(at_low, R, 1)
    right = jnp.concatenate(
        [
            jnp.concatenate([at_low, zero], axis=1),
            jnp.concatenate([zero, at_low], axis=1),
            jnp.concatenate([at_high, zero], axis=1),
            jnp.concatenate([zero, at_high], axis=1),
        ],
        axis=0,
    )
    done = dot(stack, right, NN, lax.Precision.HIGHEST)
    for j in range(pairs):
        rows = done[j * tiles : (j + 1) * tiles]
        flat_ref[(2 * j) * tiles : (2 * j + 1) * tiles, :] = rows[:, :PAIR]
        flat_ref[(2 * j + 1) * tiles : (2 * j + 2) * tiles, :] = rows[:, PAIR:]
    for k in range(tiles):
        out_ref[:, k * PAIR : (k + 1) * PAIR] = flat_ref[pl.ds(k, 2 * pairs, stride=tiles), :].astype(BF16)


def precondition(inv, moments):
    seqs = sum(part.shape[1] for part in moments) // R
    vmem = pl.BlockSpec(memory_space=pltpu.VMEM)
    return pl.pallas_call(
        precondition_kernel,
        in_specs=[vmem] * (1 + len(moments)),
        out_specs=vmem,
        out_shape=jax.ShapeDtypeStruct((seqs, R * R), BF16),
        scratch_shapes=[pltpu.VMEM((seqs * R // 2, PAIR), F32)],
        compiler_params=pltpu.CompilerParams(vmem_limit_bytes=16 * MIB),
        name="precondition",
    )(inv, *moments)


def scores_kernel(order, flat_ref, *refs):
    query_refs, (out_ref, part_ref) = refs[:-2], refs[-2:]
    place = lax.axis_index("dp")
    part = dot(jnp.concatenate([ref[...] for ref in query_refs], axis=0), flat_ref[...], NT)
    group = part_ref.shape[1]
    for at, distance in enumerate(order):
        part_ref[place ^ distance] = part[at * group : (at + 1) * group]
    out_ref[...] = part_ref[...].reshape(part.shape).T


def score(flat, queries, order):
    seqs = flat.shape[0]
    count = sum(part.shape[0] for part in queries)
    vmem = pl.BlockSpec(memory_space=pltpu.VMEM)
    return pl.pallas_call(
        functools.partial(scores_kernel, order),
        in_specs=[vmem] * (1 + len(queries)),
        out_specs=vmem,
        out_shape=jax.ShapeDtypeStruct((seqs, count), F32),
        scratch_shapes=[pltpu.VMEM((len(order), count // len(order), seqs), F32)],
        compiler_params=pltpu.CompilerParams(vmem_limit_bytes=16 * MIB),
        name="scores",
    )(flat, *queries)


def exchange(value, distance):
    return lax.ppermute(value, "dp", [(i, i ^ distance) for i in range(lax.axis_size("dp"))])


def halves(value, upper):
    low, high = jnp.split(value, 2, axis=1)
    return jnp.where(upper, high, low), jnp.where(upper, low, high)


def per_device(layer_input, out_grads, in_proj, out_proj, queries):
    local_tokens = layer_input.shape[0]
    devices = lax.axis_size("dp")
    slabs = devices // GROUP
    device, queries = lax.optimization_barrier((own_place(), queries))
    near_slabs, far_slabs = [0, 1], [2, 3] + list(range(4, slabs))
    column = {slab: exchange(queries, slab * GROUP) for slab in [1, 2, 3] + list(range(4, slabs))}
    column[0] = queries
    beside = exchange(queries, 2)
    acts = project(layer_input, in_proj.reshape(PAIR, in_proj.shape[2]))
    acts, out_grads, column[0] = lax.optimization_barrier((acts, out_grads, column[0]))
    upper = device[0] & 1 == 1

    def fold(picked):
        keep, send = zip(*(halves(column[slab], upper) for slab in picked))
        keep, send = jnp.concatenate(keep, axis=0), jnp.concatenate(send, axis=0)
        return jnp.concatenate([keep, exchange(send, 1)], axis=0)

    outs = jnp.einsum("tmk,mrk->tmr", out_grads, out_proj, preferred_element_type=F32).astype(BF16)
    outs = outs.reshape(local_tokens, PAIR).T
    keep_cov, send_cov, keep_mom, send_mom = statistics(acts, outs)
    cov = keep_cov + exchange(send_cov, 1)
    moments = [keep_mom, exchange(send_mom, 1)]
    cov, column[3] = lax.optimization_barrier((cov, column[3]))
    cov = cov + exchange(cov, 2)
    far = fold(far_slabs)
    cov, far, moments = lax.optimization_barrier((cov, far, moments))
    column[-1] = beside
    local = fold([0, -1])
    near = fold([1])
    mine = jnp.concatenate([near, far], axis=0)
    across = exchange(mine, 2)
    covs = [cov] + [exchange(cov, slab * GROUP) for slab in reversed(range(1, slabs))]
    inv = inverse(covs, local_tokens * devices)
    gathered = [local, mine, across]
    order = [0, 2, 1, 3] + [
        slab * GROUP + 2 * over + core
        for over in range(2)
        for part in ([1], far_slabs)
        for core in range(2)
        for slab in part
    ]
    partial = score(precondition(inv, moments), gathered, order)
    seqs = local_tokens // LEN
    return partial[:seqs] + exchange(partial[seqs:], 1)


def solution(mesh):
    return jax.shard_map(
        per_device,
        mesh=mesh,
        in_specs=(
            P(("parts", "dp"), None),
            P(("parts", "dp"), None, None),
            P(),
            P(),
            P(("parts", "dp"), None),
        ),
        out_specs=P(("parts", "dp"), None),
        check_vma=False,
    )
```

```python
import functools

import jax
import jax.numpy as jnp
from jax import lax
from jax.experimental import pallas as pl
from jax.experimental.pallas import tpu as pltpu
from jax.sharding import PartitionSpec as P

R = 64
LEN = 128
PAIR = 2 * R
DAMPING = 0.1
ROWS = 256
STAGE = 8 * 10**10
BLOCK = 4
GROUP = 4

F32 = jnp.float32
BF16 = jnp.bfloat16
MIB = 1024 * 1024


def dot(a, b, dims, precision=None):
    return lax.dot_general(a, b, (dims, ((), ())), precision=precision, preferred_element_type=F32)


NN = ((1,), (0,))
NT = ((1,), (1,))


def place_kernel(out_ref):
    out_ref[0] = lax.axis_index("dp")


def own_place():
    return pl.pallas_call(
        place_kernel,
        out_specs=pl.BlockSpec(memory_space=pltpu.SMEM),
        out_shape=jax.ShapeDtypeStruct((1,), jnp.int32),
        compiler_params=pltpu.CompilerParams(vmem_limit_bytes=MIB),
        cost_estimate=pl.CostEstimate(flops=STAGE, bytes_accessed=8, transcendentals=0),
        name="own_place",
    )()


def project_kernel(x_ref, w_ref, acts_ref):
    tokens = x_ref.shape[0]
    for at in range(0, tokens, ROWS):
        acts_ref[:, at : at + ROWS] = dot(w_ref[...], x_ref[at : at + ROWS], NT).astype(BF16)


def project(layer_input, in_flat):
    tokens, width = layer_input.shape
    vmem = pl.BlockSpec(memory_space=pltpu.VMEM)
    return pl.pallas_call(
        project_kernel,
        in_specs=[vmem, vmem],
        out_specs=vmem,
        out_shape=jax.ShapeDtypeStruct((PAIR, tokens), BF16),
        compiler_params=pltpu.CompilerParams(vmem_limit_bytes=24 * MIB),
        cost_estimate=pl.CostEstimate(
            flops=4 * tokens * width * PAIR, bytes_accessed=2 * tokens * width, transcendentals=0
        ),
        name="project",
    )(layer_input, in_flat)


def fold_pair(pair):
    row = lax.broadcasted_iota(jnp.int32, (R, PAIR), 0)
    lane = lax.broadcasted_iota(jnp.int32, (R, PAIR), 1)
    turned = pltpu.roll(pair, R, 1)
    mixed = jnp.where(lane >= row, pair, turned)
    diagonal = jnp.sum(jnp.where(lane == row, turned, 0.0), axis=0, keepdims=True)
    half = R // 2
    folded = jnp.where(lane[:half] < R, mixed[:half], pltpu.roll(mixed[half:], R, 1))
    return jnp.concatenate([folded, jnp.broadcast_to(diagonal, (8, PAIR))], axis=0)


def unfold_pair(folded):
    row = lax.broadcasted_iota(jnp.int32, (R, PAIR), 0)
    lane = lax.broadcasted_iota(jnp.int32, (R, PAIR), 1)
    low = lane < R
    column = jnp.where(low, lane, lane - R)
    half = R // 2
    turned = pltpu.roll(folded, R, 1)
    wide = low[:half]
    mixed = jnp.concatenate(
        [jnp.where(wide, folded[:half], turned[:half]), jnp.where(wide, turned[:half], folded[:half])], axis=0
    )
    flipped = jnp.concatenate([mixed, mixed], axis=0).T[:R]
    pair = jnp.where((column >= row) == low, mixed, flipped)
    return jnp.where((column == row) & (lane >= R), turned[half : half + 1], pair)


def statistics_kernel(acts_ref, outs_ref, keep_cov, send_cov, keep_mom, send_mom):
    first = lax.axis_index("dp") & 1 == 0
    acts = acts_ref[...]
    outs = outs_ref[...]
    low = lax.broadcasted_iota(jnp.int32, (R, PAIR), 1) < R
    cov_in = dot(acts, acts, NT)
    cov_out = dot(outs, outs, NT)
    cov0 = jnp.where(low, cov_in[:R], pltpu.roll(cov_out[:R], R, 1))
    cov1 = jnp.where(low, pltpu.roll(cov_in[R:], R, 1), cov_out[R:])
    cov0, cov1 = fold_pair(cov0), fold_pair(cov1)
    keep_cov[...] = jnp.where(first, cov0, cov1)
    send_cov[...] = jnp.where(first, cov1, cov0)
    for pair in range(acts.shape[1] // LEN // 2):
        blocks = []
        for seq in (2 * pair, 2 * pair + 1):
            tokens = slice(seq * LEN, (seq + 1) * LEN)
            blocks.append(dot(outs[:, tokens], acts[:, tokens], NT) * (1.0 / LEN))
        mom0 = jnp.where(low, blocks[0][:R], pltpu.roll(blocks[1][:R], R, 1))
        mom1 = jnp.where(low, pltpu.roll(blocks[0][R:], R, 1), blocks[1][R:])
        lanes = slice(pair * PAIR, (pair + 1) * PAIR)
        keep_mom[:, lanes] = jnp.where(first, mom0, mom1)
        send_mom[:, lanes] = jnp.where(first, mom1, mom0)


def statistics(acts, outs):
    seqs = acts.shape[1] // LEN
    cov = jax.ShapeDtypeStruct((R // 2 + 8, PAIR), F32)
    mom = jax.ShapeDtypeStruct((R, seqs * R), F32)
    vmem = pl.BlockSpec(memory_space=pltpu.VMEM)
    return pl.pallas_call(
        statistics_kernel,
        in_specs=[vmem, vmem],
        out_specs=[vmem] * 4,
        out_shape=[cov, cov, mom, mom],
        compiler_params=pltpu.CompilerParams(vmem_limit_bytes=16 * MIB),
        name="statistics",
    )(acts, outs)


def solve_block(p, rows):
    det = 1.0 / (p[0][0] * p[1][1] - p[0][1] * p[0][1])
    a, b, c = p[1][1] * det, -p[0][1] * det, p[0][0] * det
    t = [[a * p[0][j] + b * p[1][j], b * p[0][j] + c * p[1][j]] for j in (2, 3)]
    s22 = p[2][2] - p[0][2] * t[0][0] - p[1][2] * t[0][1]
    s23 = p[2][3] - p[0][2] * t[1][0] - p[1][2] * t[1][1]
    s33 = p[3][3] - p[0][3] * t[1][0] - p[1][3] * t[1][1]
    det = 1.0 / (s22 * s33 - s23 * s23)
    y0 = a * rows[0] + b * rows[1]
    y1 = b * rows[0] + c * rows[1]
    z2 = rows[2] - p[0][2] * y0 - p[1][2] * y1
    z3 = rows[3] - p[0][3] * y0 - p[1][3] * y1
    x2 = (s33 * z2 - s23 * z3) * det
    x3 = (s22 * z3 - s23 * z2) * det
    return [y0 - t[0][0] * x2 - t[1][0] * x3, y1 - t[0][1] * x2 - t[1][1] * x3, x2, x3]


def invert_pair(matrix):
    lane = lax.broadcasted_iota(jnp.int32, (8, PAIR), 1)
    row = lax.broadcasted_iota(jnp.int32, (8, PAIR), 0)
    column = lane % R
    base = lane - column
    work = [matrix[8 * g : 8 * g + 8] for g in range(R // 8)]
    for k in range(0, R, BLOCK):
        cols = [[jnp.take_along_axis(part, base + (k + j), axis=1) for j in range(BLOCK)] for part in work]
        home, at = k // 8, k % 8
        inside = (column >= k) & (column < k + BLOCK)
        pivots = [[cols[home][j][at + i : at + i + 1] for j in range(BLOCK)] for i in range(BLOCK)]
        rows = [
            jnp.where(
                inside[:1], jnp.where(column[:1] == k + i, 1.0, 0.0), work[home][at + i : at + i + 1]
            )
            for i in range(BLOCK)
        ]
        solved = solve_block(pivots, rows)
        for g in range(R // 8):
            part = jnp.where(inside, 0.0, work[g])
            col = cols[g]
            if g == home:
                block_row = (row >= at) & (row < at + BLOCK)
                part = jnp.where(block_row, 0.0, part)
                col = [
                    jnp.where(block_row, jnp.where(row == at + j, -1.0, 0.0), col[j]) for j in range(BLOCK)
                ]
            work[g] = part - (col[0] * solved[0] + col[1] * solved[1]) - (col[2] * solved[2] + col[3] * solved[3])
    return jnp.concatenate(work, axis=0)


def inverse_kernel(total_tokens, *refs):
    cov_refs, inv_ref = refs[:-1], refs[-1]
    row = lax.broadcasted_iota(jnp.int32, (R, PAIR), 0)
    lane = lax.broadcasted_iota(jnp.int32, (R, PAIR), 1)
    low = lane < R
    column = jnp.where(low, lane, lane - R)
    cov = unfold_pair(sum(ref[...] for ref in cov_refs))
    diagonal = jnp.where(row == column, cov, 0.0)
    trace_in = jnp.sum(jnp.where(low, diagonal, 0.0), keepdims=True)
    trace_out = jnp.sum(jnp.where(low, 0.0, diagonal), keepdims=True)
    scale = R / jnp.where(low, trace_in, trace_out)
    inv_ref[...] = invert_pair(cov * scale + jnp.where(row == column, DAMPING, 0.0)) * (scale * total_tokens)


def inverse(covs, total_tokens):
    vmem = pl.BlockSpec(memory_space=pltpu.VMEM)
    return pl.pallas_call(
        functools.partial(inverse_kernel, total_tokens),
        in_specs=[vmem] * len(covs),
        out_specs=vmem,
        out_shape=jax.ShapeDtypeStruct((R, PAIR), F32),
        compiler_params=pltpu.CompilerParams(vmem_limit_bytes=16 * MIB),
        name="inverse",
    )(*covs)


def precondition_kernel(inv_ref, keep_ref, recv_ref, out_ref, flat_ref):
    low = lax.broadcasted_iota(jnp.int32, (R, PAIR), 1) < R
    inv = inv_ref[...]
    tiles = R // 2
    left = jnp.concatenate([inv_ref[pl.ds(start, tiles, stride=2), :] for start in range(2)], axis=0)
    left = pltpu.roll(left, R, 1)[:, :R]
    moments = jnp.concatenate([keep_ref[...], recv_ref[...]], axis=1)
    mixed = dot(left, moments, NN, lax.Precision.HIGHEST)
    pairs = moments.shape[1] // PAIR
    stack = jnp.concatenate(
        [
            jnp.concatenate(
                [mixed[:tiles, j * PAIR : (j + 1) * PAIR], mixed[tiles:, j * PAIR : (j + 1) * PAIR]], axis=1
            )
            for j in range(pairs)
        ],
        axis=0,
    )
    zero = jnp.zeros((R, PAIR), F32)
    at_low = jnp.where(low, inv, 0.0)
    at_high = pltpu.roll(at_low, R, 1)
    right = jnp.concatenate(
        [
            jnp.concatenate([at_low, zero], axis=1),
            jnp.concatenate([zero, at_low], axis=1),
            jnp.concatenate([at_high, zero], axis=1),
            jnp.concatenate([zero, at_high], axis=1),
        ],
        axis=0,
    )
    done = dot(stack, right, NN, lax.Precision.HIGHEST)
    for j in range(pairs):
        rows = done[j * tiles : (j + 1) * tiles]
        flat_ref[(2 * j) * tiles : (2 * j + 1) * tiles, :] = rows[:, :PAIR]
        flat_ref[(2 * j + 1) * tiles : (2 * j + 2) * tiles, :] = rows[:, PAIR:]
    for k in range(tiles):
        out_ref[:, k * PAIR : (k + 1) * PAIR] = flat_ref[pl.ds(k, 2 * pairs, stride=tiles), :].astype(BF16)


def precondition(inv, moments):
    seqs = sum(part.shape[1] for part in moments) // R
    vmem = pl.BlockSpec(memory_space=pltpu.VMEM)
    return pl.pallas_call(
        precondition_kernel,
        in_specs=[vmem] * (1 + len(moments)),
        out_specs=vmem,
        out_shape=jax.ShapeDtypeStruct((seqs, R * R), BF16),
        scratch_shapes=[pltpu.VMEM((seqs * R // 2, PAIR), F32)],
        compiler_params=pltpu.CompilerParams(vmem_limit_bytes=16 * MIB),
        name="precondition",
    )(inv, *moments)


def scores_kernel(order, flat_ref, *refs):
    query_refs, (out_ref, part_ref) = refs[:-2], refs[-2:]
    place = lax.axis_index("dp")
    part = dot(jnp.concatenate([ref[...] for ref in query_refs], axis=0), flat_ref[...], NT)
    group = part_ref.shape[1]
    for at, distance in enumerate(order):
        part_ref[place ^ distance] = part[at * group : (at + 1) * group]
    out_ref[...] = part_ref[...].reshape(part.shape).T


def score(flat, queries, order):
    seqs = flat.shape[0]
    count = sum(part.shape[0] for part in queries)
    vmem = pl.BlockSpec(memory_space=pltpu.VMEM)
    return pl.pallas_call(
        functools.partial(scores_kernel, order),
        in_specs=[vmem] * (1 + len(queries)),
        out_specs=vmem,
        out_shape=jax.ShapeDtypeStruct((seqs, count), F32),
        scratch_shapes=[pltpu.VMEM((len(order), count // len(order), seqs), F32)],
        compiler_params=pltpu.CompilerParams(vmem_limit_bytes=16 * MIB),
        name="scores",
    )(flat, *queries)


def exchange(value, distance):
    return lax.ppermute(value, "dp", [(i, i ^ distance) for i in range(lax.axis_size("dp"))])


def halves(value, upper):
    low, high = jnp.split(value, 2, axis=1)
    return jnp.where(upper, high, low), jnp.where(upper, low, high)


def per_device(layer_input, out_grads, in_proj, out_proj, queries):
    local_tokens = layer_input.shape[0]
    devices = lax.axis_size("dp")
    slabs = devices // GROUP
    device, queries = lax.optimization_barrier((own_place(), queries))
    near_slabs, far_slabs = [1, 2], list(range(3, slabs))
    column = {slab: exchange(queries, slab * GROUP) for slab in [1, 2, 3] + list(range(4, slabs))}
    column[0] = queries
    beside = exchange(queries, 2)
    acts = project(layer_input, in_proj.reshape(PAIR, in_proj.shape[2]))
    acts, out_grads, column[0] = lax.optimization_barrier((acts, out_grads, column[0]))
    upper = device[0] & 1 == 1

    def fold(picked):
        keep, send = zip(*(halves(column[slab], upper) for slab in picked))
        keep, send = jnp.concatenate(keep, axis=0), jnp.concatenate(send, axis=0)
        return jnp.concatenate([keep, exchange(send, 1)], axis=0)

    outs = jnp.einsum("tmk,mrk->tmr", out_grads, out_proj, preferred_element_type=F32).astype(BF16)
    outs = outs.reshape(local_tokens, PAIR).T
    keep_cov, send_cov, keep_mom, send_mom = statistics(acts, outs)
    cov = keep_cov + exchange(send_cov, 1)
    moments = [keep_mom, exchange(send_mom, 1)]
    cov, column[3] = lax.optimization_barrier((cov, column[3]))
    cov = cov + exchange(cov, 2)
    far = fold(far_slabs)
    cov, far, moments = lax.optimization_barrier((cov, far, moments))
    column[-1] = beside
    local = fold([0, -1])
    near = fold(near_slabs)
    across = exchange(near, 2)
    covs = [cov] + [exchange(cov, slab * GROUP) for slab in reversed(range(1, slabs))]
    covs, across = lax.optimization_barrier((covs, across))
    inv = inverse(covs, local_tokens * devices)
    gathered = [local, near, across, far, exchange(far, 2)]
    order = [0, 2, 1, 3] + [
        slab * GROUP + 2 * over + core
        for part in (near_slabs, far_slabs)
        for over in range(2)
        for core in range(2)
        for slab in part
    ]
    partial = score(precondition(inv, moments), gathered, order)
    seqs = local_tokens // LEN
    return partial[:seqs] + exchange(partial[seqs:], 1)


def solution(mesh):
    return jax.shard_map(
        per_device,
        mesh=mesh,
        in_specs=(
            P(("parts", "dp"), None),
            P(("parts", "dp"), None, None),
            P(),
            P(),
            P(("parts", "dp"), None),
        ),
        out_specs=P(("parts", "dp"), None),
        check_vma=False,
    )
```
